256 devices in a mesh: dp: 256 (over y, x, z, core).
Axes of the slice: x: 4, y: 4, z: 8, core: 2. Of those that a mesh axis runs over, the one named last changes fastest.
Arguments:
- telemetry_pooled_features: bfloat16 [32768, 1152], P('dp')
- picture_pooled_features: bfloat16 [32768, 1152], P('dp')
- telemetry_projection_weights: bfloat16 [1152, 1152], replicated, may hold values from -0.1875 to 0.1875
- picture_projection_weights: bfloat16 [1152, 1152], replicated, may hold values from -0.1875 to 0.1875
- positive_position: int32 [32768], P('dp'), may hold values from 0 to 127, as said below
- logarithmic_scale_param: float32 [1], replicated, may hold values from 0.7 to 1.5
- affinity_shift: float32 [1], replicated, may hold values from -3 to -1
Outputs:
- grad_w_text: bfloat16 [1152, 1152], replicated
- grad_w_image: bfloat16 [1152, 1152], replicated
The draws below stay inside these ranges and needn't reach their ends.
Inputs may be any that keep to these rules, and one draw needn't show every extreme that they name: `positive_position`: most rows name themselves; some name another row of their block, so that an image may be the positive of several texts or of none. The first and last row of every block name themselves.
All inputs are finite; a program needn't handle non-finite values.
Results may differ from the reference program's by a relative error of at most 0.0063.
Values may be sent and summed in bfloat16 or wider, within the bound.
No kernel may reach another device: no remote copies, remote signals or barrier semaphores. Data moves between devices by JAX's collectives and lax.ppermute only.
A program may use at most 128 MiB of HBM per device.

```python
import math
import jax
import jax.numpy as jnp
from jax import lax

D = 1152
E = 1152
ROWS = 128
HALF = 3
TOKENS = 32768
N_DP = 256


def scaled_rows(key):
    row_key, col_key, base_key = jax.random.split(key, 3)
    row_scale = jnp.exp(jax.random.uniform(row_key, (TOKENS, 1), jnp.float32) * math.log(10.0))
    col_scale = jnp.exp(jax.random.uniform(col_key, (1, D), jnp.float32) * math.log(3.0))
    base = jax.random.normal(base_key, (TOKENS, D), jnp.float32)
    return (base * row_scale * col_scale).astype(jnp.bfloat16)


def draw_telemetry_pooled_features(key, part):
    key = jax.random.fold_in(key, 11)
    return scaled_rows(key)


def draw_picture_pooled_features(key, part):
    key = jax.random.fold_in(key, 23)
    return scaled_rows(key)


def draw_positive_position(key, part):
    key = jax.random.fold_in(key, 37)
    pick_key, other_key = jax.random.split(key)
    within = jnp.arange(TOKENS, dtype=jnp.int32) % ROWS
    replace = jax.random.randint(pick_key, (TOKENS,), 0, 4) == 0
    replace = replace & (within > 0) & (within < ROWS - 1)
    other = jax.random.randint(other_key, (TOKENS,), 0, ROWS)
    return jnp.where(replace, other, within).astype(jnp.int32)


def scatter_about(stream_key, dims, spread, reach, kind=jnp.bfloat16):
    values = jax.random.normal(stream_key, dims, jnp.float32) * spread
    return jnp.minimum(jnp.maximum(values, -reach), reach).astype(kind)


def setup_inputs(seed: int = 0) -> dict:
    splits = jax.random.split(jax.random.key(seed), 8)
    return {
        "telemetry_pooled_features": draw_telemetry_pooled_features(jax.random.fold_in(splits[7], 71), 0),
        "picture_pooled_features": draw_picture_pooled_features(jax.random.fold_in(splits[7], 71), 0),
        "telemetry_projection_weights": scatter_about(splits[2], (D, E), D ** -0.5, 0.1875),
        "picture_projection_weights": scatter_about(splits[3], (D, E), D ** -0.5, 0.1875),
        "positive_position": draw_positive_position(jax.random.fold_in(splits[7], 71), 0),
        "logarithmic_scale_param": jnp.clip(jax.random.uniform(splits[5], (1,), jnp.float32, 0.7, 1.5), 0.7, 1.5),
        "affinity_shift": jnp.clip(jax.random.uniform(splits[6], (1,), jnp.float32, -3.0, -1.0), -3.0, -1.0),
    }


epsilon = 1e-06

def embed(features, weight):
    projected = jnp.dot(features, weight, preferred_element_type=jnp.float32)
    length = jnp.sqrt(lax.optimization_barrier(jnp.sum(projected * projected, axis=-1, keepdims=True)) + epsilon)
    return (projected / length, length)

def pull_back(gradient, unit_rows, length):
    radial = lax.optimization_barrier(jnp.sum(gradient * unit_rows, axis=-1, keepdims=True))
    return ((gradient - unit_rows * radial) / length).astype(jnp.bfloat16)

def reference(telemetry_pooled_features, picture_pooled_features, telemetry_projection_weights, picture_projection_weights, positive_position, logarithmic_scale_param, affinity_shift):
    text_unit, text_norm = embed(telemetry_pooled_features, telemetry_projection_weights)
    image_unit, image_norm = embed(picture_pooled_features, picture_projection_weights)
    telemetry_group_sequence = text_unit.astype(jnp.bfloat16).reshape(N_DP, ROWS, E)
    image_blocks = image_unit.astype(jnp.bfloat16).reshape(N_DP, ROWS, E)
    affinity_scale = jnp.exp(logarithmic_scale_param[0])
    affinity_additive_term = affinity_shift[0]
    labels = (positive_position.reshape(N_DP, ROWS)[:, :, None] == jnp.arange(ROWS, dtype=jnp.int32)[None, None, :]).astype(jnp.float32)
    telemetry_derivative = jnp.zeros((N_DP, ROWS, E), jnp.float32)
    image_grad = jnp.zeros((N_DP, ROWS, E), jnp.float32)
    for offset in range(-HALF, HALF + 1):
        neighbour_group = jnp.roll(image_blocks, offset, axis=0)
        similarity_array = jnp.einsum('nre,nse->nrs', telemetry_group_sequence.astype(jnp.float32), neighbour_group.astype(jnp.float32))
        affinity_array = affinity_scale * similarity_array + affinity_additive_term
        if offset == 0:
            match_coefficient = jax.nn.sigmoid(affinity_array) - labels
        else:
            match_coefficient = jax.nn.sigmoid(affinity_array)
        match_coefficient = lax.optimization_barrier(match_coefficient.astype(jnp.bfloat16)).astype(jnp.float32)
        telemetry_derivative = telemetry_derivative + affinity_scale * jnp.einsum('szr,srk->szk', match_coefficient, neighbour_group.astype(jnp.float32))
        picture_share = affinity_scale * jnp.einsum('ckv,cko->cvo', match_coefficient, telemetry_group_sequence.astype(jnp.float32))
        image_grad = image_grad + jnp.roll(picture_share, -offset, axis=0)
    text_back = pull_back(telemetry_derivative.reshape(TOKENS, E), text_unit, text_norm)
    image_back = pull_back(image_grad.reshape(TOKENS, E), image_unit, image_norm)
    grad_w_text = jnp.dot(telemetry_pooled_features.T, text_back, preferred_element_type=jnp.float32)
    grad_w_image = jnp.dot(picture_pooled_features.T, image_back, preferred_element_type=jnp.float32)
    return (grad_w_text.astype(jnp.bfloat16), grad_w_image.astype(jnp.bfloat16))
```

```python
import jax
import jax.numpy as jnp
from jax import lax
from jax.sharding import PartitionSpec as P

NY, NX, NZ = 4, 4, 8
N = 2 * NX * NY * NZ
epsilon = 1e-06
bf16, f32 = jnp.bfloat16, jnp.float32


def index(y, x, z, c):
    return ((y * NX + x) * NZ + z) * 2 + c


PLANES = [
    [index(y, x, z, c) for y in range(NY) for x in range(NX)] for z in range(NZ) for c in range(2)
]
LINES = [
    [index(y, x, z, c) for z in range(NZ)]
    for y in range(NY)
    for x in range(NX)
    for c in range(2)
]
SWAP = [(i, i ^ 1) for i in range(N)]


def shifted(distance):
    return [(i, (i + distance) % N) for i in range(N)]


def embed(features, weight):
    projected = jnp.dot(features, weight, preferred_element_type=f32)
    length = jnp.sqrt(jnp.sum(projected * projected, axis=-1, keepdims=True) + epsilon)
    return projected / length, length


def pull_back(gradient, unit_rows, length):
    radial = jnp.sum(gradient * unit_rows, axis=-1, keepdims=True)
    return ((gradient - unit_rows * radial) / length).astype(bf16)


def contract(a, b, da, db):
    return lax.dot_general(a, b, (((da,), (db,)), ((), ())), preferred_element_type=f32)


def exchange(parts, groups):
    return lax.all_to_all(parts, "dp", 0, 0, axis_index_groups=groups, tiled=True)


def to_tiles(matrix):
    rows, columns = matrix.shape
    return (
        matrix.reshape(rows // 8, 8, columns // 128, 128)
        .transpose(0, 2, 1, 3)
        .reshape(-1, 8, 128)
    )


def from_tiles(tiles, rows, columns):
    return (
        tiles.reshape(rows // 8, columns // 128, 8, 128)
        .transpose(0, 2, 1, 3)
        .reshape(rows, columns)
    )


def on_device(text_x, image_x, text_w, image_w, position, log_scale, shift):
    rows = text_x.shape[0]
    depth, width = text_w.shape
    core = lax.rem(lax.axis_index("dp"), 2)
    scale = jnp.exp(log_scale[0])
    bias = shift[0]
    with jax.named_scope("band_exchange"):
        below = lax.ppermute(text_x, "dp", shifted(2))
        above = lax.ppermute(text_x, "dp", shifted(-2))
        far = lax.ppermute(
            text_x, "dp", [(i, (i + 3) % N if i % 2 else (i - 3) % N) for i in range(N)]
        )
        partner = lax.ppermute(text_x, "dp", SWAP)
        below_partner = lax.ppermute(below, "dp", SWAP)
        above_partner = lax.ppermute(above, "dp", SWAP)
    image_unit, image_norm = embed(image_x, image_w)
    image_emb = image_unit.astype(bf16)
    labels = (position[:, None] == jnp.arange(rows, dtype=jnp.int32)[None, :]).astype(f32)

    def visit(block, targets):
        unit, norm = embed(block, text_w)
        emb = unit.astype(bf16)
        logits = scale * contract(emb, image_emb, 1, 1) + bias
        sigmoid = jax.nn.sigmoid(logits)
        coefficient = (sigmoid - targets).astype(bf16)
        text_grad = scale * jnp.dot(coefficient, image_emb, preferred_element_type=f32)
        return pull_back(text_grad, unit, norm), scale * contract(coefficient, emb, 0, 0)

    with jax.named_scope("near_blocks"):
        near = jnp.concatenate([text_x, partner])
        targets = jnp.concatenate([labels, jnp.zeros_like(labels)])
        near_back, image_grad = visit(near, targets)
    with jax.named_scope("far_blocks"):
        others = jnp.concatenate([below, above, far, below_partner, above_partner])
        others_back, image_share = visit(others, 0.0)
        image_grad = image_grad + image_share
    image_back = pull_back(image_grad, image_unit, image_norm)
    with jax.named_scope("heads"):
        head_text = contract(
            jnp.concatenate([near, others]), jnp.concatenate([near_back, others_back]), 0, 0
        )
        head_image = contract(image_x, image_back, 0, 0)
        mine = jnp.where(core == 0, head_text, head_image)
        theirs = jnp.where(core == 0, head_image, head_text).astype(bf16)
        total = mine + lax.ppermute(theirs, "dp", SWAP).astype(f32)
    with jax.named_scope("sum_planes"):
        tiles = to_tiles(total.astype(bf16))
        slices = exchange(tiles, PLANES).reshape(NX * NY, -1, 8, 128)
        part = jnp.sum(slices.astype(f32), axis=0).astype(bf16)
    count = part.shape[0]
    each = -(-count // NZ)
    with jax.named_scope("sum_lines"):
        part = jnp.concatenate([part, jnp.zeros((each * NZ - count, 8, 128), bf16)])
        part = exchange(part, LINES).reshape(NZ, each, 8, 128)
        part = jnp.sum(part.astype(f32), axis=0).astype(bf16)
    with jax.named_scope("share_lines"):
        part = exchange(jnp.tile(part, (NZ, 1, 1)), LINES)[:count]
    with jax.named_scope("share_planes"):
        whole = exchange(jnp.tile(part, (NX * NY, 1, 1)), PLANES)
        mine = from_tiles(whole, depth, width)
    with jax.named_scope("finish"):
        theirs = lax.ppermute(mine, "dp", SWAP)
        return jnp.where(core == 0, mine, theirs), jnp.where(core == 0, theirs, mine)


def solution(mesh):
    return jax.shard_map(
        on_device,
        mesh=mesh,
        in_specs=(P("dp", None), P("dp", None), P(), P(), P("dp"), P(), P()),
        out_specs=(P(), P()),
        check_vma=False,
    )
```

```python
import functools

import jax
import jax.numpy as jnp
from jax import lax
from jax.experimental import pallas as pl
from jax.experimental.pallas import tpu as pltpu
from jax.sharding import PartitionSpec as P

NY, NX, NZ, CORES = 4, 4, 8, 2
N = NY * NX * NZ * CORES
epsilon = 1e-06
bf16, f32 = jnp.bfloat16, jnp.float32
MIB = 1 << 20


def index(y, x, z, c):
    return ((y % NY * NX + x % NX) * NZ + z % NZ) * CORES + c


PLACES = [
    (y, x, z, c) for y in range(NY) for x in range(NX) for z in range(NZ) for c in range(CORES)
]


def route(move):
    return [(index(*place), index(*move(*place))) for place in PLACES]


def groups(key):
    found = {}
    for place in PLACES:
        found.setdefault(key(*place), []).append(index(*place))
    return list(found.values())


def along_first(step):
    return route(lambda y, x, z, c: (y, x + step, z, c) if c == 0 else (y + step, x, z, c))


SWAP = route(lambda y, x, z, c: (y, x, z, 1 - c))
RIGHT, LEFT = along_first(1), along_first(-1)
SECOND = groups(lambda y, x, z, c: (c, z, x if c == 0 else y))
LINES = groups(lambda y, x, z, c: (c, x, y))
FAR = [(i, (i + 3) % N if i % 2 else (i - 3) % N) for i in range(N)]


def shifted(distance):
    return [(i, (i + distance) % N) for i in range(N)]


def send(block, pairs):
    return lax.ppermute(block, "dp", pairs)


def exchange(parts, members):
    return lax.all_to_all(parts, "dp", 0, 0, axis_index_groups=members, tiled=True)


def call(body, outs, scratch=(), limit=32):
    def run(scalars, *arrays):
        smem = [pl.BlockSpec(memory_space=pltpu.SMEM)] * len(scalars)
        vmem = [pl.BlockSpec(memory_space=pltpu.VMEM)] * len(arrays)
        return pl.pallas_call(
            body,
            out_shape=[jax.ShapeDtypeStruct(s, d) for s, d in outs],
            in_specs=smem + vmem,
            out_specs=[pl.BlockSpec(memory_space=pltpu.VMEM)] * len(outs),
            scratch_shapes=list(scratch),
            compiler_params=pltpu.CompilerParams(vmem_limit_bytes=limit * MIB),
        )(*scalars, *[pltpu.with_memory_space_constraint(a, pltpu.VMEM) for a in arrays])

    return run


def embed(features, weight):
    projected = jnp.dot(features, weight, preferred_element_type=f32)
    length = jnp.sqrt(jnp.sum(projected * projected, axis=-1, keepdims=True) + epsilon)
    return projected / length, length


def pull_back(gradient, unit_rows, length):
    radial = jnp.sum(gradient * unit_rows, axis=-1, keepdims=True)
    return ((gradient - unit_rows * radial) / length).astype(bf16)


def contract(a, b, da, db):
    return lax.dot_general(a, b, (((da,), (db,)), ((), ())), preferred_element_type=f32)


def near_kernel(
    place, factors, text_own, text_other, image_own, image_other, text_w, image_w, target,
    image_emb, image_unit, image_norm, text_back, image_grad,
):
    scale, bias = factors[0], factors[1]
    unit, norm = embed(jnp.concatenate([image_own[...], image_other[...]]), image_w[...])
    emb = unit.astype(bf16)
    image_emb[...] = emb
    image_unit[...] = unit
    image_norm[...] = norm
    unit, norm = embed(jnp.concatenate([text_own[...], text_other[...]]), text_w[...])
    text_emb = unit.astype(bf16)
    logits = scale * contract(text_emb, emb, 1, 1) + bias
    labels = (lax.broadcasted_iota(jnp.int32, logits.shape, 1) == target[...]).astype(f32)
    coefficient = (jax.nn.sigmoid(logits) - labels).astype(bf16)

    @pl.when(place[0] == 0)
    def _():
        gradient = scale * jnp.dot(coefficient, emb, preferred_element_type=f32)
        text_back[...] = pull_back(gradient, unit, norm)

    @pl.when(place[0] != 0)
    def _():
        image_grad[...] = contract(coefficient, text_emb, 0, 0)


def far_kernel(
    place, factors, text_own, text_other, below, below_other, above, above_other, far, far_other,
    image_own, image_other, text_w, image_emb, image_unit, image_norm, text_back, image_grad,
    own, right_top, right_bottom, left_top, left_bottom, far_right, far_left,
    xs, backs, grad, head,
):
    rows, width = text_own.shape
    depth = head.shape[0]
    scale, bias = factors[0], factors[1]
    for k, (a, b) in enumerate([(below, below_other), (above, above_other), (far, far_other)]):
        x = jnp.concatenate([a[...], b[...]])
        unit, norm = embed(x, text_w[...])
        emb = unit.astype(bf16)
        logits = scale * contract(emb, image_emb[...], 1, 1) + bias
        sigmoid = jax.nn.sigmoid(logits)
        if k == 2:
            row = lax.broadcasted_iota(jnp.int32, logits.shape, 0) < rows
            column = lax.broadcasted_iota(jnp.int32, logits.shape, 1) < rows
            sigmoid = jnp.where(row == column, sigmoid, 0.0)
        coefficient = sigmoid.astype(bf16)

        @pl.when(place[0] == 0)
        def _():
            gradient = scale * jnp.dot(coefficient, image_emb[...], preferred_element_type=f32)
            at = pl.ds(2 * rows * k, 2 * rows)
            backs[at, :] = pull_back(gradient, unit, norm)
            xs[at, :] = x

        @pl.when(place[0] != 0)
        def _():
            share = contract(coefficient, emb, 0, 0)
            if k == 0:
                grad[...] = image_grad[...] + share
            else:
                grad[...] = grad[...] + share

    step = depth // 3

    @pl.when(place[0] == 0)
    def _():
        at = 6 * rows
        xs[pl.ds(at, rows), :] = text_own[...]
        xs[pl.ds(at + rows, rows), :] = text_other[...]
        backs[pl.ds(at, 2 * rows), :] = text_back[...]
        for k in range(3):
            at = pl.ds(k * step, step)
            head[at, :] = contract(xs[:, at], backs[...], 0, 0)

    @pl.when(place[0] != 0)
    def _():
        back = pull_back(scale * grad[...], image_unit[...], image_norm[...])
        backs[pl.ds(0, 2 * rows), :] = back
        xs[pl.ds(0, rows), :] = image_own[...]
        xs[pl.ds(rows, rows), :] = image_other[...]
        for k in range(3):
            at = pl.ds(k * step, step)
            head[at, :] = contract(xs[pl.ds(0, 2 * rows), at], back, 0, 0)

    slab = depth // 4
    half = slab // 2

    def part(turn, upper, size):
        start = lax.rem(place[1] + turn, 4) * slab + upper
        return head[pl.ds(pl.multiple_of(start, 16), size), :].astype(bf16)

    far_right[...] = part(2, 0, half)
    far_left[...] = part(2, half, half)
    right_top[...] = part(1, 0, half)
    right_bottom[...] = part(1, half, half)
    left_top[...] = part(3, 0, half)
    left_bottom[...] = part(3, half, half)
    own[...] = part(0, 0, slab)


def add_kernel(a, b, c, d, ab, cd):
    ab[...] = (a[...].astype(f32) + b[...].astype(f32)).astype(bf16)
    cd[...] = (c[...].astype(f32) + d[...].astype(f32)).astype(bf16)


def join_kernel(own, a_top, a_bottom, b_top, b_bottom, out):
    half = a_top.shape[0]
    upper, lower = pl.ds(0, half), pl.ds(half, half)
    out[upper, :] = (
        own[upper, :].astype(f32) + a_top[...].astype(f32) + b_top[...].astype(f32)
    ).astype(bf16)
    out[lower, :] = (
        own[lower, :].astype(f32) + a_bottom[...].astype(f32) + b_bottom[...].astype(f32)
    ).astype(bf16)


def write_kernel(*refs):
    mine, theirs, (text, image, sems) = refs[:5], refs[5:10], refs[10:]
    me = lax.axis_index("dp")
    core = lax.rem(me, CORES)
    x = lax.rem(me // (NZ * CORES), NX)
    y = me // (NX * NZ * CORES)
    slab = mine[0].shape[0]
    half = slab // 2

    def copies(pieces, position, out, first):
        turns = [(0, 0), (3, 0), (1, 0), (2, 0), (2, half)]
        return [
            pltpu.make_async_copy(
                piece,
                out.at[
                    pl.ds(
                        pl.multiple_of(lax.rem(position + turn, 4) * slab + upper, 16),
                        piece.shape[0],
                    ),
                    :,
                ],
                sems.at[first + k],
            )
            for k, (piece, (turn, upper)) in enumerate(zip(pieces, turns))
        ]

    def go(moves):
        for move in moves:
            move.start()
        for move in moves:
            move.wait()

    @pl.when(core == 0)
    def _():
        go(copies(mine, x, text, 0) + copies(theirs, y, image, 5))

    @pl.when(core != 0)
    def _():
        go(copies(mine, y, image, 0) + copies(theirs, x, text, 5))


def on_device(text_x, image_x, text_w, image_w, position, log_scale, shift):
    rows, width = text_x.shape
    depth = text_w.shape[0]
    slab = depth // 4
    half = slab // 2
    me = lax.axis_index("dp")
    core = lax.rem(me, CORES)
    x = lax.rem(me // (NZ * CORES), NX)
    y = me // (NX * NZ * CORES)
    place = jnp.stack([core, jnp.where(core == 0, x, y)]).astype(jnp.int32)
    factors = jnp.concatenate([jnp.exp(log_scale), shift])
    with jax.named_scope("band_exchange"):
        below = send(text_x, shifted(2))
        above = send(text_x, shifted(-2))
        far = send(text_x, FAR)
        text_other = send(text_x, SWAP)
        image_other = send(image_x, SWAP)
        target = jnp.concatenate([position, send(position, SWAP) + rows])[:, None]
        below_other = send(below, SWAP)
        above_other = send(above, SWAP)
        far_other = send(far, SWAP)
    near = call(
        near_kernel,
        [
            ((2 * rows, width), bf16),
            ((2 * rows, width), f32),
            ((2 * rows, 1), f32),
            ((2 * rows, width), bf16),
            ((2 * rows, width), f32),
        ],
    )
    with jax.named_scope("near"):
        known = near(
            (place, factors), text_x, text_other, image_x, image_other, text_w, image_w, target
        )
    halves = ((half, width), bf16)
    far_call = call(
        far_kernel,
        [((slab, width), bf16)] + [halves] * 6,
        [
            pltpu.VMEM((8 * rows, depth), bf16),
            pltpu.VMEM((8 * rows, width), bf16),
            pltpu.VMEM((2 * rows, width), f32),
            pltpu.VMEM((depth, width), f32),
        ],
    )
    with jax.named_scope("far"):
        own, right_top, right_bottom, left_top, left_bottom, far_right, far_left = far_call(
            (place, factors), text_x, text_other, below, below_other, above, above_other, far,
            far_other, image_x, image_other, text_w, *known,
        )
    with jax.named_scope("sum_first"):
        from_left = send(far_right, RIGHT)
        from_right = send(far_left, LEFT)
        a_bottom = send(right_bottom, RIGHT)
        b_top = send(left_top, LEFT)
        right_top, left_bottom = call(add_kernel, [halves] * 2)(
            (), right_top, from_left, left_bottom, from_right
        )
        a_top = send(right_top, RIGHT)
        b_bottom = send(left_bottom, LEFT)
        [part] = call(join_kernel, [((slab, width), bf16)])(
            (), own, a_top, a_bottom, b_top, b_bottom
        )
    with jax.named_scope("sum_second"):
        part = exchange(part.reshape(4, slab // 4, width), SECOND)
        part = jnp.sum(part.astype(f32), axis=0).astype(bf16)
    with jax.named_scope("sum_lines"):
        tiles = (
            part.reshape(slab // 32, 8, width // 128, 128).transpose(0, 2, 1, 3).reshape(-1, 8, 128)
        )
        count = tiles.shape[0]
        each = -(-count // NZ)
        tiles = jnp.concatenate([tiles, jnp.zeros((each * NZ - count, 8, 128), bf16)])
        tiles = exchange(tiles, LINES).reshape(NZ, each, 8, 128)
        tiles = jnp.sum(tiles.astype(f32), axis=0).astype(bf16)
    with jax.named_scope("share_lines"):
        tiles = exchange(jnp.tile(tiles, (NZ, 1, 1)), LINES)[:count]
        part = (
            tiles.reshape(slab // 32, width // 128, 8, 128).transpose(0, 2, 1, 3).reshape(-1, width)
        )
    with jax.named_scope("share_second"):
        whole = exchange(jnp.tile(part[None], (4, 1, 1)), SECOND)
        own = whole.reshape(slab, width)
    with jax.named_scope("share_first"):
        left = send(own, RIGHT)
        right = send(own, LEFT)
        own_other = send(own, SWAP)
        across_top = send(left[:half], RIGHT)
        across_bottom = send(right[half:], LEFT)
        mine = [own, left, right, across_top, across_bottom]
        theirs = [own_other] + [send(piece, SWAP) for piece in mine[1:]]
    with jax.named_scope("write"):
        return pl.pallas_call(
            write_kernel,
            out_shape=[jax.ShapeDtypeStruct((depth, width), bf16)] * 2,
            in_specs=[pl.BlockSpec(memory_space=pl.ANY)] * 10,
            out_specs=[pl.BlockSpec(memory_space=pl.ANY)] * 2,
            scratch_shapes=[pltpu.SemaphoreType.DMA((10,))],
        )(*mine, *theirs)


def solution(mesh):
    return jax.shard_map(
        on_device,
        mesh=mesh,
        in_specs=(P("dp", None), P("dp", None), P(), P(), P("dp"), P(), P()),
        out_specs=(P(), P()),
        check_vma=False,
    )
```

```python
import functools

import jax
import jax.numpy as jnp
from jax import lax
from jax.experimental import pallas as pl
from jax.experimental.pallas import tpu as pltpu
from jax.sharding import PartitionSpec as P

NY, NX, NZ, CORES = 4, 4, 8, 2
N = NY * NX * NZ * CORES
epsilon = 1e-06
bf16, f32 = jnp.bfloat16, jnp.float32
MIB = 1 << 20


def index(y, x, z, c):
    return ((y % NY * NX + x % NX) * NZ + z % NZ) * CORES + c


PLACES = [
    (y, x, z, c) for y in range(NY) for x in range(NX) for z in range(NZ) for c in range(CORES)
]


def route(move):
    return [(index(*place), index(*move(*place))) for place in PLACES]


def groups(key):
    found = {}
    for place in PLACES:
        found.setdefault(key(*place), []).append(index(*place))
    return list(found.values())


def along_first(step):
    return route(lambda y, x, z, c: (y, x + step, z, c) if c == 0 else (y + step, x, z, c))


SWAP = route(lambda y, x, z, c: (y, x, z, 1 - c))
RIGHT, LEFT = along_first(1), along_first(-1)
SECOND = groups(lambda y, x, z, c: (c, z, x if c == 0 else y))
LINES = groups(lambda y, x, z, c: (c, x, y))
FAR = [(i, (i + 3) % N if i % 2 else (i - 3) % N) for i in range(N)]


def shifted(distance):
    return [(i, (i + distance) % N) for i in range(N)]


def send(block, pairs):
    return lax.ppermute(block, "dp", pairs)


def exchange(parts, members):
    return lax.all_to_all(parts, "dp", 0, 0, axis_index_groups=members, tiled=True)


def call(body, outs, scratch=(), limit=32, flops=0, aliases=()):
    def run(scalars, outside, *arrays):
        specs = (
            [pl.BlockSpec(memory_space=pltpu.SMEM)] * len(scalars)
            + [pl.BlockSpec(memory_space=pltpu.HBM)] * len(outside)
            + [pl.BlockSpec(memory_space=pltpu.VMEM)] * len(arrays)
        )
        held = [pltpu.with_memory_space_constraint(a, pltpu.VMEM) for a in arrays]
        outside = [pltpu.with_memory_space_constraint(a, pltpu.HBM) for a in outside]
        return pl.pallas_call(
            body,
            out_shape=[jax.ShapeDtypeStruct(s, d) for s, d in outs],
            in_specs=specs,
            out_specs=[pl.BlockSpec(memory_space=pltpu.VMEM)] * len(outs),
            scratch_shapes=list(scratch),
            input_output_aliases=dict(aliases),
            cost_estimate=pl.CostEstimate(flops=flops, bytes_accessed=0, transcendentals=0),
            compiler_params=pltpu.CompilerParams(vmem_limit_bytes=limit * MIB),
        )(*scalars, *outside, *held)

    return run


def embed(features, weight):
    projected = jnp.dot(features, weight, preferred_element_type=f32)
    length = jnp.sqrt(jnp.sum(projected * projected, axis=-1, keepdims=True) + epsilon)
    inverse = 1.0 / length
    return projected * inverse, inverse


def pull_back(gradient, unit_rows, inverse):
    radial = jnp.sum(gradient * unit_rows, axis=-1, keepdims=True)
    return ((gradient - unit_rows * radial) * inverse).astype(bf16)


def contract(a, b, da, db):
    return lax.dot_general(a, b, (((da,), (db,)), ((), ())), preferred_element_type=f32)


def add_head(head, x, back, before):
    step = head.shape[0] // 3
    for k in range(3):
        at = pl.ds(k * step, step)
        new = contract(x[:, at], back[...], 0, 0)
        head[at, :] = new if before is None else before[at, :] + new


def near_kernel(
    place, factors, text_hbm, image_hbm, text_w_hbm, image_w_hbm, text_other, image_other, target,
    image_near, text_w, image_emb, image_unit, image_norm, grad, head,
    text_near, image_w, back, sems,
):
    scale, bias = factors[0], factors[1]
    rows = text_other.shape[0]
    first = pl.ds(0, rows)
    moves = [
        pltpu.make_async_copy(image_hbm, image_near.at[first, :], sems.at[0]),
        pltpu.make_async_copy(image_w_hbm, image_w, sems.at[1]),
        pltpu.make_async_copy(text_hbm, text_near.at[first, :], sems.at[2]),
        pltpu.make_async_copy(text_w_hbm, text_w, sems.at[3]),
    ]
    for move in moves:
        move.start()
    image_near[pl.ds(rows, rows), :] = image_other[...]
    text_near[pl.ds(rows, rows), :] = text_other[...]
    moves[0].wait()
    moves[1].wait()
    unit, norm = embed(image_near[...], image_w[...])
    emb = unit.astype(bf16)
    image_emb[...] = emb
    image_unit[...] = unit
    image_norm[...] = norm
    moves[2].wait()
    moves[3].wait()
    unit, norm = embed(text_near[...], text_w[...])
    text_emb = unit.astype(bf16)
    logits = scale * contract(text_emb, emb, 1, 1) + bias
    labels = (lax.broadcasted_iota(jnp.int32, logits.shape, 1) == target[...]).astype(f32)
    coefficient = (jax.nn.sigmoid(logits) - labels).astype(bf16)

    @pl.when(place[0] == 0)
    def _():
        gradient = scale * jnp.dot(coefficient, emb, preferred_element_type=f32)
        back[...] = pull_back(gradient, unit, norm)
        add_head(head, text_near, back, None)

    @pl.when(place[0] != 0)
    def _():
        grad[...] = contract(coefficient, text_emb, 0, 0)


def gate_kernel(*refs):
    pass


def visit(place, factors, blocks, text_w, image_emb, mine, xs, backs, grad_before, grad):
    scale, bias = factors[0], factors[1]
    rows = blocks[0].shape[0]
    for k, block in enumerate(blocks):
        xs[pl.ds(rows * k, rows), :] = block[...]
    unit, norm = embed(xs[...], text_w[...])
    emb = unit.astype(bf16)
    logits = scale * contract(emb, image_emb[...], 1, 1) + bias
    row = lax.broadcasted_iota(jnp.int32, logits.shape, 0)
    column = lax.broadcasted_iota(jnp.int32, logits.shape, 1)
    inside = jnp.logical_or(row < 2 * rows, (column < rows) == mine)
    coefficient = jnp.where(inside, jax.nn.sigmoid(logits), 0.0).astype(bf16)

    @pl.when(place[0] == 0)
    def _():
        gradient = scale * jnp.dot(coefficient, image_emb[...], preferred_element_type=f32)
        backs[...] = pull_back(gradient, unit, norm)

    @pl.when(place[0] != 0)
    def _():
        grad[...] = grad_before[...] + contract(coefficient, emb, 0, 0)


def received_kernel(
    place, factors, below, above, far, text_w, image_emb, grad_before, head_before,
    grad, head, xs, backs,
):
    visit(
        place, factors, (below, above, far), text_w, image_emb, True, xs, backs, grad_before, grad
    )

    @pl.when(place[0] == 0)
    def _():
        add_head(head, xs, backs, head_before)


def last_kernel(
    place, factors, below, above, far, text_w, image_emb, grad_before, head_before,
    image_near, image_unit, image_norm,
    own, right, left, far_right, far_left, grad, head, xs, backs,
):
    visit(
        place, factors, (below, above, far), text_w, image_emb, False, xs, backs, grad_before, grad
    )

    @pl.when(place[0] == 0)
    def _():
        add_head(head, xs, backs, head_before)

    @pl.when(place[0] != 0)
    def _():
        back = pull_back(factors[0] * grad[...], image_unit[...], image_norm[...])
        add_head(head, image_near, back, None)

    slab = head.shape[0] // 4
    half = slab // 2

    def part(turn, upper, size):
        start = lax.rem(place[1] + turn, 4) * slab + upper
        return head[pl.ds(pl.multiple_of(start, 16), size), :].astype(bf16)

    far_right[...] = part(2, 0, half)
    far_left[...] = part(2, half, half)
    right[...] = part(1, 0, slab)
    left[...] = part(3, 0, slab)
    own[...] = part(0, 0, slab)


def add_kernel(right, upper, left, lower, right_sum, left_sum):
    half = upper.shape[0]
    first, second = pl.ds(0, half), pl.ds(half, half)
    right_sum[first, :] = (right[first, :].astype(f32) + upper[...].astype(f32)).astype(bf16)
    right_sum[second, :] = right[second, :]
    left_sum[first, :] = left[first, :]
    left_sum[second, :] = (left[second, :].astype(f32) + lower[...].astype(f32)).astype(bf16)


def join_kernel(own, a, b, out):
    out[...] = (own[...].astype(f32) + a[...].astype(f32) + b[...].astype(f32)).astype(bf16)


def pack_kernel(own, left_top, right_bottom, to_right, to_left):
    half = left_top.shape[0]
    first, second = pl.ds(0, half), pl.ds(half, half)
    to_right[first, :] = own[second, :]
    to_right[second, :] = left_top[...]
    to_left[first, :] = own[first, :]
    to_left[second, :] = right_bottom[...]


def write_kernel(place, *refs):
    mine, theirs, (text, image, sems) = refs[:5], refs[5:10], refs[10:]
    slab = mine[0].shape[0]
    half = slab // 2

    def copies(pieces, position, out, first):
        own, left_top, right_bottom, from_left, from_right = pieces
        upper, lower = pl.ds(0, half), pl.ds(half, half)
        placed = [
            (own, 0, 0),
            (left_top, 3, 0),
            (right_bottom, 1, 1),
            (from_left.at[upper, :], 3, 1),
            (from_left.at[lower, :], 2, 0),
            (from_right.at[upper, :], 1, 0),
            (from_right.at[lower, :], 2, 1),
        ]
        moves = []
        for k, (piece, turn, part) in enumerate(placed):
            start = lax.rem(position + turn, 4) * slab + part * half
            target = out.at[pl.ds(pl.multiple_of(start, 16), piece.shape[0]), :]
            moves.append(pltpu.make_async_copy(piece, target, sems.at[first + k]))
        return moves

    def go(moves):
        for move in moves:
            move.start()
        for move in moves:
            move.wait()

    @pl.when(place[0] == 0)
    def _():
        go(copies(mine, place[1], text, 0) + copies(theirs, place[2], image, 7))

    @pl.when(place[0] != 0)
    def _():
        go(copies(mine, place[1], image, 0) + copies(theirs, place[2], text, 7))


def on_device(text_x, image_x, text_w, image_w, position, log_scale, shift):
    rows, width = text_x.shape
    depth = text_w.shape[0]
    slab = depth // 4
    half = slab // 2
    me = lax.axis_index("dp")
    core = lax.rem(me, CORES)
    x = lax.rem(me // (NZ * CORES), NX)
    y = me // (NX * NZ * CORES)
    place = jnp.stack([core, jnp.where(core == 0, x, y), jnp.where(core == 0, y, x)])
    place = place.astype(jnp.int32)
    factors = jnp.concatenate([jnp.exp(log_scale), shift])
    with jax.named_scope("band_exchange"):
        below = send(text_x, shifted(2))
        above = send(text_x, shifted(-2))
        far = send(text_x, FAR)
        text_other = send(text_x, SWAP)
        image_other = send(image_x, SWAP)
        target = jnp.concatenate([position, send(position, SWAP) + rows])[:, None]
    pair = ((2 * rows, width), bf16)
    pair_f32 = ((2 * rows, width), f32)
    total = ((depth, width), f32)
    matrix = pltpu.VMEM((depth, width), bf16)
    blocks = pltpu.VMEM((3 * rows, width), bf16)
    piece = ((slab, width), bf16)
    near = call(
        near_kernel,
        [pair, ((depth, width), bf16), pair, pair_f32, ((2 * rows, 1), f32), pair_f32, total],
        [pltpu.VMEM(*pair), matrix, pltpu.VMEM(*pair), pltpu.SemaphoreType.DMA((4,))],
        flops=4 * 10**9,
    )
    with jax.named_scope("near"):
        image_near, weight, image_emb, image_unit, image_norm, grad, head = near(
            (place, factors), (text_x, image_x, text_w, image_w), text_other, image_other, target
        )
    with jax.named_scope("between"):
        block = ((rows, width), bf16)
        below, above, far = call(gate_kernel, [block] * 3, aliases=[(0, 0), (1, 1), (2, 2)])(
            (), (), below, above, far, image_norm
        )
        below_other = send(below, SWAP)
        above_other = send(above, SWAP)
        far_other = send(far, SWAP)
    with jax.named_scope("received"):
        grad, head = call(received_kernel, [pair_f32, total], [blocks, blocks], flops=4 * 10**9)(
            (place, factors), (), below, above, far, weight, image_emb, grad, head
        )
    with jax.named_scope("last"):
        own, right, left, far_right, far_left = call(
            last_kernel,
            [piece, piece, piece, ((half, width), bf16), ((half, width), bf16)],
            [pltpu.VMEM(*pair_f32), pltpu.VMEM(*total), blocks, blocks],
            flops=4 * 10**9,
        )(
            (place, factors), (), below_other, above_other, far_other, weight, image_emb, grad,
            head, image_near, image_unit, image_norm,
        )
    with jax.named_scope("sum_first"):
        from_left = send(far_right, RIGHT)
        from_right = send(far_left, LEFT)
        right, left = call(add_kernel, [piece, piece])((), (), right, from_left, left, from_right)
        from_left = send(right, RIGHT)
        from_right = send(left, LEFT)
        [part] = call(join_kernel, [piece])((), (), own, from_left, from_right)
    with jax.named_scope("sum_second"):
        part = exchange(part.reshape(4, slab // 4, width), SECOND)
        part = jnp.sum(part.astype(f32), axis=0).astype(bf16)
    with jax.named_scope("sum_lines"):
        tiles = (
            part.reshape(slab // 32, 8, width // 128, 128).transpose(0, 2, 1, 3).reshape(-1, 8, 128)
        )
        count = tiles.shape[0]
        each = -(-count // NZ)
        tiles = jnp.concatenate([tiles, jnp.zeros((each * NZ - count, 8, 128), bf16)])
        tiles = exchange(tiles, LINES).reshape(NZ, each, 8, 128)
        tiles = jnp.sum(tiles.astype(f32), axis=0).astype(bf16)
    with jax.named_scope("share_lines"):
        tiles = exchange(jnp.tile(tiles, (NZ, 1, 1)), LINES)[:count]
        part = (
            tiles.reshape(slab // 32, width // 128, 8, 128).transpose(0, 2, 1, 3).reshape(-1, width)
        )
    with jax.named_scope("share_second"):
        whole = exchange(jnp.tile(part[None], (4, 1, 1)), SECOND)
        own = whole.reshape(slab, width)
    with jax.named_scope("share_first"):
        left_top = send(own[:half], RIGHT)
        right_bottom = send(own[half:], LEFT)
        to_right, to_left = call(pack_kernel, [piece, piece])(
            (), (), own, left_top, right_bottom
        )
        mine = [own, left_top, right_bottom, send(to_right, RIGHT), send(to_left, LEFT)]
        theirs = [send(one, SWAP) for one in mine]
    with jax.named_scope("write"):
        pieces = mine + theirs
        return pl.pallas_call(
            write_kernel,
            out_shape=[jax.ShapeDtypeStruct((depth, width), bf16)] * 2,
            in_specs=[pl.BlockSpec(memory_space=pltpu.SMEM)]
            + [pl.BlockSpec(memory_space=pltpu.VMEM)] * len(pieces),
            out_specs=[pl.BlockSpec(memory_space=pl.ANY)] * 2,
            scratch_shapes=[pltpu.SemaphoreType.DMA((14,))],
            compiler_params=pltpu.CompilerParams(vmem_limit_bytes=32 * MIB),
        )(place, *[pltpu.with_memory_space_constraint(a, pltpu.VMEM) for a in pieces])


def solution(mesh):
    return jax.shard_map(
        on_device,
        mesh=mesh,
        in_specs=(P("dp", None), P("dp", None), P(), P(), P("dp"), P(), P()),
        out_specs=(P(), P()),
        check_vma=False,
    )
```

```python
import jax
import jax.numpy as jnp
from jax import lax
from jax.experimental import pallas as pl
from jax.experimental.pallas import tpu as pltpu
from jax.sharding import PartitionSpec as P

NY, NX, NZ, CORES = 4, 4, 8, 2
N = NY * NX * NZ * CORES
epsilon = 1e-06
bf16, f32 = jnp.bfloat16, jnp.float32
MIB = 1 << 20


def index(y, x, z, c):
    return ((y % NY * NX + x % NX) * NZ + z % NZ) * CORES + c


PLACES = [
    (y, x, z, c) for y in range(NY) for x in range(NX) for z in range(NZ) for c in range(CORES)
]


def route(move):
    return [(index(*place), index(*move(*place))) for place in PLACES]


def groups(key):
    found = {}
    for place in PLACES:
        found.setdefault(key(*place), []).append(index(*place))
    return list(found.values())


def along_first(step):
    return route(lambda y, x, z, c: (y, x + step, z, c) if c == 0 else (y + step, x, z, c))


SWAP = route(lambda y, x, z, c: (y, x, z, 1 - c))
RIGHT, LEFT = along_first(1), along_first(-1)
SECOND = groups(lambda y, x, z, c: (c, z, x if c == 0 else y))
LINES = groups(lambda y, x, z, c: (c, x, y))
FORWARD = [(i, (i + 1) % N if i % 2 else (i - 1) % N) for i in range(N)]
TEXT = 1


def shifted(distance):
    return [(i, (i + distance) % N) for i in range(N)]


def send(block, pairs):
    return lax.ppermute(block, "dp", pairs)


def exchange(parts, members):
    return lax.all_to_all(parts, "dp", 0, 0, axis_index_groups=members, tiled=True)


def call(body, outs, scratch=(), flops=0, result=pltpu.VMEM):
    def run(smem, outside, *arrays):
        specs = (
            [pl.BlockSpec(memory_space=pltpu.SMEM)] * len(smem)
            + [pl.BlockSpec(memory_space=pltpu.HBM)] * len(outside)
            + [pl.BlockSpec(memory_space=pltpu.VMEM)] * len(arrays)
        )
        held = [pltpu.with_memory_space_constraint(a, pltpu.VMEM) for a in arrays]
        outside = [pltpu.with_memory_space_constraint(a, pltpu.HBM) for a in outside]
        return pl.pallas_call(
            body,
            out_shape=[jax.ShapeDtypeStruct(s, d) for s, d in outs],
            in_specs=specs,
            out_specs=[pl.BlockSpec(memory_space=result)] * len(outs),
            scratch_shapes=list(scratch),
            cost_estimate=pl.CostEstimate(flops=flops, bytes_accessed=0, transcendentals=0),
            compiler_params=pltpu.CompilerParams(vmem_limit_bytes=32 * MIB),
        )(*smem, *outside, *held)

    return run


def contract(a, b, da, db):
    return lax.dot_general(a, b, (((da,), (db,)), ((), ())), preferred_element_type=f32)


def core_place():
    me = lax.axis_index("dp")
    core = lax.rem(me, CORES)
    x = lax.rem(me // (NZ * CORES), NX)
    y = me // (NX * NZ * CORES)
    return core, jnp.where(core == 0, x, y), jnp.where(core == 0, y, x)


def on_text():
    return core_place()[0] == TEXT


def factor(log_scale):
    return jnp.exp(jnp.full((1, 1), log_scale[0], f32))


def embed(features, weight):
    projected = jnp.dot(features, weight, preferred_element_type=f32)
    square = jnp.sum(projected * projected, axis=-1, keepdims=True)
    inverse = 1.0 / jnp.sqrt(square + epsilon)
    return projected, inverse


def add_head(head, x, back, before):
    step = head.shape[0] // 3
    for k in range(3):
        at = pl.ds(k * step, step)
        new = contract(x[:, at], back[...], 0, 0)
        head[at, :] = new if before is None else before[at, :] + new


def visit(log_scale, shift, x, text_w, image_emb, finish, back, grad, grad_before):
    scale = factor(log_scale)
    projected, inverse = embed(x[...], text_w[...])
    emb = (projected * inverse).astype(bf16)
    similarity = contract(emb, image_emb[...], 1, 1)
    coefficient = finish(jax.nn.sigmoid(scale * similarity + shift[0])).astype(bf16)

    @pl.when(on_text())
    def _():
        radial = jnp.sum(coefficient.astype(f32) * similarity, axis=-1, keepdims=True)
        gradient = jnp.dot(coefficient, image_emb[...], preferred_element_type=f32)
        outer = scale * inverse
        back[...] = (gradient * outer - projected * (outer * inverse * radial)).astype(bf16)

    @pl.when(jnp.logical_not(on_text()))
    def _():
        share = contract(coefficient, emb, 0, 0)
        grad[...] = share if grad_before is None else grad_before[...] + share


def near_kernel(
    log_scale, shift, text_hbm, image_hbm, text_w_hbm, image_w_hbm, text_other, image_other,
    position, position_other,
    image_near, text_w, image_emb, image_projected, image_inverse, grad, head,
    text_near, image_w, back, sems,
):
    rows = text_other.shape[0]
    first, second = pl.ds(0, rows), pl.ds(rows, rows)
    moves = [
        pltpu.make_async_copy(image_hbm, image_near.at[first, :], sems.at[0]),
        pltpu.make_async_copy(image_w_hbm, image_w, sems.at[1]),
        pltpu.make_async_copy(text_hbm, text_near.at[first, :], sems.at[2]),
        pltpu.make_async_copy(text_w_hbm, text_w, sems.at[3]),
    ]
    for move in moves:
        move.start()
    image_near[second, :] = image_other[...]
    text_near[second, :] = text_other[...]
    moves[0].wait()
    moves[1].wait()
    projected, inverse = embed(image_near[...], image_w[...])
    image_emb[...] = (projected * inverse).astype(bf16)
    image_projected[...] = projected
    image_inverse[...] = inverse
    moves[2].wait()
    moves[3].wait()

    def with_labels(sigmoid):
        column = lax.broadcasted_iota(jnp.int32, (2 * rows, rows), 0)
        own = (column == position[...]).astype(f32)
        other = (column == position_other[...] + rows).astype(f32)
        return sigmoid - jnp.concatenate([own, other], axis=1).T

    visit(log_scale, shift, text_near, text_w, image_emb, with_labels, back, grad, None)

    @pl.when(on_text())
    def _():
        add_head(head, text_near, back, None)


def choose_kernel(below, above, done_first, out):
    core = core_place()[0]

    @pl.when(core == 1)
    def _():
        out[...] = below[...]

    @pl.when(core == 0)
    def _():
        out[...] = above[...]


def pair_kernel(
    log_scale, shift, below, above, text_w, image_emb, grad_before, head_before,
    grad, head, x, back,
):
    rows = below.shape[0]
    x[pl.ds(0, rows), :] = below[...]
    x[pl.ds(rows, rows), :] = above[...]
    visit(log_scale, shift, x, text_w, image_emb, lambda c: c, back, grad, grad_before)

    @pl.when(on_text())
    def _():
        add_head(head, x, back, head_before)


def far_kernel(
    log_scale, shift, far, far_other, text_w, image_emb, grad_before, head_before,
    image_near, image_projected, image_inverse,
    own, right_top, right_bottom, left_top, left_bottom, far_right, far_left,
    grad, head, x, back,
):
    rows = far.shape[0]
    x[pl.ds(0, rows), :] = far[...]
    x[pl.ds(rows, rows), :] = far_other[...]

    def inside(sigmoid):
        row = lax.broadcasted_iota(jnp.int32, sigmoid.shape, 0) < rows
        column = lax.broadcasted_iota(jnp.int32, sigmoid.shape, 1) < rows
        return jnp.where(row == column, sigmoid, 0.0)

    visit(log_scale, shift, x, text_w, image_emb, inside, back, grad, grad_before)

    @pl.when(on_text())
    def _():
        add_head(head, x, back, head_before)

    @pl.when(jnp.logical_not(on_text()))
    def _():
        gradient = factor(log_scale) * grad[...]
        inverse = image_inverse[...]
        unit = image_projected[...] * inverse
        radial = jnp.sum(gradient * unit, axis=-1, keepdims=True)
        back[...] = ((gradient - unit * radial) * inverse).astype(bf16)
        add_head(head, image_near, back, None)

    slab = head.shape[0] // 4
    half = slab // 2
    place = core_place()[1]

    def part(turn, upper, size):
        start = lax.rem(place + turn, 4) * slab + upper
        return head[pl.ds(pl.multiple_of(start, 16), size), :].astype(bf16)

    far_right[...] = part(2, 0, half)
    far_left[...] = part(2, half, half)
    right_top[...] = part(1, 0, half)
    right_bottom[...] = part(1, half, half)
    left_top[...] = part(3, 0, half)
    left_bottom[...] = part(3, half, half)
    own[...] = part(0, 0, slab)


def add_kernel(a, b, c, d, ab, cd):
    ab[...] = (a[...].astype(f32) + b[...].astype(f32)).astype(bf16)
    cd[...] = (c[...].astype(f32) + d[...].astype(f32)).astype(bf16)


def join_kernel(own, a_top, a_bottom, b_top, b_bottom, out):
    half = a_top.shape[0]
    upper, lower = pl.ds(0, half), pl.ds(half, half)
    out[upper, :] = (
        own[upper, :].astype(f32) + a_top[...].astype(f32) + b_top[...].astype(f32)
    ).astype(bf16)
    out[lower, :] = (
        own[lower, :].astype(f32) + a_bottom[...].astype(f32) + b_bottom[...].astype(f32)
    ).astype(bf16)


PIECES = [(0, 0), (3, 0), (1, 1), (3, 1), (1, 0), (2, 0), (2, 1)]


def write_kernel(*refs):
    count = len(PIECES)
    mine, theirs, (text, image, sems) = refs[:count], refs[count : 2 * count], refs[2 * count :]
    core, place, other_place = core_place()
    slab = mine[0].shape[0]

    def copies(pieces, position, out, first):
        moves = []
        for k, (piece, (turn, part)) in enumerate(zip(pieces, PIECES)):
            start = lax.rem(position + turn, 4) * slab + part * (slab // 2)
            target = out.at[pl.ds(pl.multiple_of(start, 16), piece.shape[0]), :]
            moves.append(pltpu.make_async_copy(piece, target, sems.at[first + k]))
        return moves

    def go(moves):
        for move in moves:
            move.start()
        for move in moves:
            move.wait()

    @pl.when(core == TEXT)
    def _():
        go(copies(mine, place, text, 0) + copies(theirs, other_place, image, count))

    @pl.when(core != TEXT)
    def _():
        go(copies(mine, place, image, 0) + copies(theirs, other_place, text, count))


def on_device(text_x, image_x, text_w, image_w, position, log_scale, shift):
    rows, width = text_x.shape
    depth = text_w.shape[0]
    slab = depth // 4
    half = slab // 2
    scalars = (log_scale, shift)
    block = ((rows, width), bf16)
    pair, pair_f32 = ((2 * rows, width), bf16), ((2 * rows, width), f32)
    total = ((depth, width), f32)
    matrix = ((depth, width), bf16)
    piece, half_piece = ((slab, width), bf16), ((half, width), bf16)
    with jax.named_scope("band_exchange"):
        text_other = send(text_x, SWAP)
        image_other = send(image_x, SWAP)
        position_other = send(position, SWAP)
        below = send(text_x, shifted(2))
        above = send(text_x, shifted(-2))
    with jax.named_scope("near"):
        image_near, weight, image_emb, image_projected, image_inverse, grad, head = call(
            near_kernel,
            [pair, matrix, pair, pair_f32, ((2 * rows, 1), f32), pair_f32, total],
            [
                pltpu.VMEM(*pair),
                pltpu.VMEM(*matrix),
                pltpu.VMEM(*pair),
                pltpu.SemaphoreType.DMA((4,)),
            ],
            flops=4 * 10**9,
        )(
            scalars, (text_x, image_x, text_w, image_w), text_other, image_other,
            position[None], position_other[None],
        )
    with jax.named_scope("forward"):
        [onward] = call(choose_kernel, [block])((), (), below, above, image_inverse)
        far = send(onward, FORWARD)
        below_other = send(below, SWAP)
        above_other = send(above, SWAP)
    visits = call(
        pair_kernel, [pair_f32, total], [pltpu.VMEM(*pair), pltpu.VMEM(*pair)], flops=4 * 10**9
    )
    with jax.named_scope("received"):
        grad, head = visits(scalars, (), below, above, weight, image_emb, grad, head)
    with jax.named_scope("partners"):
        grad, head = visits(scalars, (), below_other, above_other, weight, image_emb, grad, head)
    with jax.named_scope("far"):
        far_other = send(far, SWAP)
        own, right_top, right_bottom, left_top, left_bottom, far_right, far_left = call(
            far_kernel,
            [piece] + [half_piece] * 6,
            [pltpu.VMEM(*pair_f32), pltpu.VMEM(*total), pltpu.VMEM(*pair), pltpu.VMEM(*pair)],
            flops=4 * 10**9,
        )(
            scalars, (), far, far_other, weight, image_emb, grad, head, image_near,
            image_projected, image_inverse,
        )
    with jax.named_scope("sum_first"):
        from_left = send(far_right, RIGHT)
        from_right = send(far_left, LEFT)
        a_bottom = send(right_bottom, RIGHT)
        b_top = send(left_top, LEFT)
        right_top, left_bottom = call(add_kernel, [half_piece] * 2)(
            (), (), right_top, from_left, left_bottom, from_right
        )
        a_top = send(right_top, RIGHT)
        b_bottom = send(left_bottom, LEFT)
        [part] = call(join_kernel, [piece])((), (), own, a_top, a_bottom, b_top, b_bottom)
    with jax.named_scope("sum_second"):
        part = exchange(part.reshape(4, slab // 4, width), SECOND)
        part = jnp.sum(part.astype(f32), axis=0).astype(bf16)
    with jax.named_scope("sum_lines"):
        tiles = (
            part.reshape(slab // 32, 8, width // 128, 128).transpose(0, 2, 1, 3).reshape(-1, 8, 128)
        )
        count = tiles.shape[0]
        each = -(-count // NZ)
        tiles = jnp.concatenate([tiles, jnp.zeros((each * NZ - count, 8, 128), bf16)])
        tiles = exchange(tiles, LINES).reshape(NZ, each, 8, 128)
        tiles = jnp.sum(tiles.astype(f32), axis=0).astype(bf16)
    with jax.named_scope("share_lines"):
        tiles = exchange(jnp.tile(tiles, (NZ, 1, 1)), LINES)[:count]
        part = (
            tiles.reshape(slab // 32, width // 128, 8, 128).transpose(0, 2, 1, 3).reshape(-1, width)
        )
    with jax.named_scope("share_second"):
        own = exchange(jnp.tile(part[None], (4, 1, 1)), SECOND).reshape(slab, width)
    with jax.named_scope("share_first"):
        top, bottom = own[:half], own[half:]
        left_top = send(top, RIGHT)
        right_bottom = send(bottom, LEFT)
        left_bottom = send(bottom, RIGHT)
        right_top = send(top, LEFT)
        across_top = send(left_top, RIGHT)
        across_bottom = send(right_bottom, LEFT)
        mine = [own, left_top, right_bottom, left_bottom, right_top, across_top, across_bottom]
        theirs = [send(one, SWAP) for one in mine]
    with jax.named_scope("write"):
        return call(
            write_kernel,
            [matrix, matrix],
            [pltpu.SemaphoreType.DMA((2 * len(PIECES),))],
            result=pltpu.HBM,
        )((), (), *mine, *theirs)


def solution(mesh):
    return jax.shard_map(
        on_device,
        mesh=mesh,
        in_specs=(P("dp", None), P("dp", None), P(), P(), P("dp"), P(), P()),
        out_specs=(P(), P()),
        check_vma=False,
    )
```

```python
import jax
import jax.numpy as jnp
from jax import lax
from jax.experimental import pallas as pl
from jax.experimental.pallas import tpu as pltpu
from jax.sharding import PartitionSpec as P

NY, NX, NZ, CORES = 4, 4, 8, 2
N = NY * NX * NZ * CORES
epsilon = 1e-06
bf16, f32 = jnp.bfloat16, jnp.float32
MIB = 1 << 20


def index(y, x, z, c):
    return ((y % NY * NX + x % NX) * NZ + z % NZ) * CORES + c


PLACES = [
    (y, x, z, c) for y in range(NY) for x in range(NX) for z in range(NZ) for c in range(CORES)
]


def route(move):
    return [(index(*place), index(*move(*place))) for place in PLACES]


def groups(key):
    found = {}
    for place in PLACES:
        found.setdefault(key(*place), []).append(index(*place))
    return list(found.values())


def along_first(step):
    return route(lambda y, x, z, c: (y, x + step, z, c) if c == 0 else (y + step, x, z, c))


SWAP = route(lambda y, x, z, c: (y, x, z, 1 - c))
RIGHT, LEFT = along_first(1), along_first(-1)
SECOND = groups(lambda y, x, z, c: (c, z, x if c == 0 else y))
LINES = groups(lambda y, x, z, c: (c, x, y))
FAR = [(i, (i + 3) % N if i % 2 else (i - 3) % N) for i in range(N)]
TEXT = 1


def shifted(distance):
    return [(i, (i + distance) % N) for i in range(N)]


def send(block, pairs):
    return lax.ppermute(block, "dp", pairs)


def exchange(parts, members):
    return lax.all_to_all(parts, "dp", 0, 0, axis_index_groups=members, tiled=True)


def call(body, outs, scratch=(), flops=0, result=pltpu.VMEM, aliases=()):
    def run(smem, outside, *arrays):
        specs = (
            [pl.BlockSpec(memory_space=pltpu.SMEM)] * len(smem)
            + [pl.BlockSpec(memory_space=pltpu.HBM)] * len(outside)
            + [pl.BlockSpec(memory_space=pltpu.VMEM)] * len(arrays)
        )
        held = [pltpu.with_memory_space_constraint(a, pltpu.VMEM) for a in arrays]
        outside = [pltpu.with_memory_space_constraint(a, pltpu.HBM) for a in outside]
        return pl.pallas_call(
            body,
            out_shape=[jax.ShapeDtypeStruct(s, d) for s, d in outs],
            in_specs=specs,
            out_specs=[pl.BlockSpec(memory_space=result)] * len(outs),
            scratch_shapes=list(scratch),
            input_output_aliases=dict(aliases),
            cost_estimate=pl.CostEstimate(flops=flops, bytes_accessed=0, transcendentals=0),
            compiler_params=pltpu.CompilerParams(vmem_limit_bytes=32 * MIB),
        )(*smem, *outside, *held)

    return run


def contract(a, b, da, db):
    return lax.dot_general(a, b, (((da,), (db,)), ((), ())), preferred_element_type=f32)


def core_place():
    me = lax.axis_index("dp")
    core = lax.rem(me, CORES)
    x = lax.rem(me // (NZ * CORES), NX)
    y = me // (NX * NZ * CORES)
    return core, jnp.where(core == 0, x, y), jnp.where(core == 0, y, x)


def on_text():
    return core_place()[0] == TEXT


def factor(log_scale):
    return jnp.exp(jnp.full((1, 1), log_scale[0], f32))


def embed(features, weight):
    projected = jnp.dot(features, weight, preferred_element_type=f32)
    square = jnp.sum(projected * projected, axis=-1, keepdims=True)
    inverse = 1.0 / jnp.sqrt(square + epsilon)
    return projected, inverse


def add_head(head, x, back, before):
    step = head.shape[0] // 3
    for k in range(3):
        at = pl.ds(k * step, step)
        new = contract(x[:, at], back[...], 0, 0)
        head[at, :] = new if before is None else before[at, :] + new


def visit(log_scale, shift, x, text_w, image_emb, finish, back, grad, grad_before):
    scale = factor(log_scale)
    projected, inverse = embed(x[...], text_w[...])
    emb = (projected * inverse).astype(bf16)
    similarity = contract(emb, image_emb[...], 1, 1)
    coefficient = finish(jax.nn.sigmoid(scale * similarity + shift[0])).astype(bf16)

    @pl.when(on_text())
    def _():
        radial = jnp.sum(coefficient.astype(f32) * similarity, axis=-1, keepdims=True)
        gradient = jnp.dot(coefficient, image_emb[...], preferred_element_type=f32)
        outer = scale * inverse
        back[...] = (gradient * outer - projected * (outer * inverse * radial)).astype(bf16)

    @pl.when(jnp.logical_not(on_text()))
    def _():
        share = contract(coefficient, emb, 0, 0)
        grad[...] = share if grad_before is None else grad_before[...] + share


def near_kernel(
    log_scale, shift, text_hbm, image_hbm, text_w_hbm, image_w_hbm, text_other, image_other,
    position, position_other,
    image_near, text_w, image_emb, image_projected, image_inverse, grad, head,
    text_near, image_w, back, sems,
):
    rows = text_other.shape[0]
    first, second = pl.ds(0, rows), pl.ds(rows, rows)
    moves = [
        pltpu.make_async_copy(image_hbm, image_near.at[first, :], sems.at[0]),
        pltpu.make_async_copy(image_w_hbm, image_w, sems.at[1]),
        pltpu.make_async_copy(text_hbm, text_near.at[first, :], sems.at[2]),
        pltpu.make_async_copy(text_w_hbm, text_w, sems.at[3]),
    ]
    for move in moves:
        move.start()
    image_near[second, :] = image_other[...]
    text_near[second, :] = text_other[...]
    moves[0].wait()
    moves[1].wait()
    projected, inverse = embed(image_near[...], image_w[...])
    image_emb[...] = (projected * inverse).astype(bf16)
    image_projected[...] = projected
    image_inverse[...] = inverse
    moves[2].wait()
    moves[3].wait()

    def with_labels(sigmoid):
        column = lax.broadcasted_iota(jnp.int32, (2 * rows, rows), 0)
        own = (column == position[...]).astype(f32)
        other = (column == position_other[...] + rows).astype(f32)
        return sigmoid - jnp.concatenate([own, other], axis=1).T

    visit(log_scale, shift, text_near, text_w, image_emb, with_labels, back, grad, None)

    @pl.when(on_text())
    def _():
        add_head(head, text_near, back, None)


def gate_kernel(*refs):
    pass


def after(token, *arrays):
    outs = [(a.shape, a.dtype) for a in arrays]
    return call(gate_kernel, outs, aliases=[(k, k) for k in range(len(arrays))])(
        (), (), *arrays, token
    )


def pair_kernel(
    log_scale, shift, below, above, text_w, image_emb, grad_before, head_before,
    grad, head, x, back,
):
    rows = below.shape[0]
    x[pl.ds(0, rows), :] = below[...]
    x[pl.ds(rows, rows), :] = above[...]
    visit(log_scale, shift, x, text_w, image_emb, lambda c: c, back, grad, grad_before)

    @pl.when(on_text())
    def _():
        add_head(head, x, back, head_before)


def far_kernel(
    log_scale, shift, far, far_other, text_w, image_emb, grad_before, head_before,
    image_near, image_projected, image_inverse,
    own, right_top, right_bottom, left_top, left_bottom, far_right, far_left,
    grad, head, x, back,
):
    rows = far.shape[0]
    x[pl.ds(0, rows), :] = far[...]
    x[pl.ds(rows, rows), :] = far_other[...]

    def inside(sigmoid):
        row = lax.broadcasted_iota(jnp.int32, sigmoid.shape, 0) < rows
        column = lax.broadcasted_iota(jnp.int32, sigmoid.shape, 1) < rows
        return jnp.where(row == column, sigmoid, 0.0)

    visit(log_scale, shift, x, text_w, image_emb, inside, back, grad, grad_before)

    @pl.when(on_text())
    def _():
        add_head(head, x, back, head_before)

    @pl.when(jnp.logical_not(on_text()))
    def _():
        gradient = factor(log_scale) * grad[...]
        inverse = image_inverse[...]
        unit = image_projected[...] * inverse
        radial = jnp.sum(gradient * unit, axis=-1, keepdims=True)
        back[...] = ((gradient - unit * radial) * inverse).astype(bf16)
        add_head(head, image_near, back, None)

    slab = head.shape[0] // 4
    half = slab // 2
    place = core_place()[1]

    def part(turn, upper, size):
        start = lax.rem(place + turn, 4) * slab + upper
        return head[pl.ds(pl.multiple_of(start, 16), size), :].astype(bf16)

    far_right[...] = part(2, 0, half)
    far_left[...] = part(2, half, half)
    right_top[...] = part(1, 0, half)
    right_bottom[...] = part(1, half, half)
    left_top[...] = part(3, 0, half)
    left_bottom[...] = part(3, half, half)
    own[...] = part(0, 0, slab)


def add_kernel(a, b, c, d, ab, cd):
    ab[...] = (a[...].astype(f32) + b[...].astype(f32)).astype(bf16)
    cd[...] = (c[...].astype(f32) + d[...].astype(f32)).astype(bf16)


def join_kernel(own, a_top, a_bottom, b_top, b_bottom, out):
    half = a_top.shape[0]
    upper, lower = pl.ds(0, half), pl.ds(half, half)
    out[upper, :] = (
        own[upper, :].astype(f32) + a_top[...].astype(f32) + b_top[...].astype(f32)
    ).astype(bf16)
    out[lower, :] = (
        own[lower, :].astype(f32) + a_bottom[...].astype(f32) + b_bottom[...].astype(f32)
    ).astype(bf16)


PIECES = [(0, 0), (3, 0), (1, 1), (3, 1), (1, 0), (2, 0), (2, 1)]


def write_kernel(*refs):
    count = len(PIECES)
    mine, theirs, (text, image, sems) = refs[:count], refs[count : 2 * count], refs[2 * count :]
    core, place, other_place = core_place()
    slab = mine[0].shape[0]

    def copies(pieces, position, out, first):
        moves = []
        for k, (piece, (turn, part)) in enumerate(zip(pieces, PIECES)):
            start = lax.rem(position + turn, 4) * slab + part * (slab // 2)
            target = out.at[pl.ds(pl.multiple_of(start, 16), piece.shape[0]), :]
            moves.append(pltpu.make_async_copy(piece, target, sems.at[first + k]))
        return moves

    def go(moves):
        for move in moves:
            move.start()
        for move in moves:
            move.wait()

    @pl.when(core == TEXT)
    def _():
        go(copies(mine, place, text, 0) + copies(theirs, other_place, image, count))

    @pl.when(core != TEXT)
    def _():
        go(copies(mine, place, image, 0) + copies(theirs, other_place, text, count))


def on_device(text_x, image_x, text_w, image_w, position, log_scale, shift):
    rows, width = text_x.shape
    depth = text_w.shape[0]
    slab = depth // 4
    half = slab // 2
    scalars = (log_scale, shift)
    pair, pair_f32 = ((2 * rows, width), bf16), ((2 * rows, width), f32)
    total = ((depth, width), f32)
    matrix = ((depth, width), bf16)
    piece, half_piece = ((slab, width), bf16), ((half, width), bf16)
    with jax.named_scope("band_exchange"):
        text_other = send(text_x, SWAP)
        image_other = send(image_x, SWAP)
        position_other = send(position, SWAP)
        below = send(text_x, shifted(2))
        above = send(text_x, shifted(-2))
        far = send(text_x, FAR)
    with jax.named_scope("near"):
        image_near, weight, image_emb, image_projected, image_inverse, grad, head = call(
            near_kernel,
            [pair, matrix, pair, pair_f32, ((2 * rows, 1), f32), pair_f32, total],
            [
                pltpu.VMEM(*pair),
                pltpu.VMEM(*matrix),
                pltpu.VMEM(*pair),
                pltpu.SemaphoreType.DMA((4,)),
            ],
            flops=4 * 10**9,
        )(
            scalars, (text_x, image_x, text_w, image_w), text_other, image_other,
            position[None], position_other[None],
        )
    with jax.named_scope("swap_neighbours"):
        below, above = after(image_inverse, below, above)
        below_other = send(below, SWAP)
        above_other = send(above, SWAP)
    visits = call(
        pair_kernel, [pair_f32, total], [pltpu.VMEM(*pair), pltpu.VMEM(*pair)], flops=4 * 10**9
    )
    with jax.named_scope("received"):
        grad, head = visits(scalars, (), below, above, weight, image_emb, grad, head)
    with jax.named_scope("partners"):
        grad, head = visits(scalars, (), below_other, above_other, weight, image_emb, grad, head)
    with jax.named_scope("far"):
        far_other = send(far, SWAP)
        own, right_top, right_bottom, left_top, left_bottom, far_right, far_left = call(
            far_kernel,
            [piece] + [half_piece] * 6,
            [pltpu.VMEM(*pair_f32), pltpu.VMEM(*total), pltpu.VMEM(*pair), pltpu.VMEM(*pair)],
            flops=4 * 10**9,
        )(
            scalars, (), far, far_other, weight, image_emb, grad, head, image_near,
            image_projected, image_inverse,
        )
    with jax.named_scope("sum_first"):
        from_left = send(far_right, RIGHT)
        from_right = send(far_left, LEFT)
        a_bottom = send(right_bottom, RIGHT)
        b_top = send(left_top, LEFT)
        right_top, left_bottom = call(add_kernel, [half_piece] * 2)(
            (), (), right_top, from_left, left_bottom, from_right
        )
        a_top = send(right_top, RIGHT)
        b_bottom = send(left_bottom, LEFT)
        [part] = call(join_kernel, [piece])((), (), own, a_top, a_bottom, b_top, b_bottom)
    with jax.named_scope("sum_second"):
        part = exchange(part.reshape(4, slab // 4, width), SECOND)
        part = jnp.sum(part.astype(f32), axis=0).astype(bf16)
    with jax.named_scope("sum_lines"):
        tiles = (
            part.reshape(slab // 32, 8, width // 128, 128).transpose(0, 2, 1, 3).reshape(-1, 8, 128)
        )
        count = tiles.shape[0]
        each = -(-count // NZ)
        tiles = jnp.concatenate([tiles, jnp.zeros((each * NZ - count, 8, 128), bf16)])
        tiles = exchange(tiles, LINES).reshape(NZ, each, 8, 128)
        tiles = jnp.sum(tiles.astype(f32), axis=0).astype(bf16)
    with jax.named_scope("share_lines"):
        tiles = exchange(jnp.tile(tiles, (NZ, 1, 1)), LINES)[:count]
        part = (
            tiles.reshape(slab // 32, width // 128, 8, 128).transpose(0, 2, 1, 3).reshape(-1, width)
        )
    with jax.named_scope("share_second"):
        own = exchange(jnp.tile(part[None], (4, 1, 1)), SECOND).reshape(slab, width)
    with jax.named_scope("share_first"):
        top, bottom = own[:half], own[half:]
        left_top = send(top, RIGHT)
        right_top = send(top, LEFT)
        left_bottom = send(bottom, RIGHT)
        right_bottom = send(bottom, LEFT)
        own_other = send(own, SWAP)
        across_top = send(left_top, RIGHT)
        across_bottom = send(right_bottom, LEFT)
        mine = [left_top, right_bottom, left_bottom, right_top, across_top, across_bottom]
        theirs = [own_other] + [send(one, SWAP) for one in mine]
        mine = [own] + mine
    with jax.named_scope("write"):
        return call(
            write_kernel,
            [matrix, matrix],
            [pltpu.SemaphoreType.DMA((2 * len(PIECES),))],
            result=pltpu.HBM,
        )((), (), *mine, *theirs)


def solution(mesh):
    return jax.shard_map(
        on_device,
        mesh=mesh,
        in_specs=(P("dp", None), P("dp", None), P(), P(), P("dp"), P(), P()),
        out_specs=(P(), P()),
        check_vma=False,
    )
```

```python
import jax
import jax.numpy as jnp
from jax import lax
from jax.experimental import pallas as pl
from jax.experimental.pallas import tpu as pltpu
from jax.sharding import PartitionSpec as P

NY, NX, NZ, CORES = 4, 4, 8, 2
N = NY * NX * NZ * CORES
epsilon = 1e-06
bf16, f32 = jnp.bfloat16, jnp.float32
MIB = 1 << 20


def index(y, x, z, c):
    return ((y % NY * NX + x % NX) * NZ + z % NZ) * CORES + c


PLACES = [
    (y, x, z, c) for y in range(NY) for x in range(NX) for z in range(NZ) for c in range(CORES)
]


def route(move):
    return [(index(*place), index(*move(*place))) for place in PLACES]


def groups(key):
    found = {}
    for place in PLACES:
        found.setdefault(key(*place), []).append(index(*place))
    return list(found.values())


def along_first(step):
    return route(lambda y, x, z, c: (y, x + step, z, c) if c == 0 else (y + step, x, z, c))


SWAP = route(lambda y, x, z, c: (y, x, z, 1 - c))
RIGHT, LEFT = along_first(1), along_first(-1)
SECOND = groups(lambda y, x, z, c: (c, z, x if c == 0 else y))
LINES = groups(lambda y, x, z, c: (c, x, y))
FAR = [(i, (i + 3) % N if i % 2 else (i - 3) % N) for i in range(N)]
TEXT = 1


def shifted(distance):
    return [(i, (i + distance) % N) for i in range(N)]


def send(block, pairs):
    return lax.ppermute(block, "dp", pairs)


def exchange(parts, members):
    return lax.all_to_all(parts, "dp", 0, 0, axis_index_groups=members, tiled=True)


def call(body, outs, scratch=(), flops=0, result=pltpu.VMEM, aliases=()):
    def run(smem, outside, *arrays):
        specs = (
            [pl.BlockSpec(memory_space=pltpu.SMEM)] * len(smem)
            + [pl.BlockSpec(memory_space=pltpu.HBM)] * len(outside)
            + [pl.BlockSpec(memory_space=pltpu.VMEM)] * len(arrays)
        )
        held = [pltpu.with_memory_space_constraint(a, pltpu.VMEM) for a in arrays]
        outside = [pltpu.with_memory_space_constraint(a, pltpu.HBM) for a in outside]
        return pl.pallas_call(
            body,
            out_shape=[jax.ShapeDtypeStruct(s, d) for s, d in outs],
            in_specs=specs,
            out_specs=[pl.BlockSpec(memory_space=result)] * len(outs),
            scratch_shapes=list(scratch),
            input_output_aliases=dict(aliases),
            cost_estimate=pl.CostEstimate(flops=flops, bytes_accessed=0, transcendentals=0),
            compiler_params=pltpu.CompilerParams(vmem_limit_bytes=32 * MIB),
        )(*smem, *outside, *held)

    return run


def contract(a, b, da, db):
    return lax.dot_general(a, b, (((da,), (db,)), ((), ())), preferred_element_type=f32)


def core_place():
    me = lax.axis_index("dp")
    core = lax.rem(me, CORES)
    x = lax.rem(me // (NZ * CORES), NX)
    y = me // (NX * NZ * CORES)
    return core, jnp.where(core == 0, x, y), jnp.where(core == 0, y, x)


def on_text():
    return core_place()[0] == TEXT


def factor(log_scale):
    return jnp.exp(jnp.full((1, 1), log_scale[0], f32))


def embed(features, weight):
    projected = jnp.dot(features, weight, preferred_element_type=f32)
    square = jnp.sum(projected * projected, axis=-1, keepdims=True)
    inverse = 1.0 / jnp.sqrt(square + epsilon)
    return projected, inverse


def add_head(head, x, back, before):
    step = head.shape[0] // 3
    for k in range(3):
        at = pl.ds(k * step, step)
        new = contract(x[:, at], back[...], 0, 0)
        head[at, :] = new if before is None else before[at, :] + new


def visit(log_scale, shift, x, text_w, image_emb, finish, back, grad, grad_before):
    scale = factor(log_scale)
    projected, inverse = embed(x[...], text_w[...])
    emb = (projected * inverse).astype(bf16)
    similarity = contract(emb, image_emb[...], 1, 1)
    coefficient = finish(jax.nn.sigmoid(scale * similarity + shift[0])).astype(bf16)

    @pl.when(on_text())
    def _():
        radial = jnp.sum(coefficient.astype(f32) * similarity, axis=-1, keepdims=True)
        gradient = jnp.dot(coefficient, image_emb[...], preferred_element_type=f32)
        outer = scale * inverse
        back[...] = (gradient * outer - projected * (outer * inverse * radial)).astype(bf16)

    @pl.when(jnp.logical_not(on_text()))
    def _():
        share = contract(coefficient, emb, 0, 0)
        grad[...] = share if grad_before is None else grad_before[...] + share


def near_kernel(
    log_scale, shift, text_hbm, image_hbm, text_w_hbm, image_w_hbm, text_other, image_other,
    position, position_other,
    image_near, text_w, image_emb, image_projected, image_inverse, grad, head,
    text_near, image_w, back, sems,
):
    rows = text_other.shape[0]
    first, second = pl.ds(0, rows), pl.ds(rows, rows)
    moves = [
        pltpu.make_async_copy(image_hbm, image_near.at[first, :], sems.at[0]),
        pltpu.make_async_copy(image_w_hbm, image_w, sems.at[1]),
        pltpu.make_async_copy(text_hbm, text_near.at[first, :], sems.at[2]),
        pltpu.make_async_copy(text_w_hbm, text_w, sems.at[3]),
    ]
    for move in moves:
        move.start()
    image_near[second, :] = image_other[...]
    text_near[second, :] = text_other[...]
    moves[0].wait()
    moves[1].wait()
    projected, inverse = embed(image_near[...], image_w[...])
    image_emb[...] = (projected * inverse).astype(bf16)
    image_projected[...] = projected
    image_inverse[...] = inverse
    moves[2].wait()
    moves[3].wait()

    def with_labels(sigmoid):
        column = lax.broadcasted_iota(jnp.int32, (2 * rows, rows), 0)
        own = (column == position[...]).astype(f32)
        other = (column == position_other[...] + rows).astype(f32)
        return sigmoid - jnp.concatenate([own, other], axis=1).T

    visit(log_scale, shift, text_near, text_w, image_emb, with_labels, back, grad, None)

    @pl.when(on_text())
    def _():
        add_head(head, text_near, back, None)


def gate_kernel(*refs):
    pass


def after(token, *arrays, in_hbm=False):
    outs = [(a.shape, a.dtype) for a in arrays]
    first = 1 if in_hbm else 0
    gate = call(gate_kernel, outs, aliases=[(first + k, k) for k in range(len(arrays))])
    return gate((), (token,), *arrays) if in_hbm else gate((), (), *arrays, token)


def pair_kernel(
    log_scale, shift, below, above, text_w, image_emb, grad_before, head_before,
    grad, head, x, back,
):
    rows = below.shape[0]
    x[pl.ds(0, rows), :] = below[...]
    x[pl.ds(rows, rows), :] = above[...]
    visit(log_scale, shift, x, text_w, image_emb, lambda c: c, back, grad, grad_before)

    @pl.when(on_text())
    def _():
        add_head(head, x, back, head_before)


def far_kernel(
    log_scale, shift, far, far_other, text_w, image_emb, grad_before, head_before,
    image_near, image_projected, image_inverse,
    own, right_top, right_bottom, left_top, left_bottom, far_right, far_left,
    grad, head, x, back,
):
    rows = far.shape[0]
    x[pl.ds(0, rows), :] = far[...]
    x[pl.ds(rows, rows), :] = far_other[...]

    def inside(sigmoid):
        row = lax.broadcasted_iota(jnp.int32, sigmoid.shape, 0) < rows
        column = lax.broadcasted_iota(jnp.int32, sigmoid.shape, 1) < rows
        return jnp.where(row == column, sigmoid, 0.0)

    visit(log_scale, shift, x, text_w, image_emb, inside, back, grad, grad_before)

    @pl.when(on_text())
    def _():
        add_head(head, x, back, head_before)

    @pl.when(jnp.logical_not(on_text()))
    def _():
        gradient = factor(log_scale) * grad[...]
        inverse = image_inverse[...]
        unit = image_projected[...] * inverse
        radial = jnp.sum(gradient * unit, axis=-1, keepdims=True)
        back[...] = ((gradient - unit * radial) * inverse).astype(bf16)
        add_head(head, image_near, back, None)

    slab = head.shape[0] // 4
    half = slab // 2
    place = core_place()[1]

    def part(turn, upper, size):
        start = lax.rem(place + turn, 4) * slab + upper
        return head[pl.ds(pl.multiple_of(start, 16), size), :].astype(bf16)

    far_right[...] = part(2, 0, half)
    far_left[...] = part(2, half, half)
    right_top[...] = part(1, 0, half)
    right_bottom[...] = part(1, half, half)
    left_top[...] = part(3, 0, half)
    left_bottom[...] = part(3, half, half)
    own[...] = part(0, 0, slab)


def add_kernel(a, b, c, d, ab, cd):
    ab[...] = (a[...].astype(f32) + b[...].astype(f32)).astype(bf16)
    cd[...] = (c[...].astype(f32) + d[...].astype(f32)).astype(bf16)


def join_kernel(own, a_top, a_bottom, b_top, b_bottom, out):
    half = a_top.shape[0]
    upper, lower = pl.ds(0, half), pl.ds(half, half)
    out[upper, :] = (
        own[upper, :].astype(f32) + a_top[...].astype(f32) + b_top[...].astype(f32)
    ).astype(bf16)
    out[lower, :] = (
        own[lower, :].astype(f32) + a_bottom[...].astype(f32) + b_bottom[...].astype(f32)
    ).astype(bf16)


OWN, LEFT_TOP, RIGHT_BOTTOM, LEFT_BOTTOM, RIGHT_TOP, ACROSS_TOP, ACROSS_BOTTOM = PIECES = (
    (0, 0), (3, 0), (1, 1), (3, 1), (1, 0), (2, 0), (2, 1)
)


def write(outs, mine, theirs):
    places = [*mine, *theirs]

    def body(*refs):
        pieces, (text, image, sems) = refs[len(outs) : len(outs) + len(places)], refs[-3:]
        core, place, other_place = core_place()

        def copies(first, other):
            moves = []
            for k, (piece, (turn, part)) in enumerate(zip(pieces, places)):
                own = k < len(mine)
                slab = piece.shape[0] * (1 if (turn, part) == OWN else 2)
                start = lax.rem((place if own else other_place) + turn, 4) * slab + part * slab // 2
                at = pl.ds(pl.multiple_of(start, 16), piece.shape[0])
                moves.append(
                    pltpu.make_async_copy(piece, (first if own else other).at[at, :], sems.at[k])
                )
            for move in moves:
                move.start()
            for move in moves:
                move.wait()

        @pl.when(core == TEXT)
        def _():
            copies(text, image)

        @pl.when(core != TEXT)
        def _():
            copies(image, text)

    def run(*arrays, shape):
        return call(
            body,
            [shape, shape],
            [pltpu.SemaphoreType.DMA((len(places),))],
            result=pltpu.HBM,
            aliases=[(k, k) for k in range(len(outs))],
        )((), outs, *arrays)

    return run


def on_device(text_x, image_x, text_w, image_w, position, log_scale, shift):
    rows, width = text_x.shape
    depth = text_w.shape[0]
    slab = depth // 4
    half = slab // 2
    scalars = (log_scale, shift)
    pair, pair_f32 = ((2 * rows, width), bf16), ((2 * rows, width), f32)
    total = ((depth, width), f32)
    matrix = ((depth, width), bf16)
    piece, half_piece = ((slab, width), bf16), ((half, width), bf16)
    with jax.named_scope("band_exchange"):
        text_other = send(text_x, SWAP)
        image_other = send(image_x, SWAP)
        position_other = send(position, SWAP)
        below = send(text_x, shifted(2))
        above = send(text_x, shifted(-2))
        far = send(text_x, FAR)
    with jax.named_scope("near"):
        image_near, weight, image_emb, image_projected, image_inverse, grad, head = call(
            near_kernel,
            [pair, matrix, pair, pair_f32, ((2 * rows, 1), f32), pair_f32, total],
            [
                pltpu.VMEM(*pair),
                pltpu.VMEM(*matrix),
                pltpu.VMEM(*pair),
                pltpu.SemaphoreType.DMA((4,)),
            ],
            flops=4 * 10**9,
        )(
            scalars, (text_x, image_x, text_w, image_w), text_other, image_other,
            position[None], position_other[None],
        )
    with jax.named_scope("swap_neighbours"):
        below, above = after(image_inverse, below, above)
        below_other = send(below, SWAP)
        above_other = send(above, SWAP)
    visits = call(
        pair_kernel, [pair_f32, total], [pltpu.VMEM(*pair), pltpu.VMEM(*pair)], flops=4 * 10**9
    )
    with jax.named_scope("received"):
        grad, head = visits(scalars, (), below, above, weight, image_emb, grad, head)
        [far] = after(grad, far)
        far_other = send(far, SWAP)
    with jax.named_scope("partners"):
        grad, head = visits(scalars, (), below_other, above_other, weight, image_emb, grad, head)
    with jax.named_scope("far"):
        own, right_top, right_bottom, left_top, left_bottom, far_right, far_left = call(
            far_kernel,
            [piece] + [half_piece] * 6,
            [pltpu.VMEM(*pair_f32), pltpu.VMEM(*total), pltpu.VMEM(*pair), pltpu.VMEM(*pair)],
            flops=4 * 10**9,
        )(
            scalars, (), far, far_other, weight, image_emb, grad, head, image_near,
            image_projected, image_inverse,
        )
    with jax.named_scope("sum_first"):
        from_left = send(far_right, RIGHT)
        from_right = send(far_left, LEFT)
        a_bottom = send(right_bottom, RIGHT)
        b_top = send(left_top, LEFT)
        right_top, left_bottom = call(add_kernel, [half_piece] * 2)(
            (), (), right_top, from_left, left_bottom, from_right
        )
        a_top = send(right_top, RIGHT)
        b_bottom = send(left_bottom, LEFT)
        [part] = call(join_kernel, [piece])((), (), own, a_top, a_bottom, b_top, b_bottom)
    with jax.named_scope("sum_second"):
        part = exchange(part.reshape(4, slab // 4, width), SECOND)
        part = jnp.sum(part.astype(f32), axis=0).astype(bf16)
    with jax.named_scope("sum_lines"):
        tiles = (
            part.reshape(slab // 32, 8, width // 128, 128).transpose(0, 2, 1, 3).reshape(-1, 8, 128)
        )
        count = tiles.shape[0]
        each = -(-count // NZ)
        tiles = jnp.concatenate([tiles, jnp.zeros((each * NZ - count, 8, 128), bf16)])
        tiles = exchange(tiles, LINES).reshape(NZ, each, 8, 128)
        tiles = jnp.sum(tiles.astype(f32), axis=0).astype(bf16)
    with jax.named_scope("share_lines"):
        tiles = exchange(jnp.tile(tiles, (NZ, 1, 1)), LINES)[:count]
        part = (
            tiles.reshape(slab // 32, width // 128, 8, 128).transpose(0, 2, 1, 3).reshape(-1, width)
        )
    with jax.named_scope("share_second"):
        own = exchange(jnp.tile(part[None], (4, 1, 1)), SECOND).reshape(slab, width)
    with jax.named_scope("share_first"):
        top, bottom = own[:half], own[half:]
        left_top = send(top, RIGHT)
        right_top = send(top, LEFT)
        left_bottom = send(bottom, RIGHT)
        right_bottom = send(bottom, LEFT)
        own_other = send(own, SWAP)
        across_top = send(left_top, RIGHT)
        across_bottom = send(right_bottom, LEFT)
        others = [send(piece, SWAP) for piece in (left_top, right_bottom, left_bottom, right_top)]
    with jax.named_scope("write"):
        outs = write((), [OWN, LEFT_TOP, RIGHT_BOTTOM, LEFT_BOTTOM, RIGHT_TOP], [OWN])(
            own, left_top, right_bottom, left_bottom, right_top, own_other, shape=matrix
        )
        across_top, across_bottom = after(outs[0], across_top, across_bottom, in_hbm=True)
        others += [send(across_top, SWAP), send(across_bottom, SWAP)]
        return write(tuple(outs), [ACROSS_TOP, ACROSS_BOTTOM], PIECES[1:])(
            across_top, across_bottom, *others, shape=matrix
        )


def solution(mesh):
    return jax.shard_map(
        on_device,
        mesh=mesh,
        in_specs=(P("dp", None), P("dp", None), P(), P(), P("dp"), P(), P()),
        out_specs=(P(), P()),
        check_vma=False,
    )
```

```python
import jax
import jax.numpy as jnp
from jax import lax
from jax.experimental import pallas as pl
from jax.experimental.pallas import tpu as pltpu
from jax.sharding import PartitionSpec as P

NY, NX, NZ, CORES = 4, 4, 8, 2
N = NY * NX * NZ * CORES
epsilon = 1e-06
bf16, f32 = jnp.bfloat16, jnp.float32
MIB = 1 << 20


def index(y, x, z, c):
    return ((y % NY * NX + x % NX) * NZ + z % NZ) * CORES + c


PLACES = [
    (y, x, z, c) for y in range(NY) for x in range(NX) for z in range(NZ) for c in range(CORES)
]


def route(move):
    return [(index(*place), index(*move(*place))) for place in PLACES]


def groups(key):
    found = {}
    for place in PLACES:
        found.setdefault(key(*place), []).append(index(*place))
    return list(found.values())


def along_first(step):
    return route(lambda y, x, z, c: (y, x + step, z, c) if c == 0 else (y + step, x, z, c))


SWAP = route(lambda y, x, z, c: (y, x, z, 1 - c))
RIGHT, LEFT = along_first(1), along_first(-1)
SECOND = groups(lambda y, x, z, c: (c, z, x if c == 0 else y))
LINES = groups(lambda y, x, z, c: (c, x, y))
FAR = [(i, (i + 3) % N if i % 2 else (i - 3) % N) for i in range(N)]
TAIL = 16
TEXT = 1


def shifted(distance):
    return [(i, (i + distance) % N) for i in range(N)]


def send(block, pairs):
    return lax.ppermute(block, "dp", pairs)


def exchange(parts, members):
    return lax.all_to_all(parts, "dp", 0, 0, axis_index_groups=members, tiled=True)


def call(body, outs, scratch=(), flops=0, result=pltpu.VMEM, aliases=()):
    def run(smem, outside, *arrays):
        specs = (
            [pl.BlockSpec(memory_space=pltpu.SMEM)] * len(smem)
            + [pl.BlockSpec(memory_space=pltpu.HBM)] * len(outside)
            + [pl.BlockSpec(memory_space=pltpu.VMEM)] * len(arrays)
        )
        held = [pltpu.with_memory_space_constraint(a, pltpu.VMEM) for a in arrays]
        outside = [pltpu.with_memory_space_constraint(a, pltpu.HBM) for a in outside]
        return pl.pallas_call(
            body,
            out_shape=[jax.ShapeDtypeStruct(s, d) for s, d in outs],
            in_specs=specs,
            out_specs=[pl.BlockSpec(memory_space=result)] * len(outs),
            scratch_shapes=list(scratch),
            input_output_aliases=dict(aliases),
            cost_estimate=pl.CostEstimate(flops=flops, bytes_accessed=0, transcendentals=0),
            compiler_params=pltpu.CompilerParams(vmem_limit_bytes=32 * MIB),
        )(*smem, *outside, *held)

    return run


def contract(a, b, da, db):
    return lax.dot_general(a, b, (((da,), (db,)), ((), ())), preferred_element_type=f32)


def core_place():
    me = lax.axis_index("dp")
    core = lax.rem(me, CORES)
    x = lax.rem(me // (NZ * CORES), NX)
    y = me // (NX * NZ * CORES)
    return core, jnp.where(core == 0, x, y), jnp.where(core == 0, y, x)


def on_text():
    return core_place()[0] == TEXT


def factor(log_scale):
    return jnp.exp(jnp.full((1, 1), log_scale[0], f32))


def embed(features, weight):
    projected = jnp.dot(features, weight, preferred_element_type=f32)
    square = jnp.sum(projected * projected, axis=-1, keepdims=True)
    inverse = 1.0 / jnp.sqrt(square + epsilon)
    return projected, inverse


def add_head(head, x, back, before):
    step = head.shape[0] // 3
    for k in range(3):
        at = pl.ds(k * step, step)
        new = contract(x[:, at], back[...], 0, 0)
        head[at, :] = new if before is None else before[at, :] + new


def visit(log_scale, shift, x, text_w, image_emb, finish, back, grad, grad_before):
    scale = factor(log_scale)
    projected, inverse = embed(x[...], text_w[...])
    emb = (projected * inverse).astype(bf16)
    similarity = contract(emb, image_emb[...], 1, 1)
    coefficient = finish(jax.nn.sigmoid(scale * similarity + shift[0])).astype(bf16)

    @pl.when(on_text())
    def _():
        radial = jnp.sum(coefficient.astype(f32) * similarity, axis=-1, keepdims=True)
        gradient = jnp.dot(coefficient, image_emb[...], preferred_element_type=f32)
        outer = scale * inverse
        back[...] = (gradient * outer - projected * (outer * inverse * radial)).astype(bf16)

    @pl.when(jnp.logical_not(on_text()))
    def _():
        share = contract(coefficient, emb, 0, 0)
        grad[...] = share if grad_before is None else grad_before[...] + share


def near_kernel(
    log_scale, shift, text_hbm, text_w_hbm, image_w_hbm, text_other, image_own, image_other,
    image_near, text_w, image_emb, image_projected, image_inverse, grad, head,
    text_near, image_w, back, sems,
):
    rows = text_other.shape[0]
    first, second = pl.ds(0, rows), pl.ds(rows, rows)
    moves = [
        pltpu.make_async_copy(image_w_hbm, image_w, sems.at[0]),
        pltpu.make_async_copy(text_hbm, text_near.at[first, :], sems.at[1]),
        pltpu.make_async_copy(text_w_hbm, text_w, sems.at[2]),
    ]
    for move in moves:
        move.start()
    image_near[first, :] = image_own[first, :]
    image_near[second, :] = image_other[first, :]
    text_near[second, :] = text_other[...]
    moves[0].wait()
    projected, inverse = embed(image_near[...], image_w[...])
    image_emb[...] = (projected * inverse).astype(bf16)
    image_projected[...] = projected
    image_inverse[...] = inverse
    moves[1].wait()
    moves[2].wait()

    def with_labels(sigmoid):
        column = lax.broadcasted_iota(jnp.int32, (2 * rows, rows), 0)

        def positions(block):
            tail = block[pl.ds(rows, TAIL), pl.ds(0, rows)]
            return tail.astype(f32)[:1].astype(jnp.int32)

        own = (column == positions(image_own)).astype(f32)
        other = (column == positions(image_other) + rows).astype(f32)
        return sigmoid - jnp.concatenate([own, other], axis=1).T

    visit(log_scale, shift, text_near, text_w, image_emb, with_labels, back, grad, None)

    @pl.when(on_text())
    def _():
        add_head(head, text_near, back, None)


def gate_kernel(*refs):
    pass


def after(token, *arrays, in_hbm=False):
    outs = [(a.shape, a.dtype) for a in arrays]
    first = 1 if in_hbm else 0
    gate = call(gate_kernel, outs, aliases=[(first + k, k) for k in range(len(arrays))])
    return gate((), (token,), *arrays) if in_hbm else gate((), (), *arrays, token)


def pair_kernel(
    log_scale, shift, below, above, text_w, image_emb, grad_before, head_before,
    grad, head, x, back,
):
    rows = below.shape[0]
    x[pl.ds(0, rows), :] = below[...]
    x[pl.ds(rows, rows), :] = above[...]
    visit(log_scale, shift, x, text_w, image_emb, lambda c: c, back, grad, grad_before)

    @pl.when(on_text())
    def _():
        add_head(head, x, back, head_before)


def far_kernel(
    log_scale, shift, far, far_other, text_w, image_emb, grad_before, head_before,
    image_near, image_projected, image_inverse,
    own, right_top, right_bottom, left_top, left_bottom, far_right, far_left,
    grad, head, x, back,
):
    rows = far.shape[0]
    x[pl.ds(0, rows), :] = far[...]
    x[pl.ds(rows, rows), :] = far_other[...]

    def inside(sigmoid):
        row = lax.broadcasted_iota(jnp.int32, sigmoid.shape, 0) < rows
        column = lax.broadcasted_iota(jnp.int32, sigmoid.shape, 1) < rows
        return jnp.where(row == column, sigmoid, 0.0)

    visit(log_scale, shift, x, text_w, image_emb, inside, back, grad, grad_before)

    @pl.when(on_text())
    def _():
        add_head(head, x, back, head_before)

    @pl.when(jnp.logical_not(on_text()))
    def _():
        gradient = factor(log_scale) * grad[...]
        inverse = image_inverse[...]
        unit = image_projected[...] * inverse
        radial = jnp.sum(gradient * unit, axis=-1, keepdims=True)
        back[...] = ((gradient - unit * radial) * inverse).astype(bf16)
        add_head(head, image_near, back, None)

    slab = head.shape[0] // 4
    half = slab // 2
    place = core_place()[1]

    def part(turn, upper, size):
        start = lax.rem(place + turn, 4) * slab + upper
        return head[pl.ds(pl.multiple_of(start, 16), size), :].astype(bf16)

    far_right[...] = part(2, 0, half)
    far_left[...] = part(2, half, half)
    right_top[...] = part(1, 0, half)
    right_bottom[...] = part(1, half, half)
    left_top[...] = part(3, 0, half)
    left_bottom[...] = part(3, half, half)
    own[...] = part(0, 0, slab)


def add_kernel(a, b, c, d, ab, cd):
    ab[...] = (a[...].astype(f32) + b[...].astype(f32)).astype(bf16)
    cd[...] = (c[...].astype(f32) + d[...].astype(f32)).astype(bf16)


def join_kernel(own, a_top, a_bottom, b_top, b_bottom, out):
    half = a_top.shape[0]
    upper, lower = pl.ds(0, half), pl.ds(half, half)
    out[upper, :] = (
        own[upper, :].astype(f32) + a_top[...].astype(f32) + b_top[...].astype(f32)
    ).astype(bf16)
    out[lower, :] = (
        own[lower, :].astype(f32) + a_bottom[...].astype(f32) + b_bottom[...].astype(f32)
    ).astype(bf16)


OWN, LEFT_TOP, RIGHT_BOTTOM, LEFT_BOTTOM, RIGHT_TOP, ACROSS_TOP, ACROSS_BOTTOM = PIECES = (
    (0, 0), (3, 0), (1, 1), (3, 1), (1, 0), (2, 0), (2, 1)
)


def write(outs, mine, theirs):
    places = [*mine, *theirs]

    def body(*refs):
        pieces, (text, image, sems) = refs[len(outs) : len(outs) + len(places)], refs[-3:]
        core, place, other_place = core_place()

        def copies(first, other):
            moves = []
            for k, (piece, (turn, part)) in enumerate(zip(pieces, places)):
                own = k < len(mine)
                slab = piece.shape[0] * (1 if (turn, part) == OWN else 2)
                start = lax.rem((place if own else other_place) + turn, 4) * slab + part * slab // 2
                at = pl.ds(pl.multiple_of(start, 16), piece.shape[0])
                moves.append(
                    pltpu.make_async_copy(piece, (first if own else other).at[at, :], sems.at[k])
                )
            for move in moves:
                move.start()
            for move in moves:
                move.wait()

        @pl.when(core == TEXT)
        def _():
            copies(text, image)

        @pl.when(core != TEXT)
        def _():
            copies(image, text)

    def run(*arrays, shape):
        return call(
            body,
            [shape, shape],
            [pltpu.SemaphoreType.DMA((len(places),))],
            result=pltpu.HBM,
            aliases=[(k, k) for k in range(len(outs))],
        )((), outs, *arrays)

    return run


def on_device(text_x, image_x, text_w, image_w, position, log_scale, shift):
    rows, width = text_x.shape
    depth = text_w.shape[0]
    slab = depth // 4
    half = slab // 2
    scalars = (log_scale, shift)
    pair, pair_f32 = ((2 * rows, width), bf16), ((2 * rows, width), f32)
    total = ((depth, width), f32)
    matrix = ((depth, width), bf16)
    piece, half_piece = ((slab, width), bf16), ((half, width), bf16)
    with jax.named_scope("band_exchange"):
        text_other = send(text_x, SWAP)
        tail = jnp.pad(position.astype(bf16)[None], ((0, TAIL - 1), (0, width - rows)))
        image_own = jnp.concatenate([image_x, tail])
        image_other = send(image_own, SWAP)
        below = send(text_x, shifted(2))
        above = send(text_x, shifted(-2))
        far = send(text_x, FAR)
    with jax.named_scope("near"):
        image_near, weight, image_emb, image_projected, image_inverse, grad, head = call(
            near_kernel,
            [pair, matrix, pair, pair_f32, ((2 * rows, 1), f32), pair_f32, total],
            [
                pltpu.VMEM(*pair),
                pltpu.VMEM(*matrix),
                pltpu.VMEM(*pair),
                pltpu.SemaphoreType.DMA((3,)),
            ],
            flops=4 * 10**9,
        )(
            scalars, (text_x, text_w, image_w), text_other, image_own, image_other
        )
    with jax.named_scope("swap_neighbours"):
        below, above = after(image_inverse, below, above)
        below_other = send(below, SWAP)
        above_other = send(above, SWAP)
    visits = call(
        pair_kernel, [pair_f32, total], [pltpu.VMEM(*pair), pltpu.VMEM(*pair)], flops=4 * 10**9
    )
    with jax.named_scope("received"):
        grad, head = visits(scalars, (), below, above, weight, image_emb, grad, head)
        [far] = after(grad, far)
        far_other = send(far, SWAP)
    with jax.named_scope("partners"):
        grad, head = visits(scalars, (), below_other, above_other, weight, image_emb, grad, head)
    with jax.named_scope("far"):
        own, right_top, right_bottom, left_top, left_bottom, far_right, far_left = call(
            far_kernel,
            [piece] + [half_piece] * 6,
            [pltpu.VMEM(*pair_f32), pltpu.VMEM(*total), pltpu.VMEM(*pair), pltpu.VMEM(*pair)],
            flops=4 * 10**9,
        )(
            scalars, (), far, far_other, weight, image_emb, grad, head, image_near,
            image_projected, image_inverse,
        )
    with jax.named_scope("sum_first"):
        from_left = send(far_right, RIGHT)
        from_right = send(far_left, LEFT)
        a_bottom = send(right_bottom, RIGHT)
        b_top = send(left_top, LEFT)
        right_top, left_bottom = call(add_kernel, [half_piece] * 2)(
            (), (), right_top, from_left, left_bottom, from_right
        )
        a_top = send(right_top, RIGHT)
        b_bottom = send(left_bottom, LEFT)
        [part] = call(join_kernel, [piece])((), (), own, a_top, a_bottom, b_top, b_bottom)
    with jax.named_scope("sum_second"):
        part = exchange(part.reshape(4, slab // 4, width), SECOND)
        part = jnp.sum(part.astype(f32), axis=0).astype(bf16)
    with jax.named_scope("sum_lines"):
        tiles = (
            part.reshape(slab // 32, 8, width // 128, 128).transpose(0, 2, 1, 3).reshape(-1, 8, 128)
        )
        count = tiles.shape[0]
        each = -(-count // NZ)
        tiles = jnp.concatenate([tiles, jnp.zeros((each * NZ - count, 8, 128), bf16)])
        tiles = exchange(tiles, LINES).reshape(NZ, each, 8, 128)
        tiles = jnp.sum(tiles.astype(f32), axis=0).astype(bf16)
    with jax.named_scope("share_lines"):
        tiles = exchange(jnp.tile(tiles, (NZ, 1, 1)), LINES)[:count]
        part = (
            tiles.reshape(slab // 32, width // 128, 8, 128).transpose(0, 2, 1, 3).reshape(-1, width)
        )
    with jax.named_scope("share_second"):
        own = exchange(jnp.tile(part[None], (4, 1, 1)), SECOND).reshape(slab, width)
    with jax.named_scope("share_first"):
        top, bottom = own[:half], own[half:]
        left_top = send(top, RIGHT)
        right_top = send(top, LEFT)
        left_bottom = send(bottom, RIGHT)
        right_bottom = send(bottom, LEFT)
        own_other = send(own, SWAP)
        across_top = send(left_top, RIGHT)
        across_bottom = send(right_bottom, LEFT)
        others = [send(piece, SWAP) for piece in (left_top, right_bottom, left_bottom, right_top)]
    with jax.named_scope("write"):
        outs = write((), [OWN, LEFT_TOP, RIGHT_BOTTOM, LEFT_BOTTOM, RIGHT_TOP], [OWN])(
            own, left_top, right_bottom, left_bottom, right_top, own_other, shape=matrix
        )
        across_top, across_bottom = after(outs[0], across_top, across_bottom, in_hbm=True)
        across_others = [send(across_top, SWAP), send(across_bottom, SWAP)]
        outs = write(
            tuple(outs),
            [ACROSS_TOP, ACROSS_BOTTOM],
            [LEFT_TOP, RIGHT_BOTTOM, LEFT_BOTTOM, RIGHT_TOP],
        )(across_top, across_bottom, *others, shape=matrix)
        return write(tuple(outs), [], [ACROSS_TOP, ACROSS_BOTTOM])(*across_others, shape=matrix)


def solution(mesh):
    return jax.shard_map(
        on_device,
        mesh=mesh,
        in_specs=(P("dp", None), P("dp", None), P(), P(), P("dp"), P(), P()),
        out_specs=(P(), P()),
        check_vma=False,
    )
```

```python
import jax
import jax.numpy as jnp
from jax import lax
from jax.experimental import pallas as pl
from jax.experimental.pallas import tpu as pltpu
from jax.sharding import PartitionSpec as P

NY, NX, NZ, CORES = 4, 4, 8, 2
N = NY * NX * NZ * CORES
epsilon = 1e-06
bf16, f32 = jnp.bfloat16, jnp.float32
MIB = 1 << 20


def index(y, x, z, c):
    return ((y % NY * NX + x % NX) * NZ + z % NZ) * CORES + c


PLACES = [
    (y, x, z, c) for y in range(NY) for x in range(NX) for z in range(NZ) for c in range(CORES)
]


def route(move):
    return [(index(*place), index(*move(*place))) for place in PLACES]


def groups(key):
    found = {}
    for place in PLACES:
        found.setdefault(key(*place), []).append(index(*place))
    return list(found.values())


def along_first(step):
    return route(lambda y, x, z, c: (y, x + step, z, c) if c == 0 else (y + step, x, z, c))


SWAP = route(lambda y, x, z, c: (y, x, z, 1 - c))
RIGHT, LEFT = along_first(1), along_first(-1)
SECOND = groups(lambda y, x, z, c: (c, z, x if c == 0 else y))
LINES = groups(lambda y, x, z, c: (c, x, y))
FAR = [(i, (i + 3) % N if i % 2 else (i - 3) % N) for i in range(N)]
TAIL = 16
TEXT = 1


def shifted(distance):
    return [(i, (i + distance) % N) for i in range(N)]


def send(block, pairs):
    return lax.ppermute(block, "dp", pairs)


def exchange(parts, members):
    return lax.all_to_all(parts, "dp", 0, 0, axis_index_groups=members, tiled=True)


def call(body, outs, scratch=(), flops=0, result=pltpu.VMEM, aliases=()):
    def run(smem, outside, *arrays):
        specs = (
            [pl.BlockSpec(memory_space=pltpu.SMEM)] * len(smem)
            + [pl.BlockSpec(memory_space=pltpu.HBM)] * len(outside)
            + [pl.BlockSpec(memory_space=pltpu.VMEM)] * len(arrays)
        )
        held = [pltpu.with_memory_space_constraint(a, pltpu.VMEM) for a in arrays]
        outside = [pltpu.with_memory_space_constraint(a, pltpu.HBM) for a in outside]
        return pl.pallas_call(
            body,
            out_shape=[jax.ShapeDtypeStruct(s, d) for s, d in outs],
            in_specs=specs,
            out_specs=[pl.BlockSpec(memory_space=result)] * len(outs),
            scratch_shapes=list(scratch),
            input_output_aliases=dict(aliases),
            cost_estimate=pl.CostEstimate(flops=flops, bytes_accessed=0, transcendentals=0),
            compiler_params=pltpu.CompilerParams(vmem_limit_bytes=32 * MIB),
        )(*smem, *outside, *held)

    return run


def contract(a, b, da, db):
    return lax.dot_general(a, b, (((da,), (db,)), ((), ())), preferred_element_type=f32)


def core_place():
    me = lax.axis_index("dp")
    core = lax.rem(me, CORES)
    x = lax.rem(me // (NZ * CORES), NX)
    y = me // (NX * NZ * CORES)
    return core, jnp.where(core == 0, x, y), jnp.where(core == 0, y, x)


def on_text():
    return core_place()[0] == TEXT


def factor(log_scale):
    return jnp.exp(jnp.full((1, 1), log_scale[0], f32))


def embed(features, weight):
    projected = jnp.dot(features, weight, preferred_element_type=f32)
    square = jnp.sum(projected * projected, axis=-1, keepdims=True)
    inverse = 1.0 / jnp.sqrt(square + epsilon)
    return projected, inverse


def make_head(head, pairs):
    step = 128
    for k in range(head.shape[0] // step):
        at = pl.ds(k * step, step)
        head[at, :] = sum(contract(x[:, at], back[...], 0, 0) for x, back in pairs)


def join_positions(image_hbm, position_hbm, out, position, sems):
    rows = position.shape[0]
    moves = [
        pltpu.make_async_copy(position_hbm, position, sems.at[0]),
        pltpu.make_async_copy(image_hbm, out.at[pl.ds(0, rows), :], sems.at[1]),
    ]
    for move in moves:
        move.start()
    tail = pl.ds(rows, TAIL)
    out[tail, :] = jnp.zeros((TAIL, out.shape[1]), bf16)
    moves[0].wait()
    row = position[...].reshape(1, rows).astype(f32)
    out[tail, pl.ds(0, rows)] = jnp.broadcast_to(row, (TAIL, rows)).astype(bf16)
    moves[1].wait()


def visit(log_scale, shift, x, text_w, image_emb, finish, back, grad, grad_before):
    scale = factor(log_scale)
    projected, inverse = embed(x[...], text_w[...])
    emb = (projected * inverse).astype(bf16)
    similarity = contract(emb, image_emb[...], 1, 1)
    coefficient = finish(jax.nn.sigmoid(scale * similarity + shift[0])).astype(bf16)

    @pl.when(on_text())
    def _():
        radial = jnp.sum(coefficient.astype(f32) * similarity, axis=-1, keepdims=True)
        gradient = jnp.dot(coefficient, image_emb[...], preferred_element_type=f32)
        outer = scale * inverse
        back[...] = (gradient * outer - projected * (outer * inverse * radial)).astype(bf16)

    @pl.when(jnp.logical_not(on_text()))
    def _():
        share = contract(coefficient, emb, 0, 0)
        grad[...] = share if grad_before is None else grad_before[...] + share


def near_kernel(
    log_scale, shift, text_hbm, text_w_hbm, image_w_hbm, text_other, image_own, image_other,
    image_near, text_w, image_emb, image_projected, image_inverse, grad, text_near, back,
    image_w, sems,
):
    rows = text_other.shape[0]
    first, second = pl.ds(0, rows), pl.ds(rows, rows)
    moves = [
        pltpu.make_async_copy(image_w_hbm, image_w, sems.at[0]),
        pltpu.make_async_copy(text_hbm, text_near.at[first, :], sems.at[1]),
        pltpu.make_async_copy(text_w_hbm, text_w, sems.at[2]),
    ]
    for move in moves:
        move.start()
    image_near[first, :] = image_own[first, :]
    image_near[second, :] = image_other[first, :]
    text_near[second, :] = text_other[...]
    moves[0].wait()
    projected, inverse = embed(image_near[...], image_w[...])
    image_emb[...] = (projected * inverse).astype(bf16)
    image_projected[...] = projected
    image_inverse[...] = inverse
    moves[1].wait()
    moves[2].wait()

    def with_labels(sigmoid):
        column = lax.broadcasted_iota(jnp.int32, (2 * rows, rows), 0)

        def positions(block):
            tail = block[pl.ds(rows, TAIL), pl.ds(0, rows)]
            return tail.astype(f32)[:1].astype(jnp.int32)

        own = (column == positions(image_own)).astype(f32)
        other = (column == positions(image_other) + rows).astype(f32)
        return sigmoid - jnp.concatenate([own, other], axis=1).T

    visit(log_scale, shift, text_near, text_w, image_emb, with_labels, back, grad, None)


def gate_kernel(*refs):
    pass


def after(token, *arrays, in_hbm=False):
    outs = [(a.shape, a.dtype) for a in arrays]
    first = 1 if in_hbm else 0
    gate = call(gate_kernel, outs, aliases=[(first + k, k) for k in range(len(arrays))])
    return gate((), (token,), *arrays) if in_hbm else gate((), (), *arrays, token)


def pair_kernel(log_scale, shift, below, above, text_w, image_emb, grad_before, grad, x, back):
    rows = below.shape[0]
    x[pl.ds(0, rows), :] = below[...]
    x[pl.ds(rows, rows), :] = above[...]
    visit(log_scale, shift, x, text_w, image_emb, lambda c: c, back, grad, grad_before)


def far_kernel(
    log_scale, shift, far, far_other, text_w, image_emb, grad_before,
    image_near, image_projected, image_inverse, x_1, back_1, x_2, back_2, x_3, back_3,
    own, right_top, right_bottom, left_top, left_bottom, far_right, far_left,
    grad, head, x, back,
):
    rows = far.shape[0]
    x[pl.ds(0, rows), :] = far[...]
    x[pl.ds(rows, rows), :] = far_other[...]

    def inside(sigmoid):
        row = lax.broadcasted_iota(jnp.int32, sigmoid.shape, 0) < rows
        column = lax.broadcasted_iota(jnp.int32, sigmoid.shape, 1) < rows
        return jnp.where(row == column, sigmoid, 0.0)

    visit(log_scale, shift, x, text_w, image_emb, inside, back, grad, grad_before)

    @pl.when(on_text())
    def _():
        make_head(head, [(x_1, back_1), (x_2, back_2), (x_3, back_3), (x, back)])

    @pl.when(jnp.logical_not(on_text()))
    def _():
        gradient = factor(log_scale) * grad[...]
        inverse = image_inverse[...]
        unit = image_projected[...] * inverse
        radial = jnp.sum(gradient * unit, axis=-1, keepdims=True)
        back[...] = ((gradient - unit * radial) * inverse).astype(bf16)
        make_head(head, [(image_near, back)])

    slab = head.shape[0] // 4
    half = slab // 2
    place = core_place()[1]

    def part(turn, upper, size):
        start = lax.rem(place + turn, 4) * slab + upper
        return head[pl.ds(pl.multiple_of(start, 16), size), :].astype(bf16)

    far_right[...] = part(2, 0, half)
    far_left[...] = part(2, half, half)
    right_top[...] = part(1, 0, half)
    right_bottom[...] = part(1, half, half)
    left_top[...] = part(3, 0, half)
    left_bottom[...] = part(3, half, half)
    own[...] = part(0, 0, slab)


def add_kernel(a, b, c, d, ab, cd):
    ab[...] = (a[...].astype(f32) + b[...].astype(f32)).astype(bf16)
    cd[...] = (c[...].astype(f32) + d[...].astype(f32)).astype(bf16)


def join_kernel(own, a_top, a_bottom, b_top, b_bottom, out):
    half = a_top.shape[0]
    upper, lower = pl.ds(0, half), pl.ds(half, half)
    out[upper, :] = (
        own[upper, :].astype(f32) + a_top[...].astype(f32) + b_top[...].astype(f32)
    ).astype(bf16)
    out[lower, :] = (
        own[lower, :].astype(f32) + a_bottom[...].astype(f32) + b_bottom[...].astype(f32)
    ).astype(bf16)


OWN, LEFT_TOP, RIGHT_BOTTOM, LEFT_BOTTOM, RIGHT_TOP, ACROSS_TOP, ACROSS_BOTTOM = PIECES = (
    (0, 0), (3, 0), (1, 1), (3, 1), (1, 0), (2, 0), (2, 1)
)


def write(outs, mine, theirs):
    places = [*mine, *theirs]

    def body(*refs):
        pieces, (text, image, sems) = refs[len(outs) : len(outs) + len(places)], refs[-3:]
        core, place, other_place = core_place()

        def copies(first, other):
            moves = []
            for k, (piece, (turn, part)) in enumerate(zip(pieces, places)):
                own = k < len(mine)
                slab = piece.shape[0] * (1 if (turn, part) == OWN else 2)
                start = lax.rem((place if own else other_place) + turn, 4) * slab + part * slab // 2
                at = pl.ds(pl.multiple_of(start, 16), piece.shape[0])
                moves.append(
                    pltpu.make_async_copy(piece, (first if own else other).at[at, :], sems.at[k])
                )
            for move in moves:
                move.start()
            for move in moves:
                move.wait()

        @pl.when(core == TEXT)
        def _():
            copies(text, image)

        @pl.when(core != TEXT)
        def _():
            copies(image, text)

    def run(*arrays, shape):
        return call(
            body,
            [shape, shape],
            [pltpu.SemaphoreType.DMA((len(places),))],
            result=pltpu.HBM,
            aliases=[(k, k) for k in range(len(outs))],
        )((), outs, *arrays)

    return run


def on_device(text_x, image_x, text_w, image_w, position, log_scale, shift):
    rows, width = text_x.shape
    depth = text_w.shape[0]
    slab = depth // 4
    half = slab // 2
    scalars = (log_scale, shift)
    pair, pair_f32 = ((2 * rows, width), bf16), ((2 * rows, width), f32)
    total = ((depth, width), f32)
    matrix = ((depth, width), bf16)
    piece, half_piece = ((slab, width), bf16), ((half, width), bf16)
    with jax.named_scope("band_exchange"):
        text_other = send(text_x, SWAP)
        [image_own] = call(
            join_positions,
            [((rows + TAIL, width), bf16)],
            [pltpu.VMEM((rows,), jnp.int32), pltpu.SemaphoreType.DMA((2,))],
        )((), (image_x, position))
        image_other = send(image_own, SWAP)
        below = send(text_x, shifted(2))
        above = send(text_x, shifted(-2))
        far = send(text_x, FAR)
    with jax.named_scope("near"):
        image_near, weight, image_emb, image_projected, image_inverse, grad, *near = call(
            near_kernel,
            [pair, matrix, pair, pair_f32, ((2 * rows, 1), f32), pair_f32, pair, pair],
            [pltpu.VMEM(*matrix), pltpu.SemaphoreType.DMA((3,))],
            flops=4 * 10**9,
        )(
            scalars, (text_x, text_w, image_w), text_other, image_own, image_other
        )
    with jax.named_scope("swap_neighbours"):
        below, above = after(image_inverse, below, above)
        below_other = send(below, SWAP)
        above_other = send(above, SWAP)
    visits = call(pair_kernel, [pair_f32, pair, pair], flops=4 * 10**9)
    with jax.named_scope("received"):
        grad, *first = visits(scalars, (), below, above, weight, image_emb, grad)
        [far] = after(grad, far)
        far_other = send(far, SWAP)
    with jax.named_scope("partners"):
        grad, *second = visits(scalars, (), below_other, above_other, weight, image_emb, grad)
    with jax.named_scope("far"):
        own, right_top, right_bottom, left_top, left_bottom, far_right, far_left = call(
            far_kernel,
            [piece] + [half_piece] * 6,
            [pltpu.VMEM(*pair_f32), pltpu.VMEM(*total), pltpu.VMEM(*pair), pltpu.VMEM(*pair)],
            flops=4 * 10**9,
        )(
            scalars, (), far, far_other, weight, image_emb, grad, image_near, image_projected,
            image_inverse, *near, *first, *second,
        )
    with jax.named_scope("sum_first"):
        from_left = send(far_right, RIGHT)
        from_right = send(far_left, LEFT)
        a_bottom = send(right_bottom, RIGHT)
        b_top = send(left_top, LEFT)
        right_top, left_bottom = call(add_kernel, [half_piece] * 2)(
            (), (), right_top, from_left, left_bottom, from_right
        )
        a_top = send(right_top, RIGHT)
        b_bottom = send(left_bottom, LEFT)
        [part] = call(join_kernel, [piece])((), (), own, a_top, a_bottom, b_top, b_bottom)
    with jax.named_scope("sum_second"):
        part = exchange(part.reshape(4, slab // 4, width), SECOND)
        part = jnp.sum(part.astype(f32), axis=0).astype(bf16)
    with jax.named_scope("sum_lines"):
        tiles = (
            part.reshape(slab // 32, 8, width // 128, 128).transpose(0, 2, 1, 3).reshape(-1, 8, 128)
        )
        count = tiles.shape[0]
        each = -(-count // NZ)
        tiles = jnp.concatenate([tiles, jnp.zeros((each * NZ - count, 8, 128), bf16)])
        tiles = exchange(tiles, LINES).reshape(NZ, each, 8, 128)
        tiles = jnp.sum(tiles.astype(f32), axis=0).astype(bf16)
    with jax.named_scope("share_lines"):
        tiles = exchange(jnp.tile(tiles, (NZ, 1, 1)), LINES)[:count]
        part = (
            tiles.reshape(slab // 32, width // 128, 8, 128).transpose(0, 2, 1, 3).reshape(-1, width)
        )
    with jax.named_scope("share_second"):
        own = exchange(jnp.tile(part[None], (4, 1, 1)), SECOND).reshape(slab, width)
    with jax.named_scope("share_first"):
        top, bottom = own[:half], own[half:]
        left_top = send(top, RIGHT)
        right_top = send(top, LEFT)
        left_bottom = send(bottom, RIGHT)
        right_bottom = send(bottom, LEFT)
        own_other = send(own, SWAP)
        across_top = send(left_top, RIGHT)
        across_bottom = send(right_bottom, LEFT)
        others = [send(piece, SWAP) for piece in (left_top, right_bottom, left_bottom, right_top)]
    with jax.named_scope("write"):
        outs = write((), [OWN, LEFT_TOP, RIGHT_BOTTOM, LEFT_BOTTOM, RIGHT_TOP], [OWN])(
            own, left_top, right_bottom, left_bottom, right_top, own_other, shape=matrix
        )
        across_top, across_bottom = after(outs[0], across_top, across_bottom, in_hbm=True)
        across_others = [send(across_top, SWAP), send(across_bottom, SWAP)]
        outs = write(
            tuple(outs),
            [ACROSS_TOP, ACROSS_BOTTOM],
            [LEFT_TOP, RIGHT_BOTTOM, LEFT_BOTTOM, RIGHT_TOP],
        )(across_top, across_bottom, *others, shape=matrix)
        return write(tuple(outs), [], [ACROSS_TOP, ACROSS_BOTTOM])(*across_others, shape=matrix)


def solution(mesh):
    return jax.shard_map(
        on_device,
        mesh=mesh,
        in_specs=(P("dp", None), P("dp", None), P(), P(), P("dp"), P(), P()),
        out_specs=(P(), P()),
        check_vma=False,
    )
```

```python
import jax
import jax.numpy as jnp
from jax import lax
from jax.experimental import pallas as pl
from jax.experimental.pallas import tpu as pltpu
from jax.sharding import PartitionSpec as P

NY, NX, NZ, CORES = 4, 4, 8, 2
N = NY * NX * NZ * CORES
epsilon = 1e-06
bf16, f32 = jnp.bfloat16, jnp.float32
MIB = 1 << 20


def index(y, x, z, c):
    return ((y % NY * NX + x % NX) * NZ + z % NZ) * CORES + c


PLACES = [
    (y, x, z, c) for y in range(NY) for x in range(NX) for z in range(NZ) for c in range(CORES)
]


def route(move):
    return [(index(*place), index(*move(*place))) for place in PLACES]


def groups(key):
    found = {}
    for place in PLACES:
        found.setdefault(key(*place), []).append(index(*place))
    return list(found.values())


def along_first(step):
    return route(lambda y, x, z, c: (y, x + step, z, c) if c == 0 else (y + step, x, z, c))


SWAP = route(lambda y, x, z, c: (y, x, z, 1 - c))
RIGHT, LEFT = along_first(1), along_first(-1)
SECOND = groups(lambda y, x, z, c: (c, z, x if c == 0 else y))
LINES = groups(lambda y, x, z, c: (c, x, y))
FAR = [(i, (i + 3) % N if i % 2 else (i - 3) % N) for i in range(N)]
TAIL = 16
TEXT = 1


def shifted(distance):
    return [(i, (i + distance) % N) for i in range(N)]


def send(block, pairs):
    return lax.ppermute(block, "dp", pairs)


def exchange(parts, members):
    return lax.all_to_all(parts, "dp", 0, 0, axis_index_groups=members, tiled=True)


def call(body, outs, scratch=(), flops=0, result=pltpu.VMEM, aliases=()):
    def run(smem, outside, *arrays):
        specs = (
            [pl.BlockSpec(memory_space=pltpu.SMEM)] * len(smem)
            + [pl.BlockSpec(memory_space=pltpu.HBM)] * len(outside)
            + [pl.BlockSpec(memory_space=pltpu.VMEM)] * len(arrays)
        )
        held = [pltpu.with_memory_space_constraint(a, pltpu.VMEM) for a in arrays]
        outside = [pltpu.with_memory_space_constraint(a, pltpu.HBM) for a in outside]
        return pl.pallas_call(
            body,
            out_shape=[jax.ShapeDtypeStruct(s, d) for s, d in outs],
            in_specs=specs,
            out_specs=[pl.BlockSpec(memory_space=result)] * len(outs),
            scratch_shapes=list(scratch),
            input_output_aliases=dict(aliases),
            cost_estimate=pl.CostEstimate(flops=flops, bytes_accessed=0, transcendentals=0),
            compiler_params=pltpu.CompilerParams(vmem_limit_bytes=32 * MIB),
        )(*smem, *outside, *held)

    return run


def contract(a, b, da, db):
    return lax.dot_general(a, b, (((da,), (db,)), ((), ())), preferred_element_type=f32)


def core_place():
    me = lax.axis_index("dp")
    core = lax.rem(me, CORES)
    x = lax.rem(me // (NZ * CORES), NX)
    y = me // (NX * NZ * CORES)
    return core, jnp.where(core == 0, x, y), jnp.where(core == 0, y, x)


def on_text():
    return core_place()[0] == TEXT


def factor(log_scale):
    return jnp.exp(jnp.full((1, 1), log_scale[0], f32))


def embed(features, weight):
    projected = jnp.dot(features, weight, preferred_element_type=f32)
    square = jnp.sum(projected * projected, axis=-1, keepdims=True)
    inverse = 1.0 / jnp.sqrt(square + epsilon)
    return projected, inverse


def make_head(head, pairs):
    step = 128
    for k in range(head.shape[0] // step):
        at = pl.ds(k * step, step)
        head[at, :] = sum(contract(x[:, at], back[...], 0, 0) for x, back in pairs)


def join_positions(image_hbm, position_hbm, out, position, sems):
    rows = position.shape[0]
    moves = [
        pltpu.make_async_copy(position_hbm, position, sems.at[0]),
        pltpu.make_async_copy(image_hbm, out.at[pl.ds(0, rows), :], sems.at[1]),
    ]
    for move in moves:
        move.start()
    tail = pl.ds(rows, TAIL)
    out[tail, :] = jnp.zeros((TAIL, out.shape[1]), bf16)
    moves[0].wait()
    row = position[...].reshape(1, rows).astype(f32)
    out[tail, pl.ds(0, rows)] = jnp.broadcast_to(row, (TAIL, rows)).astype(bf16)
    moves[1].wait()


def visit(log_scale, shift, x, text_w, image_emb, finish, back, grad, grad_before):
    scale = factor(log_scale)
    projected, inverse = embed(x[...], text_w[...])
    emb = (projected * inverse).astype(bf16)
    similarity = contract(emb, image_emb[...], 1, 1)
    coefficient = finish(jax.nn.sigmoid(scale * similarity + shift[0])).astype(bf16)

    @pl.when(on_text())
    def _():
        radial = jnp.sum(coefficient.astype(f32) * similarity, axis=-1, keepdims=True)
        gradient = jnp.dot(coefficient, image_emb[...], preferred_element_type=f32)
        outer = scale * inverse
        back[...] = (gradient * outer - projected * (outer * inverse * radial)).astype(bf16)

    @pl.when(jnp.logical_not(on_text()))
    def _():
        share = contract(coefficient, emb, 0, 0)
        grad[...] = share if grad_before is None else grad_before[...] + share


def near_kernel(
    log_scale, shift, text_hbm, text_w_hbm, image_w_hbm, text_other, image_own, image_other,
    image_near, text_w, image_emb, image_projected, image_inverse, grad, text_near, back,
    image_w, sems,
):
    rows = text_other.shape[0]
    first, second = pl.ds(0, rows), pl.ds(rows, rows)
    moves = [
        pltpu.make_async_copy(image_w_hbm, image_w, sems.at[0]),
        pltpu.make_async_copy(text_hbm, text_near.at[first, :], sems.at[1]),
        pltpu.make_async_copy(text_w_hbm, text_w, sems.at[2]),
    ]
    for move in moves:
        move.start()
    image_near[first, :] = image_own[first, :]
    image_near[second, :] = image_other[first, :]
    text_near[second, :] = text_other[...]
    moves[0].wait()
    projected, inverse = embed(image_near[...], image_w[...])
    image_emb[...] = (projected * inverse).astype(bf16)
    image_projected[...] = projected
    image_inverse[...] = inverse
    moves[1].wait()
    moves[2].wait()

    def with_labels(sigmoid):
        column = lax.broadcasted_iota(jnp.int32, (2 * rows, rows), 0)

        def positions(block):
            tail = block[pl.ds(rows, TAIL), pl.ds(0, rows)]
            return tail.astype(f32)[:1].astype(jnp.int32)

        own = (column == positions(image_own)).astype(f32)
        other = (column == positions(image_other) + rows).astype(f32)
        return sigmoid - jnp.concatenate([own, other], axis=1).T

    visit(log_scale, shift, text_near, text_w, image_emb, with_labels, back, grad, None)


def gate_kernel(*refs):
    pass


def after(token, *arrays, in_hbm=False):
    outs = [(a.shape, a.dtype) for a in arrays]
    first = 1 if in_hbm else 0
    gate = call(gate_kernel, outs, aliases=[(first + k, k) for k in range(len(arrays))])
    return gate((), (token,), *arrays) if in_hbm else gate((), (), *arrays, token)


def pair_kernel(log_scale, shift, below, above, text_w, image_emb, grad_before, grad, x, back):
    rows = below.shape[0]
    x[pl.ds(0, rows), :] = below[...]
    x[pl.ds(rows, rows), :] = above[...]
    visit(log_scale, shift, x, text_w, image_emb, lambda c: c, back, grad, grad_before)


def far_kernel(
    log_scale, shift, far, far_other, text_w, image_emb, grad_before,
    image_near, image_projected, image_inverse, x_1, back_1, x_2, back_2, x_3, back_3,
    own, right_top, right_bottom, left_top, left_bottom, far_right, far_left,
    grad, head, x, back,
):
    rows = far.shape[0]
    x[pl.ds(0, rows), :] = far[...]
    x[pl.ds(rows, rows), :] = far_other[...]

    def inside(sigmoid):
        row = lax.broadcasted_iota(jnp.int32, sigmoid.shape, 0) < rows
        column = lax.broadcasted_iota(jnp.int32, sigmoid.shape, 1) < rows
        return jnp.where(row == column, sigmoid, 0.0)

    visit(log_scale, shift, x, text_w, image_emb, inside, back, grad, grad_before)

    @pl.when(on_text())
    def _():
        make_head(head, [(x_1, back_1), (x_2, back_2), (x_3, back_3), (x, back)])

    @pl.when(jnp.logical_not(on_text()))
    def _():
        gradient = factor(log_scale) * grad[...]
        inverse = image_inverse[...]
        unit = image_projected[...] * inverse
        radial = jnp.sum(gradient * unit, axis=-1, keepdims=True)
        back[...] = ((gradient - unit * radial) * inverse).astype(bf16)
        make_head(head, [(image_near, back)])

    slab = head.shape[0] // 4
    half = slab // 2
    place = core_place()[1]

    def part(turn, upper, size):
        start = lax.rem(place + turn, 4) * slab + upper
        return head[pl.ds(pl.multiple_of(start, 16), size), :].astype(bf16)

    far_right[...] = part(2, 0, half)
    far_left[...] = part(2, half, half)
    right_top[...] = part(1, 0, half)
    right_bottom[...] = part(1, half, half)
    left_top[...] = part(3, 0, half)
    left_bottom[...] = part(3, half, half)
    own[...] = part(0, 0, slab)


def add_kernel(a, b, c, d, ab, cd):
    ab[...] = (a[...].astype(f32) + b[...].astype(f32)).astype(bf16)
    cd[...] = (c[...].astype(f32) + d[...].astype(f32)).astype(bf16)


def join_kernel(own, a_top, a_bottom, b_top, b_bottom, out):
    half = a_top.shape[0]
    upper, lower = pl.ds(0, half), pl.ds(half, half)
    out[upper, :] = (
        own[upper, :].astype(f32) + a_top[...].astype(f32) + b_top[...].astype(f32)
    ).astype(bf16)
    out[lower, :] = (
        own[lower, :].astype(f32) + a_bottom[...].astype(f32) + b_bottom[...].astype(f32)
    ).astype(bf16)


OWN, LEFT_TOP, RIGHT_BOTTOM, LEFT_BOTTOM, RIGHT_TOP, ACROSS_TOP, ACROSS_BOTTOM = PIECES = (
    (0, 0), (3, 0), (1, 1), (3, 1), (1, 0), (2, 0), (2, 1)
)


def write(outs, mine, theirs):
    places = [*mine, *theirs]

    def body(*refs):
        pieces, (text, image, sems) = refs[len(outs) : len(outs) + len(places)], refs[-3:]
        core, place, other_place = core_place()

        def copies(first, other):
            moves = []
            for k, (piece, (turn, part)) in enumerate(zip(pieces, places)):
                own = k < len(mine)
                slab = piece.shape[0] * (1 if (turn, part) == OWN else 2)
                start = lax.rem((place if own else other_place) + turn, 4) * slab + part * slab // 2
                at = pl.ds(pl.multiple_of(start, 16), piece.shape[0])
                moves.append(
                    pltpu.make_async_copy(piece, (first if own else other).at[at, :], sems.at[k])
                )
            for move in moves:
                move.start()
            for move in moves:
                move.wait()

        @pl.when(core == TEXT)
        def _():
            copies(text, image)

        @pl.when(core != TEXT)
        def _():
            copies(image, text)

    def run(*arrays, shape):
        return call(
            body,
            [shape, shape],
            [pltpu.SemaphoreType.DMA((len(places),))],
            result=pltpu.HBM,
            aliases=[(k, k) for k in range(len(outs))],
        )((), outs, *arrays)

    return run


def on_device(text_x, image_x, text_w, image_w, position, log_scale, shift):
    rows, width = text_x.shape
    depth = text_w.shape[0]
    slab = depth // 4
    half = slab // 2
    scalars = (log_scale, shift)
    pair, pair_f32 = ((2 * rows, width), bf16), ((2 * rows, width), f32)
    total = ((depth, width), f32)
    matrix = ((depth, width), bf16)
    piece, half_piece = ((slab, width), bf16), ((half, width), bf16)
    with jax.named_scope("band_exchange"):
        text_other = send(text_x, SWAP)
        [image_own] = call(
            join_positions,
            [((rows + TAIL, width), bf16)],
            [pltpu.VMEM((rows,), jnp.int32), pltpu.SemaphoreType.DMA((2,))],
        )((), (image_x, position))
        image_other = send(image_own, SWAP)
        below = send(text_x, shifted(2))
        above = send(text_x, shifted(-2))
        far = send(text_x, FAR)
    with jax.named_scope("near"):
        image_near, weight, image_emb, image_projected, image_inverse, grad, *near = call(
            near_kernel,
            [pair, matrix, pair, pair_f32, ((2 * rows, 1), f32), pair_f32, pair, pair],
            [pltpu.VMEM(*matrix), pltpu.SemaphoreType.DMA((3,))],
            flops=4 * 10**9,
        )(
            scalars, (text_x, text_w, image_w), text_other, image_own, image_other
        )
    with jax.named_scope("swap_neighbours"):
        above, below = after(image_inverse, above, below)
        below_other = send(below, SWAP)
        above_other = send(above, SWAP)
    visits = call(pair_kernel, [pair_f32, pair, pair], flops=4 * 10**9)
    with jax.named_scope("received"):
        grad, *first = visits(scalars, (), below, above, weight, image_emb, grad)
        [far] = after(grad, far)
        far_other = send(far, SWAP)
    with jax.named_scope("partners"):
        grad, *second = visits(scalars, (), below_other, above_other, weight, image_emb, grad)
    with jax.named_scope("far"):
        own, right_top, right_bottom, left_top, left_bottom, far_right, far_left = call(
            far_kernel,
            [piece] + [half_piece] * 6,
            [pltpu.VMEM(*pair_f32), pltpu.VMEM(*total), pltpu.VMEM(*pair), pltpu.VMEM(*pair)],
            flops=4 * 10**9,
        )(
            scalars, (), far, far_other, weight, image_emb, grad, image_near, image_projected,
            image_inverse, *near, *first, *second,
        )
    with jax.named_scope("sum_first"):
        from_left = send(far_right, RIGHT)
        from_right = send(far_left, LEFT)
        a_bottom = send(right_bottom, RIGHT)
        b_top = send(left_top, LEFT)
        right_top, left_bottom = call(add_kernel, [half_piece] * 2)(
            (), (), right_top, from_left, left_bottom, from_right
        )
        a_top = send(right_top, RIGHT)
        b_bottom = send(left_bottom, LEFT)
        [part] = call(join_kernel, [piece])((), (), own, a_top, a_bottom, b_top, b_bottom)
    with jax.named_scope("sum_second"):
        part = exchange(part.reshape(4, slab // 4, width), SECOND)
        part = jnp.sum(part.astype(f32), axis=0).astype(bf16)
    with jax.named_scope("sum_lines"):
        tiles = (
            part.reshape(slab // 32, 8, width // 128, 128).transpose(0, 2, 1, 3).reshape(-1, 8, 128)
        )
        count = tiles.shape[0]
        each = -(-count // NZ)
        tiles = jnp.concatenate([tiles, jnp.zeros((each * NZ - count, 8, 128), bf16)])
        tiles = exchange(tiles, LINES).reshape(NZ, each, 8, 128)
        tiles = jnp.sum(tiles.astype(f32), axis=0).astype(bf16)
    with jax.named_scope("share_lines"):
        tiles = exchange(jnp.tile(tiles, (NZ, 1, 1)), LINES)[:count]
        part = (
            tiles.reshape(slab // 32, width // 128, 8, 128).transpose(0, 2, 1, 3).reshape(-1, width)
        )
    with jax.named_scope("share_second"):
        own = exchange(jnp.tile(part[None], (4, 1, 1)), SECOND).reshape(slab, width)
    with jax.named_scope("share_first"):
        top, bottom = own[:half], own[half:]
        left_top = send(top, RIGHT)
        right_top = send(top, LEFT)
        left_bottom = send(bottom, RIGHT)
        right_bottom = send(bottom, LEFT)
        own_other = send(own, SWAP)
        across_top = send(left_top, RIGHT)
        across_bottom = send(right_bottom, LEFT)
        others = [send(piece, SWAP) for piece in (left_top, right_bottom, left_bottom, right_top)]
    with jax.named_scope("write"):
        outs = write((), [OWN, LEFT_TOP, RIGHT_BOTTOM, LEFT_BOTTOM, RIGHT_TOP], [OWN])(
            own, left_top, right_bottom, left_bottom, right_top, own_other, shape=matrix
        )
        across_top, across_bottom = after(outs[0], across_top, across_bottom, in_hbm=True)
        across_others = [send(across_top, SWAP), send(across_bottom, SWAP)]
        outs = write(
            tuple(outs),
            [ACROSS_TOP, ACROSS_BOTTOM],
            [LEFT_TOP, RIGHT_BOTTOM, LEFT_BOTTOM, RIGHT_TOP],
        )(across_top, across_bottom, *others, shape=matrix)
        return write(tuple(outs), [], [ACROSS_TOP, ACROSS_BOTTOM])(*across_others, shape=matrix)


def solution(mesh):
    return jax.shard_map(
        on_device,
        mesh=mesh,
        in_specs=(P("dp", None), P("dp", None), P(), P(), P("dp"), P(), P()),
        out_specs=(P(), P()),
        check_vma=False,
    )
```

```python
import jax
import jax.numpy as jnp
from jax import lax
from jax.experimental import pallas as pl
from jax.experimental.pallas import tpu as pltpu
from jax.sharding import PartitionSpec as P

NY, NX, NZ, CORES = 4, 4, 8, 2
N = NY * NX * NZ * CORES
epsilon = 1e-06
bf16, f32 = jnp.bfloat16, jnp.float32
MIB = 1 << 20


def index(y, x, z, c):
    return ((y % NY * NX + x % NX) * NZ + z % NZ) * CORES + c


PLACES = [
    (y, x, z, c) for y in range(NY) for x in range(NX) for z in range(NZ) for c in range(CORES)
]


def route(move):
    return [(index(*place), index(*move(*place))) for place in PLACES]


def groups(key):
    found = {}
    for place in PLACES:
        found.setdefault(key(*place), []).append(index(*place))
    return list(found.values())


def along_first(step):
    return route(lambda y, x, z, c: (y, x + step, z, c) if c == 0 else (y + step, x, z, c))


SWAP = route(lambda y, x, z, c: (y, x, z, 1 - c))
RIGHT, LEFT = along_first(1), along_first(-1)
SECOND = groups(lambda y, x, z, c: (c, z, x if c == 0 else y))
LINES = groups(lambda y, x, z, c: (c, x, y))
FAR = [(i, (i + 3) % N if i % 2 else (i - 3) % N) for i in range(N)]
TAIL = 16
TEXT = 1


def shifted(distance):
    return [(i, (i + distance) % N) for i in range(N)]


def send(block, pairs):
    return lax.ppermute(block, "dp", pairs)


def exchange(parts, members):
    return lax.all_to_all(parts, "dp", 0, 0, axis_index_groups=members, tiled=True)


def call(body, outs, scratch=(), flops=0, result=pltpu.VMEM, aliases=()):
    def run(smem, outside, *arrays):
        specs = (
            [pl.BlockSpec(memory_space=pltpu.SMEM)] * len(smem)
            + [pl.BlockSpec(memory_space=pltpu.HBM)] * len(outside)
            + [pl.BlockSpec(memory_space=pltpu.VMEM)] * len(arrays)
        )
        held = [pltpu.with_memory_space_constraint(a, pltpu.VMEM) for a in arrays]
        outside = [pltpu.with_memory_space_constraint(a, pltpu.HBM) for a in outside]
        return pl.pallas_call(
            body,
            out_shape=[jax.ShapeDtypeStruct(s, d) for s, d in outs],
            in_specs=specs,
            out_specs=[pl.BlockSpec(memory_space=result)] * len(outs),
            scratch_shapes=list(scratch),
            input_output_aliases=dict(aliases),
            cost_estimate=pl.CostEstimate(flops=flops, bytes_accessed=0, transcendentals=0),
            compiler_params=pltpu.CompilerParams(vmem_limit_bytes=32 * MIB),
        )(*smem, *outside, *held)

    return run


def contract(a, b, da, db):
    return lax.dot_general(a, b, (((da,), (db,)), ((), ())), preferred_element_type=f32)


def core_place():
    me = lax.axis_index("dp")
    core = lax.rem(me, CORES)
    x = lax.rem(me // (NZ * CORES), NX)
    y = me // (NX * NZ * CORES)
    return core, jnp.where(core == 0, x, y), jnp.where(core == 0, y, x)


def on_text():
    return core_place()[0] == TEXT


def factor(log_scale):
    return jnp.exp(jnp.full((1, 1), log_scale[0], f32))


def embed(features, weight):
    projected = jnp.dot(features, weight, preferred_element_type=f32)
    square = jnp.sum(projected * projected, axis=-1, keepdims=True)
    inverse = 1.0 / jnp.sqrt(square + epsilon)
    return projected, inverse


def make_head(head, pairs, before=None):
    step = 128
    for k in range(head.shape[0] // step):
        at = pl.ds(k * step, step)
        new = sum(contract(x[:, at], back[...], 0, 0) for x, back in pairs)
        head[at, :] = new if before is None else before[at, :] + new


def join_positions(image_hbm, position_hbm, out, position, sems):
    rows = position.shape[0]
    moves = [
        pltpu.make_async_copy(position_hbm, position, sems.at[0]),
        pltpu.make_async_copy(image_hbm, out.at[pl.ds(0, rows), :], sems.at[1]),
    ]
    for move in moves:
        move.start()
    tail = pl.ds(rows, TAIL)
    out[tail, :] = jnp.zeros((TAIL, out.shape[1]), bf16)
    moves[0].wait()
    row = position[...].reshape(1, rows).astype(f32)
    out[tail, pl.ds(0, rows)] = jnp.broadcast_to(row, (TAIL, rows)).astype(bf16)
    moves[1].wait()


def visit(log_scale, shift, x, text_w, image_emb, finish, back, grad, grad_before):
    scale = factor(log_scale)
    projected, inverse = embed(x[...], text_w[...])
    emb = (projected * inverse).astype(bf16)
    similarity = contract(emb, image_emb[...], 1, 1)
    coefficient = finish(jax.nn.sigmoid(scale * similarity + shift[0])).astype(bf16)

    @pl.when(on_text())
    def _():
        radial = jnp.sum(coefficient.astype(f32) * similarity, axis=-1, keepdims=True)
        gradient = jnp.dot(coefficient, image_emb[...], preferred_element_type=f32)
        outer = scale * inverse
        back[...] = (gradient * outer - projected * (outer * inverse * radial)).astype(bf16)

    @pl.when(jnp.logical_not(on_text()))
    def _():
        share = contract(coefficient, emb, 0, 0)
        grad[...] = share if grad_before is None else grad_before[...] + share


def near_kernel(
    log_scale, shift, text_hbm, text_w_hbm, image_w_hbm, text_other, image_own, image_other,
    image_near, text_w, image_emb, image_projected, image_inverse, grad, text_near, back,
    image_w, sems,
):
    rows = text_other.shape[0]
    first, second = pl.ds(0, rows), pl.ds(rows, rows)
    moves = [
        pltpu.make_async_copy(image_w_hbm, image_w, sems.at[0]),
        pltpu.make_async_copy(text_hbm, text_near.at[first, :], sems.at[1]),
        pltpu.make_async_copy(text_w_hbm, text_w, sems.at[2]),
    ]
    for move in moves:
        move.start()
    image_near[first, :] = image_own[first, :]
    image_near[second, :] = image_other[first, :]
    text_near[second, :] = text_other[...]
    moves[0].wait()
    projected, inverse = embed(image_near[...], image_w[...])
    image_emb[...] = (projected * inverse).astype(bf16)
    image_projected[...] = projected
    image_inverse[...] = inverse
    moves[1].wait()
    moves[2].wait()

    def with_labels(sigmoid):
        column = lax.broadcasted_iota(jnp.int32, (2 * rows, rows), 0)

        def positions(block):
            tail = block[pl.ds(rows, TAIL), pl.ds(0, rows)]
            return tail.astype(f32)[:1].astype(jnp.int32)

        own = (column == positions(image_own)).astype(f32)
        other = (column == positions(image_other) + rows).astype(f32)
        return sigmoid - jnp.concatenate([own, other], axis=1).T

    visit(log_scale, shift, text_near, text_w, image_emb, with_labels, back, grad, None)


def gate_kernel(*refs):
    pass


def after(token, *arrays, in_hbm=False):
    outs = [(a.shape, a.dtype) for a in arrays]
    first = 1 if in_hbm else 0
    gate = call(gate_kernel, outs, aliases=[(first + k, k) for k in range(len(arrays))])
    return gate((), (token,), *arrays) if in_hbm else gate((), (), *arrays, token)


def pair_kernel(log_scale, shift, below, above, text_w, image_emb, grad_before, grad, x, back):
    rows = below.shape[0]
    x[pl.ds(0, rows), :] = below[...]
    x[pl.ds(rows, rows), :] = above[...]
    visit(log_scale, shift, x, text_w, image_emb, lambda c: c, back, grad, grad_before)


def received_kernel(
    log_scale, shift, below, above, text_w, image_emb, grad_before, x_1, back_1,
    grad, head, x, back,
):
    pair_kernel(log_scale, shift, below, above, text_w, image_emb, grad_before, grad, x, back)

    @pl.when(on_text())
    def _():
        make_head(head, [(x_1, back_1), (x, back)])


def far_kernel(
    log_scale, shift, far, far_other, text_w, image_emb, grad_before,
    image_near, image_projected, image_inverse, head_before, x_1, back_1,
    own, right_top, right_bottom, left_top, left_bottom, far_right, far_left,
    grad, head, x, back,
):
    rows = far.shape[0]
    x[pl.ds(0, rows), :] = far[...]
    x[pl.ds(rows, rows), :] = far_other[...]

    def inside(sigmoid):
        row = lax.broadcasted_iota(jnp.int32, sigmoid.shape, 0) < rows
        column = lax.broadcasted_iota(jnp.int32, sigmoid.shape, 1) < rows
        return jnp.where(row == column, sigmoid, 0.0)

    visit(log_scale, shift, x, text_w, image_emb, inside, back, grad, grad_before)

    @pl.when(on_text())
    def _():
        make_head(head, [(x_1, back_1), (x, back)], head_before)

    @pl.when(jnp.logical_not(on_text()))
    def _():
        gradient = factor(log_scale) * grad[...]
        inverse = image_inverse[...]
        unit = image_projected[...] * inverse
        radial = jnp.sum(gradient * unit, axis=-1, keepdims=True)
        back[...] = ((gradient - unit * radial) * inverse).astype(bf16)
        make_head(head, [(image_near, back)])

    slab = head.shape[0] // 4
    half = slab // 2
    place = core_place()[1]

    def part(turn, upper, size):
        start = lax.rem(place + turn, 4) * slab + upper
        return head[pl.ds(pl.multiple_of(start, 16), size), :].astype(bf16)

    far_right[...] = part(2, 0, half)
    far_left[...] = part(2, half, half)
    right_top[...] = part(1, 0, half)
    right_bottom[...] = part(1, half, half)
    left_top[...] = part(3, 0, half)
    left_bottom[...] = part(3, half, half)
    own[...] = part(0, 0, slab)


def add_kernel(a, b, c, d, ab, cd):
    ab[...] = (a[...].astype(f32) + b[...].astype(f32)).astype(bf16)
    cd[...] = (c[...].astype(f32) + d[...].astype(f32)).astype(bf16)


def join_kernel(own, a_top, a_bottom, b_top, b_bottom, out):
    half = a_top.shape[0]
    upper, lower = pl.ds(0, half), pl.ds(half, half)
    out[upper, :] = (
        own[upper, :].astype(f32) + a_top[...].astype(f32) + b_top[...].astype(f32)
    ).astype(bf16)
    out[lower, :] = (
        own[lower, :].astype(f32) + a_bottom[...].astype(f32) + b_bottom[...].astype(f32)
    ).astype(bf16)


OWN, LEFT_TOP, RIGHT_BOTTOM, LEFT_BOTTOM, RIGHT_TOP, ACROSS_TOP, ACROSS_BOTTOM = PIECES = (
    (0, 0), (3, 0), (1, 1), (3, 1), (1, 0), (2, 0), (2, 1)
)


def write(outs, mine, theirs):
    places = [*mine, *theirs]

    def body(*refs):
        pieces, (text, image, sems) = refs[len(outs) : len(outs) + len(places)], refs[-3:]
        core, place, other_place = core_place()

        def copies(first, other):
            moves = []
            for k, (piece, (turn, part)) in enumerate(zip(pieces, places)):
                own = k < len(mine)
                slab = piece.shape[0] * (1 if (turn, part) == OWN else 2)
                start = lax.rem((place if own else other_place) + turn, 4) * slab + part * slab // 2
                at = pl.ds(pl.multiple_of(start, 16), piece.shape[0])
                moves.append(
                    pltpu.make_async_copy(piece, (first if own else other).at[at, :], sems.at[k])
                )
            for move in moves:
                move.start()
            for move in moves:
                move.wait()

        @pl.when(core == TEXT)
        def _():
            copies(text, image)

        @pl.when(core != TEXT)
        def _():
            copies(image, text)

    def run(*arrays, shape):
        return call(
            body,
            [shape, shape],
            [pltpu.SemaphoreType.DMA((len(places),))],
            result=pltpu.HBM,
            aliases=[(k, k) for k in range(len(outs))],
        )((), outs, *arrays)

    return run


def on_device(text_x, image_x, text_w, image_w, position, log_scale, shift):
    rows, width = text_x.shape
    depth = text_w.shape[0]
    slab = depth // 4
    half = slab // 2
    scalars = (log_scale, shift)
    pair, pair_f32 = ((2 * rows, width), bf16), ((2 * rows, width), f32)
    total = ((depth, width), f32)
    matrix = ((depth, width), bf16)
    piece, half_piece = ((slab, width), bf16), ((half, width), bf16)
    with jax.named_scope("band_exchange"):
        text_other = send(text_x, SWAP)
        [image_own] = call(
            join_positions,
            [((rows + TAIL, width), bf16)],
            [pltpu.VMEM((rows,), jnp.int32), pltpu.SemaphoreType.DMA((2,))],
        )((), (image_x, position))
        image_other = send(image_own, SWAP)
        below = send(text_x, shifted(2))
        above = send(text_x, shifted(-2))
        far = send(text_x, FAR)
    with jax.named_scope("near"):
        image_near, weight, image_emb, image_projected, image_inverse, grad, *near = call(
            near_kernel,
            [pair, matrix, pair, pair_f32, ((2 * rows, 1), f32), pair_f32, pair, pair],
            [pltpu.VMEM(*matrix), pltpu.SemaphoreType.DMA((3,))],
            flops=4 * 10**9,
        )(
            scalars, (text_x, text_w, image_w), text_other, image_own, image_other
        )
    with jax.named_scope("swap_neighbours"):
        above, below = after(image_inverse, above, below)
        below_other = send(below, SWAP)
        above_other = send(above, SWAP)
    with jax.named_scope("received"):
        grad, head = call(
            received_kernel,
            [pair_f32, total],
            [pltpu.VMEM(*pair), pltpu.VMEM(*pair)],
            flops=4 * 10**9,
        )(scalars, (), below, above, weight, image_emb, grad, *near)
        [far] = after(grad, far)
        far_other = send(far, SWAP)
    with jax.named_scope("partners"):
        grad, *second = call(pair_kernel, [pair_f32, pair, pair], flops=4 * 10**9)(
            scalars, (), below_other, above_other, weight, image_emb, grad
        )
    with jax.named_scope("far"):
        own, right_top, right_bottom, left_top, left_bottom, far_right, far_left = call(
            far_kernel,
            [piece] + [half_piece] * 6,
            [pltpu.VMEM(*pair_f32), pltpu.VMEM(*total), pltpu.VMEM(*pair), pltpu.VMEM(*pair)],
            flops=4 * 10**9,
        )(
            scalars, (), far, far_other, weight, image_emb, grad, image_near, image_projected,
            image_inverse, head, *second,
        )
    with jax.named_scope("sum_first"):
        from_left = send(far_right, RIGHT)
        from_right = send(far_left, LEFT)
        a_bottom = send(right_bottom, RIGHT)
        b_top = send(left_top, LEFT)
        right_top, left_bottom = call(add_kernel, [half_piece] * 2)(
            (), (), right_top, from_left, left_bottom, from_right
        )
        a_top = send(right_top, RIGHT)
        b_bottom = send(left_bottom, LEFT)
        [part] = call(join_kernel, [piece])((), (), own, a_top, a_bottom, b_top, b_bottom)
    with jax.named_scope("sum_second"):
        part = exchange(part.reshape(4, slab // 4, width), SECOND)
        part = jnp.sum(part.astype(f32), axis=0).astype(bf16)
    with jax.named_scope("sum_lines"):
        tiles = (
            part.reshape(slab // 32, 8, width // 128, 128).transpose(0, 2, 1, 3).reshape(-1, 8, 128)
        )
        count = tiles.shape[0]
        each = -(-count // NZ)
        tiles = jnp.concatenate([tiles, jnp.zeros((each * NZ - count, 8, 128), bf16)])
        tiles = exchange(tiles, LINES).reshape(NZ, each, 8, 128)
        tiles = jnp.sum(tiles.astype(f32), axis=0).astype(bf16)
    with jax.named_scope("share_lines"):
        tiles = exchange(jnp.tile(tiles, (NZ, 1, 1)), LINES)[:count]
        part = (
            tiles.reshape(slab // 32, width // 128, 8, 128).transpose(0, 2, 1, 3).reshape(-1, width)
        )
    with jax.named_scope("share_second"):
        own = exchange(jnp.tile(part[None], (4, 1, 1)), SECOND).reshape(slab, width)
    with jax.named_scope("share_first"):
        top, bottom = own[:half], own[half:]
        left_top = send(top, RIGHT)
        right_top = send(top, LEFT)
        left_bottom = send(bottom, RIGHT)
        right_bottom = send(bottom, LEFT)
        own_other = send(own, SWAP)
        across_top = send(left_top, RIGHT)
        across_bottom = send(right_bottom, LEFT)
        others = [send(piece, SWAP) for piece in (left_top, right_bottom, left_bottom, right_top)]
    with jax.named_scope("write"):
        outs = write((), [OWN, LEFT_TOP, RIGHT_BOTTOM, LEFT_BOTTOM, RIGHT_TOP], [OWN])(
            own, left_top, right_bottom, left_bottom, right_top, own_other, shape=matrix
        )
        across_top, across_bottom = after(outs[0], across_top, across_bottom, in_hbm=True)
        across_others = [send(across_top, SWAP), send(across_bottom, SWAP)]
        outs = write(
            tuple(outs),
            [ACROSS_TOP, ACROSS_BOTTOM],
            [LEFT_TOP, RIGHT_BOTTOM, LEFT_BOTTOM, RIGHT_TOP],
        )(across_top, across_bottom, *others, shape=matrix)
        return write(tuple(outs), [], [ACROSS_TOP, ACROSS_BOTTOM])(*across_others, shape=matrix)


def solution(mesh):
    return jax.shard_map(
        on_device,
        mesh=mesh,
        in_specs=(P("dp", None), P("dp", None), P(), P(), P("dp"), P(), P()),
        out_specs=(P(), P()),
        check_vma=False,
    )
```

```python
import jax
import jax.numpy as jnp
from jax import lax
from jax.experimental import pallas as pl
from jax.experimental.pallas import tpu as pltpu
from jax.sharding import PartitionSpec as P

NY, NX, NZ, CORES = 4, 4, 8, 2
N = NY * NX * NZ * CORES
epsilon = 1e-06
bf16, f32 = jnp.bfloat16, jnp.float32
MIB = 1 << 20


def index(y, x, z, c):
    return ((y % NY * NX + x % NX) * NZ + z % NZ) * CORES + c


PLACES = [
    (y, x, z, c) for y in range(NY) for x in range(NX) for z in range(NZ) for c in range(CORES)
]


def route(move):
    return [(index(*place), index(*move(*place))) for place in PLACES]


def groups(key):
    found = {}
    for place in PLACES:
        found.setdefault(key(*place), []).append(index(*place))
    return list(found.values())


def along_first(step):
    return route(lambda y, x, z, c: (y, x + step, z, c) if c == 0 else (y + step, x, z, c))


SWAP = route(lambda y, x, z, c: (y, x, z, 1 - c))
RIGHT, LEFT = along_first(1), along_first(-1)
SECOND = groups(lambda y, x, z, c: (c, z, x if c == 0 else y))
LINES = groups(lambda y, x, z, c: (c, x, y))
FAR = [(i, (i + 3) % N if i % 2 else (i - 3) % N) for i in range(N)]
TAIL = 16
TEXT = 1


def shifted(distance):
    return [(i, (i + distance) % N) for i in range(N)]


def send(block, pairs):
    return lax.ppermute(block, "dp", pairs)


def exchange(parts, members):
    return lax.all_to_all(parts, "dp", 0, 0, axis_index_groups=members, tiled=True)


def call(body, outs, scratch=(), flops=0, result=pltpu.VMEM, aliases=()):
    def run(smem, outside, *arrays):
        specs = (
            [pl.BlockSpec(memory_space=pltpu.SMEM)] * len(smem)
            + [pl.BlockSpec(memory_space=pltpu.HBM)] * len(outside)
            + [pl.BlockSpec(memory_space=pltpu.VMEM)] * len(arrays)
        )
        held = [pltpu.with_memory_space_constraint(a, pltpu.VMEM) for a in arrays]
        outside = [pltpu.with_memory_space_constraint(a, pltpu.HBM) for a in outside]
        return pl.pallas_call(
            body,
            out_shape=[jax.ShapeDtypeStruct(s, d) for s, d in outs],
            in_specs=specs,
            out_specs=[pl.BlockSpec(memory_space=result)] * len(outs),
            scratch_shapes=list(scratch),
            input_output_aliases=dict(aliases),
            cost_estimate=pl.CostEstimate(flops=flops, bytes_accessed=0, transcendentals=0),
            compiler_params=pltpu.CompilerParams(vmem_limit_bytes=32 * MIB),
        )(*smem, *outside, *held)

    return run


def contract(a, b, da, db):
    return lax.dot_general(a, b, (((da,), (db,)), ((), ())), preferred_element_type=f32)


def core_place():
    me = lax.axis_index("dp")
    core = lax.rem(me, CORES)
    x = lax.rem(me // (NZ * CORES), NX)
    y = me // (NX * NZ * CORES)
    return core, jnp.where(core == 0, x, y), jnp.where(core == 0, y, x)


def on_text():
    return core_place()[0] == TEXT


def factor(log_scale):
    return jnp.exp(jnp.full((1, 1), log_scale[0], f32))


def embed(features, weight):
    projected = jnp.dot(features, weight, preferred_element_type=f32)
    square = jnp.sum(projected * projected, axis=-1, keepdims=True)
    inverse = 1.0 / jnp.sqrt(square + epsilon)
    return projected, inverse


def make_head(head, pairs, before=None):
    step = 128
    for k in range(head.shape[0] // step):
        at = pl.ds(k * step, step)
        new = sum(contract(x[:, at], back[...], 0, 0) for x, back in pairs)
        head[at, :] = new if before is None else before[at, :] + new


def join_positions(image_hbm, position_hbm, out, position, sems):
    rows = position.shape[0]
    moves = [
        pltpu.make_async_copy(position_hbm, position, sems.at[0]),
        pltpu.make_async_copy(image_hbm, out.at[pl.ds(0, rows), :], sems.at[1]),
    ]
    for move in moves:
        move.start()
    tail = pl.ds(rows, TAIL)
    out[tail, :] = jnp.zeros((TAIL, out.shape[1]), bf16)
    moves[0].wait()
    row = position[...].reshape(1, rows).astype(f32)
    out[tail, pl.ds(0, rows)] = jnp.broadcast_to(row, (TAIL, rows)).astype(bf16)
    moves[1].wait()


def visit(log_scale, shift, x, text_w, image_emb, finish, back, grad, grad_before):
    scale = factor(log_scale)
    projected, inverse = embed(x[...], text_w[...])
    emb = (projected * inverse).astype(bf16)
    similarity = contract(emb, image_emb[...], 1, 1)
    coefficient = finish(jax.nn.sigmoid(scale * similarity + shift[0])).astype(bf16)

    @pl.when(on_text())
    def _():
        radial = jnp.sum(coefficient.astype(f32) * similarity, axis=-1, keepdims=True)
        gradient = jnp.dot(coefficient, image_emb[...], preferred_element_type=f32)
        outer = scale * inverse
        back[...] = (gradient * outer - projected * (outer * inverse * radial)).astype(bf16)

    @pl.when(jnp.logical_not(on_text()))
    def _():
        share = contract(coefficient, emb, 0, 0)
        grad[...] = share if grad_before is None else grad_before[...] + share


def near_kernel(
    log_scale, shift, text_hbm, text_w_hbm, image_w_hbm, text_other, image_own, image_other,
    image_near, text_w, image_emb, image_projected, image_inverse, grad, text_near, back,
    image_w, sems,
):
    rows = text_other.shape[0]
    first, second = pl.ds(0, rows), pl.ds(rows, rows)
    moves = [
        pltpu.make_async_copy(image_w_hbm, image_w, sems.at[0]),
        pltpu.make_async_copy(text_hbm, text_near.at[first, :], sems.at[1]),
        pltpu.make_async_copy(text_w_hbm, text_w, sems.at[2]),
    ]
    for move in moves:
        move.start()
    image_near[first, :] = image_own[first, :]
    image_near[second, :] = image_other[first, :]
    text_near[second, :] = text_other[...]
    moves[0].wait()
    projected, inverse = embed(image_near[...], image_w[...])
    image_emb[...] = (projected * inverse).astype(bf16)
    image_projected[...] = projected
    image_inverse[...] = inverse
    moves[1].wait()
    moves[2].wait()

    def with_labels(sigmoid):
        column = lax.broadcasted_iota(jnp.int32, (2 * rows, rows), 0)

        def positions(block):
            tail = block[pl.ds(rows, TAIL), pl.ds(0, rows)]
            return tail.astype(f32)[:1].astype(jnp.int32)

        own = (column == positions(image_own)).astype(f32)
        other = (column == positions(image_other) + rows).astype(f32)
        return sigmoid - jnp.concatenate([own, other], axis=1).T

    visit(log_scale, shift, text_near, text_w, image_emb, with_labels, back, grad, None)


def gate_kernel(*refs):
    pass


def after(token, *arrays, in_hbm=False):
    outs = [(a.shape, a.dtype) for a in arrays]
    first = 1 if in_hbm else 0
    gate = call(gate_kernel, outs, aliases=[(first + k, k) for k in range(len(arrays))])
    return gate((), (token,), *arrays) if in_hbm else gate((), (), *arrays, token)


def pair_kernel(log_scale, shift, below, above, text_w, image_emb, grad_before, grad, x, back):
    rows = below.shape[0]
    x[pl.ds(0, rows), :] = below[...]
    x[pl.ds(rows, rows), :] = above[...]
    visit(log_scale, shift, x, text_w, image_emb, lambda c: c, back, grad, grad_before)


def received_kernel(
    log_scale, shift, below, above, text_w, image_emb, grad_before, x_1, back_1,
    grad, head, x, back,
):
    pair_kernel(log_scale, shift, below, above, text_w, image_emb, grad_before, grad, x, back)

    @pl.when(on_text())
    def _():
        make_head(head, [(x_1, back_1), (x, back)])


def far_kernel(
    log_scale, shift, far, far_other, text_w, image_emb, grad_before,
    image_near, image_projected, image_inverse, head_before, x_1, back_1,
    own, right_top, right_bottom, left_top, left_bottom, far_right, far_left,
    grad, head, x, back,
):
    rows = far.shape[0]
    x[pl.ds(0, rows), :] = far[...]
    x[pl.ds(rows, rows), :] = far_other[...]

    def inside(sigmoid):
        row = lax.broadcasted_iota(jnp.int32, sigmoid.shape, 0) < rows
        column = lax.broadcasted_iota(jnp.int32, sigmoid.shape, 1) < rows
        return jnp.where(row == column, sigmoid, 0.0)

    visit(log_scale, shift, x, text_w, image_emb, inside, back, grad, grad_before)

    @pl.when(on_text())
    def _():
        make_head(head, [(x_1, back_1), (x, back)], head_before)

    @pl.when(jnp.logical_not(on_text()))
    def _():
        gradient = factor(log_scale) * grad[...]
        inverse = image_inverse[...]
        unit = image_projected[...] * inverse
        radial = jnp.sum(gradient * unit, axis=-1, keepdims=True)
        back[...] = ((gradient - unit * radial) * inverse).astype(bf16)
        make_head(head, [(image_near, back)])

    slab = head.shape[0] // 4
    half = slab // 2
    place = core_place()[1]

    def part(turn, upper, size):
        start = lax.rem(place + turn, 4) * slab + upper
        return head[pl.ds(pl.multiple_of(start, 16), size), :].astype(bf16)

    far_right[...] = part(2, 0, half)
    far_left[...] = part(2, half, half)
    right_top[...] = part(1, 0, half)
    right_bottom[...] = part(1, half, half)
    left_top[...] = part(3, 0, half)
    left_bottom[...] = part(3, half, half)
    own[...] = part(0, 0, slab)


def add_kernel(a, b, out):
    out[...] = (a[...].astype(f32) + b[...].astype(f32)).astype(bf16)


def join_kernel(own, a_top, a_bottom, b_top, b_bottom, out):
    half = a_top.shape[0]
    upper, lower = pl.ds(0, half), pl.ds(half, half)
    out[upper, :] = (
        own[upper, :].astype(f32) + a_top[...].astype(f32) + b_top[...].astype(f32)
    ).astype(bf16)
    out[lower, :] = (
        own[lower, :].astype(f32) + a_bottom[...].astype(f32) + b_bottom[...].astype(f32)
    ).astype(bf16)


OWN, LEFT_TOP, RIGHT_BOTTOM, LEFT_BOTTOM, RIGHT_TOP, ACROSS_TOP, ACROSS_BOTTOM = PIECES = (
    (0, 0), (3, 0), (1, 1), (3, 1), (1, 0), (2, 0), (2, 1)
)


def write(outs, mine, theirs):
    places = [*mine, *theirs]

    def body(*refs):
        pieces, (text, image, sems) = refs[len(outs) : len(outs) + len(places)], refs[-3:]
        core, place, other_place = core_place()

        def copies(first, other):
            moves = []
            for k, (piece, (turn, part)) in enumerate(zip(pieces, places)):
                own = k < len(mine)
                slab = piece.shape[0] * (1 if (turn, part) == OWN else 2)
                start = lax.rem((place if own else other_place) + turn, 4) * slab + part * slab // 2
                at = pl.ds(pl.multiple_of(start, 16), piece.shape[0])
                moves.append(
                    pltpu.make_async_copy(piece, (first if own else other).at[at, :], sems.at[k])
                )
            for move in moves:
                move.start()
            for move in moves:
                move.wait()

        @pl.when(core == TEXT)
        def _():
            copies(text, image)

        @pl.when(core != TEXT)
        def _():
            copies(image, text)

    def run(*arrays, shape):
        return call(
            body,
            [shape, shape],
            [pltpu.SemaphoreType.DMA((len(places),))],
            result=pltpu.HBM,
            aliases=[(k, k) for k in range(len(outs))],
        )((), outs, *arrays)

    return run


def on_device(text_x, image_x, text_w, image_w, position, log_scale, shift):
    rows, width = text_x.shape
    depth = text_w.shape[0]
    slab = depth // 4
    half = slab // 2
    scalars = (log_scale, shift)
    pair, pair_f32 = ((2 * rows, width), bf16), ((2 * rows, width), f32)
    total = ((depth, width), f32)
    matrix = ((depth, width), bf16)
    piece, half_piece = ((slab, width), bf16), ((half, width), bf16)
    with jax.named_scope("band_exchange"):
        text_other = send(text_x, SWAP)
        [image_own] = call(
            join_positions,
            [((rows + TAIL, width), bf16)],
            [pltpu.VMEM((rows,), jnp.int32), pltpu.SemaphoreType.DMA((2,))],
        )((), (image_x, position))
        image_other = send(image_own, SWAP)
        below = send(text_x, shifted(2))
        above = send(text_x, shifted(-2))
        far = send(text_x, FAR)
    with jax.named_scope("near"):
        image_near, weight, image_emb, image_projected, image_inverse, grad, *near = call(
            near_kernel,
            [pair, matrix, pair, pair_f32, ((2 * rows, 1), f32), pair_f32, pair, pair],
            [pltpu.VMEM(*matrix), pltpu.SemaphoreType.DMA((3,))],
            flops=4 * 10**9,
        )(
            scalars, (text_x, text_w, image_w), text_other, image_own, image_other
        )
    with jax.named_scope("swap_neighbours"):
        above, below = after(image_inverse, above, below)
        below_other = send(below, SWAP)
        above_other = send(above, SWAP)
    with jax.named_scope("received"):
        grad, head = call(
            received_kernel,
            [pair_f32, total],
            [pltpu.VMEM(*pair), pltpu.VMEM(*pair)],
            flops=4 * 10**9,
        )(scalars, (), below, above, weight, image_emb, grad, *near)
        [far] = after(grad, far)
        far_other = send(far, SWAP)
    with jax.named_scope("partners"):
        grad, *second = call(pair_kernel, [pair_f32, pair, pair], flops=4 * 10**9)(
            scalars, (), below_other, above_other, weight, image_emb, grad
        )
    with jax.named_scope("far"):
        own, right_top, right_bottom, left_top, left_bottom, far_right, far_left = call(
            far_kernel,
            [piece] + [half_piece] * 6,
            [pltpu.VMEM(*pair_f32), pltpu.VMEM(*total), pltpu.VMEM(*pair), pltpu.VMEM(*pair)],
            flops=4 * 10**9,
        )(
            scalars, (), far, far_other, weight, image_emb, grad, image_near, image_projected,
            image_inverse, head, *second,
        )
    with jax.named_scope("sum_first"):
        from_left = send(far_right, RIGHT)
        from_right = send(far_left, LEFT)
        a_bottom = send(right_bottom, RIGHT)
        b_top = send(left_top, LEFT)
        [right_top] = call(add_kernel, [half_piece])((), (), right_top, from_left)
        [left_bottom] = call(add_kernel, [half_piece])((), (), left_bottom, from_right)
        a_top = send(right_top, RIGHT)
        b_bottom = send(left_bottom, LEFT)
        [part] = call(join_kernel, [piece])((), (), own, a_top, a_bottom, b_top, b_bottom)
    with jax.named_scope("sum_second"):
        part = exchange(part.reshape(4, slab // 4, width), SECOND)
        part = jnp.sum(part.astype(f32), axis=0).astype(bf16)
    with jax.named_scope("sum_lines"):
        tiles = (
            part.reshape(slab // 32, 8, width // 128, 128).transpose(0, 2, 1, 3).reshape(-1, 8, 128)
        )
        count = tiles.shape[0]
        each = -(-count // NZ)
        tiles = jnp.concatenate([tiles, jnp.zeros((each * NZ - count, 8, 128), bf16)])
        tiles = exchange(tiles, LINES).reshape(NZ, each, 8, 128)
        tiles = jnp.sum(tiles.astype(f32), axis=0).astype(bf16)
    with jax.named_scope("share_lines"):
        tiles = exchange(jnp.tile(tiles, (NZ, 1, 1)), LINES)[:count]
        part = (
            tiles.reshape(slab // 32, width // 128, 8, 128).transpose(0, 2, 1, 3).reshape(-1, width)
        )
    with jax.named_scope("share_second"):
        own = exchange(jnp.tile(part[None], (4, 1, 1)), SECOND).reshape(slab, width)
    with jax.named_scope("share_first"):
        top, bottom = own[:half], own[half:]
        left_top = send(top, RIGHT)
        right_top = send(top, LEFT)
        left_bottom = send(bottom, RIGHT)
        right_bottom = send(bottom, LEFT)
        own_other = send(own, SWAP)
        across_top = send(left_top, RIGHT)
        across_bottom = send(right_bottom, LEFT)
        others = [send(piece, SWAP) for piece in (left_top, right_bottom, left_bottom, right_top)]
    with jax.named_scope("write"):
        outs = write((), [OWN, LEFT_TOP, RIGHT_BOTTOM, LEFT_BOTTOM, RIGHT_TOP], [OWN])(
            own, left_top, right_bottom, left_bottom, right_top, own_other, shape=matrix
        )
        [across_top] = after(outs[0], across_top, in_hbm=True)
        [across_bottom] = after(outs[0], across_bottom, in_hbm=True)
        across_others = [send(across_top, SWAP), send(across_bottom, SWAP)]
        outs = write(
            tuple(outs),
            [ACROSS_TOP, ACROSS_BOTTOM],
            [LEFT_TOP, RIGHT_BOTTOM, LEFT_BOTTOM, RIGHT_TOP],
        )(across_top, across_bottom, *others, shape=matrix)
        return write(tuple(outs), [], [ACROSS_TOP, ACROSS_BOTTOM])(*across_others, shape=matrix)


def solution(mesh):
    return jax.shard_map(
        on_device,
        mesh=mesh,
        in_specs=(P("dp", None), P("dp", None), P(), P(), P("dp"), P(), P()),
        out_specs=(P(), P()),
        check_vma=False,
    )
```

```python
import jax
import jax.numpy as jnp
from jax import lax
from jax.experimental import pallas as pl
from jax.experimental.pallas import tpu as pltpu
from jax.sharding import PartitionSpec as P

NY, NX, NZ, CORES = 4, 4, 8, 2
N = NY * NX * NZ * CORES
epsilon = 1e-06
bf16, f32 = jnp.bfloat16, jnp.float32
MIB = 1 << 20


def index(y, x, z, c):
    return ((y % NY * NX + x % NX) * NZ + z % NZ) * CORES + c


PLACES = [
    (y, x, z, c) for y in range(NY) for x in range(NX) for z in range(NZ) for c in range(CORES)
]


def route(move):
    return [(index(*place), index(*move(*place))) for place in PLACES]


def groups(key):
    found = {}
    for place in PLACES:
        found.setdefault(key(*place), []).append(index(*place))
    return list(found.values())


def along_first(step):
    return route(lambda y, x, z, c: (y, x + step, z, c) if c == 0 else (y + step, x, z, c))


SWAP = route(lambda y, x, z, c: (y, x, z, 1 - c))
RIGHT, LEFT = along_first(1), along_first(-1)
SECOND = groups(lambda y, x, z, c: (c, z, x if c == 0 else y))
LINES = groups(lambda y, x, z, c: (c, x, y))
FAR = [(i, (i + 3) % N if i % 2 else (i - 3) % N) for i in range(N)]
TAIL = 16
TEXT = 1


def shifted(distance):
    return [(i, (i + distance) % N) for i in range(N)]


def send(block, pairs):
    return lax.ppermute(block, "dp", pairs)


def exchange(parts, members):
    return lax.all_to_all(parts, "dp", 0, 0, axis_index_groups=members, tiled=True)


def call(body, outs, scratch=(), flops=0, result=pltpu.VMEM, aliases=()):
    def run(smem, outside, *arrays):
        specs = (
            [pl.BlockSpec(memory_space=pltpu.SMEM)] * len(smem)
            + [pl.BlockSpec(memory_space=pltpu.HBM)] * len(outside)
            + [pl.BlockSpec(memory_space=pltpu.VMEM)] * len(arrays)
        )
        held = [pltpu.with_memory_space_constraint(a, pltpu.VMEM) for a in arrays]
        outside = [pltpu.with_memory_space_constraint(a, pltpu.HBM) for a in outside]
        return pl.pallas_call(
            body,
            out_shape=[jax.ShapeDtypeStruct(s, d) for s, d in outs],
            in_specs=specs,
            out_specs=[pl.BlockSpec(memory_space=result)] * len(outs),
            scratch_shapes=list(scratch),
            input_output_aliases=dict(aliases),
            cost_estimate=pl.CostEstimate(flops=flops, bytes_accessed=0, transcendentals=0),
            compiler_params=pltpu.CompilerParams(vmem_limit_bytes=32 * MIB),
        )(*smem, *outside, *held)

    return run


def contract(a, b, da, db):
    return lax.dot_general(a, b, (((da,), (db,)), ((), ())), preferred_element_type=f32)


def core_place():
    me = lax.axis_index("dp")
    core = lax.rem(me, CORES)
    x = lax.rem(me // (NZ * CORES), NX)
    y = me // (NX * NZ * CORES)
    return core, jnp.where(core == 0, x, y), jnp.where(core == 0, y, x)


def on_text():
    return core_place()[0] == TEXT


def factor(log_scale):
    return jnp.exp(jnp.full((1, 1), log_scale[0], f32))


def embed(features, weight):
    projected = jnp.dot(features, weight, preferred_element_type=f32)
    square = jnp.sum(projected * projected, axis=-1, keepdims=True)
    inverse = 1.0 / jnp.sqrt(square + epsilon)
    return projected, inverse


def add_head(head, x, back, before):
    step = head.shape[0] // 3
    for k in range(3):
        at = pl.ds(k * step, step)
        new = contract(x[:, at], back[...], 0, 0)
        head[at, :] = new if before is None else before[at, :] + new


def join_positions(image_hbm, position_hbm, out, position, sems):
    rows = position.shape[0]
    moves = [
        pltpu.make_async_copy(position_hbm, position, sems.at[0]),
        pltpu.make_async_copy(image_hbm, out.at[pl.ds(0, rows), :], sems.at[1]),
    ]
    for move in moves:
        move.start()
    tail = pl.ds(rows, TAIL)
    out[tail, :] = jnp.zeros((TAIL, out.shape[1]), bf16)
    moves[0].wait()
    row = position[...].reshape(1, rows).astype(f32)
    out[tail, pl.ds(0, rows)] = jnp.broadcast_to(row, (TAIL, rows)).astype(bf16)
    moves[1].wait()


def visit(log_scale, shift, x, text_w, image_emb, finish, back, grad, grad_before):
    scale = factor(log_scale)
    projected, inverse = embed(x[...], text_w[...])
    emb = (projected * inverse).astype(bf16)
    similarity = contract(emb, image_emb[...], 1, 1)
    coefficient = finish(jax.nn.sigmoid(scale * similarity + shift[0])).astype(bf16)

    @pl.when(on_text())
    def _():
        radial = jnp.sum(coefficient.astype(f32) * similarity, axis=-1, keepdims=True)
        gradient = jnp.dot(coefficient, image_emb[...], preferred_element_type=f32)
        outer = scale * inverse
        back[...] = (gradient * outer - projected * (outer * inverse * radial)).astype(bf16)

    @pl.when(jnp.logical_not(on_text()))
    def _():
        share = contract(coefficient, emb, 0, 0)
        grad[...] = share if grad_before is None else grad_before[...] + share


def near_kernel(
    log_scale, shift, text_hbm, text_w_hbm, image_w_hbm, text_other, image_own, image_other,
    image_near, text_w, image_emb, image_projected, image_inverse, grad, head,
    text_near, image_w, back, sems,
):
    rows = text_other.shape[0]
    first, second = pl.ds(0, rows), pl.ds(rows, rows)
    moves = [
        pltpu.make_async_copy(image_w_hbm, image_w, sems.at[0]),
        pltpu.make_async_copy(text_hbm, text_near.at[first, :], sems.at[1]),
        pltpu.make_async_copy(text_w_hbm, text_w, sems.at[2]),
    ]
    for move in moves:
        move.start()
    image_near[first, :] = image_own[first, :]
    image_near[second, :] = image_other[first, :]
    text_near[second, :] = text_other[...]
    moves[0].wait()
    projected, inverse = embed(image_near[...], image_w[...])
    image_emb[...] = (projected * inverse).astype(bf16)
    image_projected[...] = projected
    image_inverse[...] = inverse
    moves[1].wait()
    moves[2].wait()

    def with_labels(sigmoid):
        column = lax.broadcasted_iota(jnp.int32, (2 * rows, rows), 0)

        def positions(block):
            tail = block[pl.ds(rows, TAIL), pl.ds(0, rows)]
            return tail.astype(f32)[:1].astype(jnp.int32)

        own = (column == positions(image_own)).astype(f32)
        other = (column == positions(image_other) + rows).astype(f32)
        return sigmoid - jnp.concatenate([own, other], axis=1).T

    visit(log_scale, shift, text_near, text_w, image_emb, with_labels, back, grad, None)

    @pl.when(on_text())
    def _():
        add_head(head, text_near, back, None)


def gate_kernel(*refs):
    pass


def after(token, *arrays, in_hbm=False):
    outs = [(a.shape, a.dtype) for a in arrays]
    first = 1 if in_hbm else 0
    gate = call(gate_kernel, outs, aliases=[(first + k, k) for k in range(len(arrays))])
    return gate((), (token,), *arrays) if in_hbm else gate((), (), *arrays, token)


def pair_kernel(
    log_scale, shift, below, above, text_w, image_emb, grad_before, head_before,
    grad, head, x, back,
):
    rows = below.shape[0]
    x[pl.ds(0, rows), :] = below[...]
    x[pl.ds(rows, rows), :] = above[...]
    visit(log_scale, shift, x, text_w, image_emb, lambda c: c, back, grad, grad_before)

    @pl.when(on_text())
    def _():
        add_head(head, x, back, head_before)


def far_kernel(
    log_scale, shift, far, far_other, text_w, image_emb, grad_before, head_before,
    image_near, image_projected, image_inverse,
    own, right_top, right_bottom, left_top, left_bottom, far_right, far_left,
    grad, head, x, back,
):
    rows = far.shape[0]
    x[pl.ds(0, rows), :] = far[...]
    x[pl.ds(rows, rows), :] = far_other[...]

    def inside(sigmoid):
        row = lax.broadcasted_iota(jnp.int32, sigmoid.shape, 0) < rows
        column = lax.broadcasted_iota(jnp.int32, sigmoid.shape, 1) < rows
        return jnp.where(row == column, sigmoid, 0.0)

    visit(log_scale, shift, x, text_w, image_emb, inside, back, grad, grad_before)

    @pl.when(on_text())
    def _():
        add_head(head, x, back, head_before)

    @pl.when(jnp.logical_not(on_text()))
    def _():
        gradient = factor(log_scale) * grad[...]
        inverse = image_inverse[...]
        unit = image_projected[...] * inverse
        radial = jnp.sum(gradient * unit, axis=-1, keepdims=True)
        back[...] = ((gradient - unit * radial) * inverse).astype(bf16)
        add_head(head, image_near, back, None)

    slab = head.shape[0] // 4
    half = slab // 2
    place = core_place()[1]

    def part(turn, upper, size):
        start = lax.rem(place + turn, 4) * slab + upper
        return head[pl.ds(pl.multiple_of(start, 16), size), :].astype(bf16)

    far_right[...] = part(2, 0, half)
    far_left[...] = part(2, half, half)
    right_top[...] = part(1, 0, half)
    right_bottom[...] = part(1, half, half)
    left_top[...] = part(3, 0, half)
    left_bottom[...] = part(3, half, half)
    own[...] = part(0, 0, slab)


def add_kernel(a, b, out):
    out[...] = (a[...].astype(f32) + b[...].astype(f32)).astype(bf16)


def join_kernel(own, a_top, a_bottom, b_top, b_bottom, out):
    half = a_top.shape[0]
    upper, lower = pl.ds(0, half), pl.ds(half, half)
    out[upper, :] = (
        own[upper, :].astype(f32) + a_top[...].astype(f32) + b_top[...].astype(f32)
    ).astype(bf16)
    out[lower, :] = (
        own[lower, :].astype(f32) + a_bottom[...].astype(f32) + b_bottom[...].astype(f32)
    ).astype(bf16)


OWN, LEFT_TOP, RIGHT_BOTTOM, LEFT_BOTTOM, RIGHT_TOP, ACROSS_TOP, ACROSS_BOTTOM = PIECES = (
    (0, 0), (3, 0), (1, 1), (3, 1), (1, 0), (2, 0), (2, 1)
)


def write(outs, mine, theirs):
    places = [*mine, *theirs]

    def body(*refs):
        pieces, (text, image, sems) = refs[len(outs) : len(outs) + len(places)], refs[-3:]
        core, place, other_place = core_place()

        def copies(first, other):
            moves = []
            for k, (piece, (turn, part)) in enumerate(zip(pieces, places)):
                own = k < len(mine)
                slab = piece.shape[0] * (1 if (turn, part) == OWN else 2)
                start = lax.rem((place if own else other_place) + turn, 4) * slab + part * slab // 2
                at = pl.ds(pl.multiple_of(start, 16), piece.shape[0])
                moves.append(
                    pltpu.make_async_copy(piece, (first if own else other).at[at, :], sems.at[k])
                )
            for move in moves:
                move.start()
            for move in moves:
                move.wait()

        @pl.when(core == TEXT)
        def _():
            copies(text, image)

        @pl.when(core != TEXT)
        def _():
            copies(image, text)

    def run(*arrays, shape):
        return call(
            body,
            [shape, shape],
            [pltpu.SemaphoreType.DMA((len(places),))],
            result=pltpu.HBM,
            aliases=[(k, k) for k in range(len(outs))],
        )((), outs, *arrays)

    return run


def on_device(text_x, image_x, text_w, image_w, position, log_scale, shift):
    rows, width = text_x.shape
    depth = text_w.shape[0]
    slab = depth // 4
    half = slab // 2
    scalars = (log_scale, shift)
    pair, pair_f32 = ((2 * rows, width), bf16), ((2 * rows, width), f32)
    total = ((depth, width), f32)
    matrix = ((depth, width), bf16)
    piece, half_piece = ((slab, width), bf16), ((half, width), bf16)
    with jax.named_scope("band_exchange"):
        text_other = send(text_x, SWAP)
        [image_own] = call(
            join_positions,
            [((rows + TAIL, width), bf16)],
            [pltpu.VMEM((rows,), jnp.int32), pltpu.SemaphoreType.DMA((2,))],
        )((), (image_x, position))
        image_other = send(image_own, SWAP)
        below = send(text_x, shifted(2))
        above = send(text_x, shifted(-2))
        far = send(text_x, FAR)
    with jax.named_scope("near"):
        image_near, weight, image_emb, image_projected, image_inverse, grad, head = call(
            near_kernel,
            [pair, matrix, pair, pair_f32, ((2 * rows, 1), f32), pair_f32, total],
            [
                pltpu.VMEM(*pair),
                pltpu.VMEM(*matrix),
                pltpu.VMEM(*pair),
                pltpu.SemaphoreType.DMA((3,)),
            ],
            flops=4 * 10**9,
        )(
            scalars, (text_x, text_w, image_w), text_other, image_own, image_other
        )
    with jax.named_scope("swap_neighbours"):
        below, above = after(image_inverse, below, above)
        below_other = send(below, SWAP)
        above_other = send(above, SWAP)
    visits = call(
        pair_kernel, [pair_f32, total], [pltpu.VMEM(*pair), pltpu.VMEM(*pair)], flops=4 * 10**9
    )
    with jax.named_scope("received"):
        grad, head = visits(scalars, (), below, above, weight, image_emb, grad, head)
        [far] = after(grad, far)
        far_other = send(far, SWAP)
    with jax.named_scope("partners"):
        grad, head = visits(scalars, (), below_other, above_other, weight, image_emb, grad, head)
    with jax.named_scope("far"):
        own, right_top, right_bottom, left_top, left_bottom, far_right, far_left = call(
            far_kernel,
            [piece] + [half_piece] * 6,
            [pltpu.VMEM(*pair_f32), pltpu.VMEM(*total), pltpu.VMEM(*pair), pltpu.VMEM(*pair)],
            flops=4 * 10**9,
        )(
            scalars, (), far, far_other, weight, image_emb, grad, head, image_near,
            image_projected, image_inverse,
        )
    with jax.named_scope("sum_first"):
        from_left = send(far_right, RIGHT)
        from_right = send(far_left, LEFT)
        a_bottom = send(right_bottom, RIGHT)
        b_top = send(left_top, LEFT)
        [right_top] = call(add_kernel, [half_piece])((), (), right_top, from_left)
        [left_bottom] = call(add_kernel, [half_piece])((), (), left_bottom, from_right)
        a_top = send(right_top, RIGHT)
        b_bottom = send(left_bottom, LEFT)
        [part] = call(join_kernel, [piece])((), (), own, a_top, a_bottom, b_top, b_bottom)
    with jax.named_scope("sum_second"):
        part = exchange(part.reshape(4, slab // 4, width), SECOND)
        part = jnp.sum(part.astype(f32), axis=0).astype(bf16)
    with jax.named_scope("sum_lines"):
        tiles = (
            part.reshape(slab // 32, 8, width // 128, 128).transpose(0, 2, 1, 3).reshape(-1, 8, 128)
        )
        count = tiles.shape[0]
        each = -(-count // NZ)
        tiles = jnp.concatenate([tiles, jnp.zeros((each * NZ - count, 8, 128), bf16)])
        tiles = exchange(tiles, LINES).reshape(NZ, each, 8, 128)
        tiles = jnp.sum(tiles.astype(f32), axis=0).astype(bf16)
    with jax.named_scope("share_lines"):
        tiles = exchange(jnp.tile(tiles, (NZ, 1, 1)), LINES)[:count]
        part = (
            tiles.reshape(slab // 32, width // 128, 8, 128).transpose(0, 2, 1, 3).reshape(-1, width)
        )
    with jax.named_scope("share_second"):
        own = exchange(jnp.tile(part[None], (4, 1, 1)), SECOND).reshape(slab, width)
    with jax.named_scope("share_first"):
        top, bottom = own[:half], own[half:]
        left_top = send(top, RIGHT)
        right_top = send(top, LEFT)
        left_bottom = send(bottom, RIGHT)
        right_bottom = send(bottom, LEFT)
        own_other = send(own, SWAP)
        across_top = send(left_top, RIGHT)
        across_bottom = send(right_bottom, LEFT)
        others = [send(piece, SWAP) for piece in (left_top, right_bottom, left_bottom, right_top)]
    with jax.named_scope("write"):
        outs = write((), [OWN, LEFT_TOP, RIGHT_BOTTOM, LEFT_BOTTOM, RIGHT_TOP], [OWN])(
            own, left_top, right_bottom, left_bottom, right_top, own_other, shape=matrix
        )
        across_top, across_bottom = after(outs[0], across_top, across_bottom, in_hbm=True)
        across_others = [send(across_top, SWAP), send(across_bottom, SWAP)]
        outs = write(
            tuple(outs),
            [ACROSS_TOP, ACROSS_BOTTOM],
            [LEFT_TOP, RIGHT_BOTTOM, LEFT_BOTTOM, RIGHT_TOP],
        )(across_top, across_bottom, *others, shape=matrix)
        return write(tuple(outs), [], [ACROSS_TOP, ACROSS_BOTTOM])(*across_others, shape=matrix)


def solution(mesh):
    return jax.shard_map(
        on_device,
        mesh=mesh,
        in_specs=(P("dp", None), P("dp", None), P(), P(), P("dp"), P(), P()),
        out_specs=(P(), P()),
        check_vma=False,
    )
```

```python
import jax
import jax.numpy as jnp
from jax import lax
from jax.experimental import pallas as pl
from jax.experimental.pallas import tpu as pltpu
from jax.sharding import PartitionSpec as P

NY, NX, NZ, CORES = 4, 4, 8, 2
N = NY * NX * NZ * CORES
epsilon = 1e-06
bf16, f32 = jnp.bfloat16, jnp.float32
MIB = 1 << 20


def index(y, x, z, c):
    return ((y % NY * NX + x % NX) * NZ + z % NZ) * CORES + c


PLACES = [
    (y, x, z, c) for y in range(NY) for x in range(NX) for z in range(NZ) for c in range(CORES)
]


def route(move):
    return [(index(*place), index(*move(*place))) for place in PLACES]


def groups(key):
    found = {}
    for place in PLACES:
        found.setdefault(key(*place), []).append(index(*place))
    return list(found.values())


def along_first(step):
    return route(lambda y, x, z, c: (y, x + step, z, c) if c == 0 else (y + step, x, z, c))


SWAP = route(lambda y, x, z, c: (y, x, z, 1 - c))
RIGHT, LEFT = along_first(1), along_first(-1)
SECOND = groups(lambda y, x, z, c: (c, z, x if c == 0 else y))
LINES = groups(lambda y, x, z, c: (c, x, y))
FAR = [(i, (i + 3) % N if i % 2 else (i - 3) % N) for i in range(N)]
TEXT = 1


def shifted(distance):
    return [(i, (i + distance) % N) for i in range(N)]


def send(block, pairs):
    return lax.ppermute(block, "dp", pairs)


def exchange(parts, members):
    return lax.all_to_all(parts, "dp", 0, 0, axis_index_groups=members, tiled=True)


def call(body, outs, scratch=(), flops=0, result=pltpu.VMEM, aliases=()):
    def run(smem, outside, *arrays):
        specs = (
            [pl.BlockSpec(memory_space=pltpu.SMEM)] * len(smem)
            + [pl.BlockSpec(memory_space=pltpu.HBM)] * len(outside)
            + [pl.BlockSpec(memory_space=pltpu.VMEM)] * len(arrays)
        )
        held = [pltpu.with_memory_space_constraint(a, pltpu.VMEM) for a in arrays]
        outside = [pltpu.with_memory_space_constraint(a, pltpu.HBM) for a in outside]
        return pl.pallas_call(
            body,
            out_shape=[jax.ShapeDtypeStruct(s, d) for s, d in outs],
            in_specs=specs,
            out_specs=[pl.BlockSpec(memory_space=result)] * len(outs),
            scratch_shapes=list(scratch),
            input_output_aliases=dict(aliases),
            cost_estimate=pl.CostEstimate(flops=flops, bytes_accessed=0, transcendentals=0),
            compiler_params=pltpu.CompilerParams(vmem_limit_bytes=32 * MIB),
        )(*smem, *outside, *held)

    return run


def contract(a, b, da, db):
    return lax.dot_general(a, b, (((da,), (db,)), ((), ())), preferred_element_type=f32)


def core_place():
    me = lax.axis_index("dp")
    core = lax.rem(me, CORES)
    x = lax.rem(me // (NZ * CORES), NX)
    y = me // (NX * NZ * CORES)
    return core, jnp.where(core == 0, x, y), jnp.where(core == 0, y, x)


def on_text():
    return core_place()[0] == TEXT


def factor(log_scale):
    return jnp.exp(jnp.full((1, 1), log_scale[0], f32))


def embed(features, weight):
    projected = jnp.dot(features, weight, preferred_element_type=f32)
    square = jnp.sum(projected * projected, axis=-1, keepdims=True)
    inverse = 1.0 / jnp.sqrt(square + epsilon)
    return projected, inverse


def make_head(head, pairs, before=None):
    step = 128
    for k in range(head.shape[0] // step):
        at = pl.ds(k * step, step)
        new = sum(contract(x[:, at], back[...], 0, 0) for x, back in pairs)
        head[at, :] = new if before is None else before[at, :] + new


def visit(log_scale, shift, x, text_w, image_emb, finish, back, grad, grad_before):
    scale = factor(log_scale)
    projected, inverse = embed(x[...], text_w[...])
    emb = (projected * inverse).astype(bf16)
    similarity = contract(emb, image_emb[...], 1, 1)
    coefficient = finish(jax.nn.sigmoid(scale * similarity + shift[0])).astype(bf16)

    @pl.when(on_text())
    def _():
        radial = jnp.sum(coefficient.astype(f32) * similarity, axis=-1, keepdims=True)
        gradient = jnp.dot(coefficient, image_emb[...], preferred_element_type=f32)
        outer = scale * inverse
        back[...] = (gradient * outer - projected * (outer * inverse * radial)).astype(bf16)

    @pl.when(jnp.logical_not(on_text()))
    def _():
        share = contract(coefficient, emb, 0, 0)
        grad[...] = share if grad_before is None else grad_before[...] + share


def near_kernel(
    log_scale, shift, text_hbm, image_hbm, text_w_hbm, image_w_hbm, text_other, image_other,
    position, position_other,
    image_near, text_w, image_emb, image_projected, image_inverse, grad, text_near, back,
    image_w, sems,
):
    rows = text_other.shape[0]
    first, second = pl.ds(0, rows), pl.ds(rows, rows)
    moves = [
        pltpu.make_async_copy(image_hbm, image_near.at[first, :], sems.at[0]),
        pltpu.make_async_copy(image_w_hbm, image_w, sems.at[1]),
        pltpu.make_async_copy(text_hbm, text_near.at[first, :], sems.at[2]),
        pltpu.make_async_copy(text_w_hbm, text_w, sems.at[3]),
    ]
    for move in moves:
        move.start()
    image_near[second, :] = image_other[...]
    text_near[second, :] = text_other[...]
    moves[0].wait()
    moves[1].wait()
    projected, inverse = embed(image_near[...], image_w[...])
    image_emb[...] = (projected * inverse).astype(bf16)
    image_projected[...] = projected
    image_inverse[...] = inverse
    moves[2].wait()
    moves[3].wait()

    def with_labels(sigmoid):
        column = lax.broadcasted_iota(jnp.int32, (2 * rows, rows), 0)
        own = (column == position[...]).astype(f32)
        other = (column == position_other[...] + rows).astype(f32)
        return sigmoid - jnp.concatenate([own, other], axis=1).T

    visit(log_scale, shift, text_near, text_w, image_emb, with_labels, back, grad, None)


def gate_kernel(*refs):
    pass


def after(token, *arrays, in_hbm=False):
    outs = [(a.shape, a.dtype) for a in arrays]
    first = 1 if in_hbm else 0
    gate = call(gate_kernel, outs, aliases=[(first + k, k) for k in range(len(arrays))])
    return gate((), (token,), *arrays) if in_hbm else gate((), (), *arrays, token)


def pair_kernel(log_scale, shift, below, above, text_w, image_emb, grad_before, grad, x, back):
    rows = below.shape[0]
    x[pl.ds(0, rows), :] = below[...]
    x[pl.ds(rows, rows), :] = above[...]
    visit(log_scale, shift, x, text_w, image_emb, lambda c: c, back, grad, grad_before)


def received_kernel(
    log_scale, shift, below, above, text_w, image_emb, grad_before, x_1, back_1,
    grad, head, x, back,
):
    pair_kernel(log_scale, shift, below, above, text_w, image_emb, grad_before, grad, x, back)

    @pl.when(on_text())
    def _():
        make_head(head, [(x_1, back_1), (x, back)])


def far_kernel(
    log_scale, shift, far, far_other, text_w, image_emb, grad_before,
    image_near, image_projected, image_inverse, head_before, x_1, back_1,
    own, right_top, right_bottom, left_top, left_bottom, far_right, far_left,
    grad, head, x, back,
):
    rows = far.shape[0]
    x[pl.ds(0, rows), :] = far[...]
    x[pl.ds(rows, rows), :] = far_other[...]

    def inside(sigmoid):
        row = lax.broadcasted_iota(jnp.int32, sigmoid.shape, 0) < rows
        column = lax.broadcasted_iota(jnp.int32, sigmoid.shape, 1) < rows
        return jnp.where(row == column, sigmoid, 0.0)

    visit(log_scale, shift, x, text_w, image_emb, inside, back, grad, grad_before)

    @pl.when(on_text())
    def _():
        make_head(head, [(x_1, back_1), (x, back)], head_before)

    @pl.when(jnp.logical_not(on_text()))
    def _():
        gradient = factor(log_scale) * grad[...]
        inverse = image_inverse[...]
        unit = image_projected[...] * inverse
        radial = jnp.sum(gradient * unit, axis=-1, keepdims=True)
        back[...] = ((gradient - unit * radial) * inverse).astype(bf16)
        make_head(head, [(image_near, back)])

    slab = head.shape[0] // 4
    half = slab // 2
    place = core_place()[1]

    def part(turn, upper, size):
        start = lax.rem(place + turn, 4) * slab + upper
        return head[pl.ds(pl.multiple_of(start, 16), size), :].astype(bf16)

    far_right[...] = part(2, 0, half)
    far_left[...] = part(2, half, half)
    right_top[...] = part(1, 0, half)
    right_bottom[...] = part(1, half, half)
    left_top[...] = part(3, 0, half)
    left_bottom[...] = part(3, half, half)
    own[...] = part(0, 0, slab)


def add_kernel(a, b, out):
    out[...] = (a[...].astype(f32) + b[...].astype(f32)).astype(bf16)


def join_kernel(own, a_top, a_bottom, b_top, b_bottom, out):
    half = a_top.shape[0]
    upper, lower = pl.ds(0, half), pl.ds(half, half)
    out[upper, :] = (
        own[upper, :].astype(f32) + a_top[...].astype(f32) + b_top[...].astype(f32)
    ).astype(bf16)
    out[lower, :] = (
        own[lower, :].astype(f32) + a_bottom[...].astype(f32) + b_bottom[...].astype(f32)
    ).astype(bf16)


OWN, LEFT_TOP, RIGHT_BOTTOM, LEFT_BOTTOM, RIGHT_TOP, ACROSS_TOP, ACROSS_BOTTOM = PIECES = (
    (0, 0), (3, 0), (1, 1), (3, 1), (1, 0), (2, 0), (2, 1)
)


def write(outs, mine, theirs):
    places = [*mine, *theirs]

    def body(*refs):
        pieces, (text, image, sems) = refs[len(outs) : len(outs) + len(places)], refs[-3:]
        core, place, other_place = core_place()

        def copies(first, other):
            moves = []
            for k, (piece, (turn, part)) in enumerate(zip(pieces, places)):
                own = k < len(mine)
                slab = piece.shape[0] * (1 if (turn, part) == OWN else 2)
                start = lax.rem((place if own else other_place) + turn, 4) * slab + part * slab // 2
                at = pl.ds(pl.multiple_of(start, 16), piece.shape[0])
                moves.append(
                    pltpu.make_async_copy(piece, (first if own else other).at[at, :], sems.at[k])
                )
            for move in moves:
                move.start()
            for move in moves:
                move.wait()

        @pl.when(core == TEXT)
        def _():
            copies(text, image)

        @pl.when(core != TEXT)
        def _():
            copies(image, text)

    def run(*arrays, shape):
        return call(
            body,
            [shape, shape],
            [pltpu.SemaphoreType.DMA((len(places),))],
            result=pltpu.HBM,
            aliases=[(k, k) for k in range(len(outs))],
        )((), outs, *arrays)

    return run


def on_device(text_x, image_x, text_w, image_w, position, log_scale, shift):
    rows, width = text_x.shape
    depth = text_w.shape[0]
    slab = depth // 4
    half = slab // 2
    scalars = (log_scale, shift)
    pair, pair_f32 = ((2 * rows, width), bf16), ((2 * rows, width), f32)
    total = ((depth, width), f32)
    matrix = ((depth, width), bf16)
    piece, half_piece = ((slab, width), bf16), ((half, width), bf16)
    with jax.named_scope("band_exchange"):
        text_other = send(text_x, SWAP)
        image_other = send(image_x, SWAP)
        position_other = send(position, SWAP)
        below = send(text_x, shifted(2))
        above = send(text_x, shifted(-2))
        far = send(text_x, FAR)
    with jax.named_scope("near"):
        image_near, weight, image_emb, image_projected, image_inverse, grad, *near = call(
            near_kernel,
            [pair, matrix, pair, pair_f32, ((2 * rows, 1), f32), pair_f32, pair, pair],
            [pltpu.VMEM(*matrix), pltpu.SemaphoreType.DMA((4,))],
            flops=4 * 10**9,
        )(
            scalars, (text_x, image_x, text_w, image_w), text_other, image_other,
            position[None], position_other[None],
        )
    with jax.named_scope("swap_neighbours"):
        above, below = after(image_inverse, above, below)
        below_other = send(below, SWAP)
        above_other = send(above, SWAP)
    with jax.named_scope("received"):
        grad, head = call(
            received_kernel,
            [pair_f32, total],
            [pltpu.VMEM(*pair), pltpu.VMEM(*pair)],
            flops=4 * 10**9,
        )(scalars, (), below, above, weight, image_emb, grad, *near)
        [far] = after(grad, far)
        far_other = send(far, SWAP)
    with jax.named_scope("partners"):
        grad, *second = call(pair_kernel, [pair_f32, pair, pair], flops=4 * 10**9)(
            scalars, (), below_other, above_other, weight, image_emb, grad
        )
    with jax.named_scope("far"):
        own, right_top, right_bottom, left_top, left_bottom, far_right, far_left = call(
            far_kernel,
            [piece] + [half_piece] * 6,
            [pltpu.VMEM(*pair_f32), pltpu.VMEM(*total), pltpu.VMEM(*pair), pltpu.VMEM(*pair)],
            flops=4 * 10**9,
        )(
            scalars, (), far, far_other, weight, image_emb, grad, image_near, image_projected,
            image_inverse, head, *second,
        )
    with jax.named_scope("sum_first"):
        from_left = send(far_right, RIGHT)
        from_right = send(far_left, LEFT)
        a_bottom = send(right_bottom, RIGHT)
        b_top = send(left_top, LEFT)
        [right_top] = call(add_kernel, [half_piece])((), (), right_top, from_left)
        [left_bottom] = call(add_kernel, [half_piece])((), (), left_bottom, from_right)
        a_top = send(right_top, RIGHT)
        b_bottom = send(left_bottom, LEFT)
        [part] = call(join_kernel, [piece])((), (), own, a_top, a_bottom, b_top, b_bottom)
    with jax.named_scope("sum_second"):
        part = exchange(part.reshape(4, slab // 4, width), SECOND)
        part = jnp.sum(part.astype(f32), axis=0).astype(bf16)
    with jax.named_scope("sum_lines"):
        tiles = (
            part.reshape(slab // 32, 8, width // 128, 128).transpose(0, 2, 1, 3).reshape(-1, 8, 128)
        )
        count = tiles.shape[0]
        each = -(-count // NZ)
        tiles = jnp.concatenate([tiles, jnp.zeros((each * NZ - count, 8, 128), bf16)])
        tiles = exchange(tiles, LINES).reshape(NZ, each, 8, 128)
        tiles = jnp.sum(tiles.astype(f32), axis=0).astype(bf16)
    with jax.named_scope("share_lines"):
        tiles = exchange(jnp.tile(tiles, (NZ, 1, 1)), LINES)[:count]
        part = (
            tiles.reshape(slab // 32, width // 128, 8, 128).transpose(0, 2, 1, 3).reshape(-1, width)
        )
    with jax.named_scope("share_second"):
        own = exchange(jnp.tile(part[None], (4, 1, 1)), SECOND).reshape(slab, width)
    with jax.named_scope("share_first"):
        top, bottom = own[:half], own[half:]
        left_top = send(top, RIGHT)
        right_top = send(top, LEFT)
        left_bottom = send(bottom, RIGHT)
        right_bottom = send(bottom, LEFT)
        own_other = send(own, SWAP)
        across_top = send(left_top, RIGHT)
        across_bottom = send(right_bottom, LEFT)
        others = [send(piece, SWAP) for piece in (left_top, right_bottom, left_bottom, right_top)]
    with jax.named_scope("write"):
        outs = write((), [OWN, LEFT_TOP, RIGHT_BOTTOM, LEFT_BOTTOM, RIGHT_TOP], [OWN])(
            own, left_top, right_bottom, left_bottom, right_top, own_other, shape=matrix
        )
        [across_top] = after(outs[0], across_top, in_hbm=True)
        [across_bottom] = after(outs[0], across_bottom, in_hbm=True)
        across_others = [send(across_top, SWAP), send(across_bottom, SWAP)]
        outs = write(
            tuple(outs),
            [ACROSS_TOP, ACROSS_BOTTOM],
            [LEFT_TOP, RIGHT_BOTTOM, LEFT_BOTTOM, RIGHT_TOP],
        )(across_top, across_bottom, *others, shape=matrix)
        return write(tuple(outs), [], [ACROSS_TOP, ACROSS_BOTTOM])(*across_others, shape=matrix)


def solution(mesh):
    return jax.shard_map(
        on_device,
        mesh=mesh,
        in_specs=(P("dp", None), P("dp", None), P(), P(), P("dp"), P(), P()),
        out_specs=(P(), P()),
        check_vma=False,
    )
```

```python
import jax
import jax.numpy as jnp
from jax import lax
from jax.experimental import pallas as pl
from jax.experimental.pallas import tpu as pltpu
from jax.sharding import PartitionSpec as P

NY, NX, NZ, CORES = 4, 4, 8, 2
N = NY * NX * NZ * CORES
epsilon = 1e-06
bf16, f32 = jnp.bfloat16, jnp.float32
MIB = 1 << 20


def index(y, x, z, c):
    return ((y % NY * NX + x % NX) * NZ + z % NZ) * CORES + c


PLACES = [
    (y, x, z, c) for y in range(NY) for x in range(NX) for z in range(NZ) for c in range(CORES)
]


def route(move):
    return [(index(*place), index(*move(*place))) for place in PLACES]


def groups(key):
    found = {}
    for place in PLACES:
        found.setdefault(key(*place), []).append(index(*place))
    return list(found.values())


def along_first(step):
    return route(lambda y, x, z, c: (y, x + step, z, c) if c == 0 else (y + step, x, z, c))


SWAP = route(lambda y, x, z, c: (y, x, z, 1 - c))
RIGHT, LEFT = along_first(1), along_first(-1)
SECOND = groups(lambda y, x, z, c: (c, z, x if c == 0 else y))
LINES = groups(lambda y, x, z, c: (c, x, y))
FAR = [(i, (i + 3) % N if i % 2 else (i - 3) % N) for i in range(N)]
TEXT = 1


def shifted(distance):
    return [(i, (i + distance) % N) for i in range(N)]


def send(block, pairs):
    return lax.ppermute(block, "dp", pairs)


def exchange(parts, members):
    return lax.all_to_all(parts, "dp", 0, 0, axis_index_groups=members, tiled=True)


def call(body, outs, scratch=(), flops=0, result=pltpu.VMEM, aliases=()):
    def run(smem, outside, *arrays):
        specs = (
            [pl.BlockSpec(memory_space=pltpu.SMEM)] * len(smem)
            + [pl.BlockSpec(memory_space=pltpu.HBM)] * len(outside)
            + [pl.BlockSpec(memory_space=pltpu.VMEM)] * len(arrays)
        )
        held = [pltpu.with_memory_space_constraint(a, pltpu.VMEM) for a in arrays]
        outside = [pltpu.with_memory_space_constraint(a, pltpu.HBM) for a in outside]
        return pl.pallas_call(
            body,
            out_shape=[jax.ShapeDtypeStruct(s, d) for s, d in outs],
            in_specs=specs,
            out_specs=[pl.BlockSpec(memory_space=result)] * len(outs),
            scratch_shapes=list(scratch),
            input_output_aliases=dict(aliases),
            cost_estimate=pl.CostEstimate(flops=flops, bytes_accessed=0, transcendentals=0),
            compiler_params=pltpu.CompilerParams(vmem_limit_bytes=32 * MIB),
        )(*smem, *outside, *held)

    return run


def contract(a, b, da, db):
    return lax.dot_general(a, b, (((da,), (db,)), ((), ())), preferred_element_type=f32)


def core_place():
    me = lax.axis_index("dp")
    core = lax.rem(me, CORES)
    x = lax.rem(me // (NZ * CORES), NX)
    y = me // (NX * NZ * CORES)
    return core, jnp.where(core == 0, x, y), jnp.where(core == 0, y, x)


def on_text():
    return core_place()[0] == TEXT


def factor(log_scale):
    return jnp.exp(jnp.full((1, 1), log_scale[0], f32))


def embed(features, weight):
    projected = jnp.dot(features, weight, preferred_element_type=f32)
    square = jnp.sum(projected * projected, axis=-1, keepdims=True)
    inverse = 1.0 / jnp.sqrt(square + epsilon)
    return projected, inverse


def make_head(head, pairs, before=None):
    step = 128
    for k in range(head.shape[0] // step):
        at = pl.ds(k * step, step)
        new = sum(contract(x[:, at], back[...], 0, 0) for x, back in pairs)
        head[at, :] = new if before is None else before[at, :] + new


def visit(log_scale, shift, x, text_w, image_emb, finish, back, grad, grad_before):
    scale = factor(log_scale)
    projected, inverse = embed(x[...], text_w[...])
    emb = (projected * inverse).astype(bf16)
    similarity = contract(emb, image_emb[...], 1, 1)
    coefficient = finish(jax.nn.sigmoid(scale * similarity + shift[0])).astype(bf16)

    @pl.when(on_text())
    def _():
        radial = jnp.sum(coefficient.astype(f32) * similarity, axis=-1, keepdims=True)
        gradient = jnp.dot(coefficient, image_emb[...], preferred_element_type=f32)
        outer = scale * inverse
        back[...] = (gradient * outer - projected * (outer * inverse * radial)).astype(bf16)

    @pl.when(jnp.logical_not(on_text()))
    def _():
        share = contract(coefficient, emb, 0, 0)
        grad[...] = share if grad_before is None else grad_before[...] + share


def near_kernel(
    log_scale, shift, text_hbm, image_hbm, text_w_hbm, image_w_hbm, position_hbm,
    text_other, image_other, position_other,
    image_near, text_w, image_emb, image_projected, image_inverse, grad, text_near, back,
    image_w, position, sems,
):
    rows = text_other.shape[0]
    first, second = pl.ds(0, rows), pl.ds(rows, rows)
    moves = [
        pltpu.make_async_copy(image_hbm, image_near.at[first, :], sems.at[0]),
        pltpu.make_async_copy(image_w_hbm, image_w, sems.at[1]),
        pltpu.make_async_copy(text_hbm, text_near.at[first, :], sems.at[2]),
        pltpu.make_async_copy(text_w_hbm, text_w, sems.at[3]),
        pltpu.make_async_copy(position_hbm, position, sems.at[4]),
    ]
    for move in moves:
        move.start()
    image_near[second, :] = image_other[...]
    text_near[second, :] = text_other[...]
    moves[0].wait()
    moves[1].wait()
    projected, inverse = embed(image_near[...], image_w[...])
    image_emb[...] = (projected * inverse).astype(bf16)
    image_projected[...] = projected
    image_inverse[...] = inverse
    moves[2].wait()
    moves[3].wait()
    moves[4].wait()

    def with_labels(sigmoid):
        column = lax.broadcasted_iota(jnp.int32, (2 * rows, rows), 0)
        own = (column == position[...].reshape(1, rows)).astype(f32)
        other = (column == position_other[...] + rows).astype(f32)
        return sigmoid - jnp.concatenate([own, other], axis=1).T

    visit(log_scale, shift, text_near, text_w, image_emb, with_labels, back, grad, None)


def gate_kernel(*refs):
    pass


def after(token, *arrays, in_hbm=False):
    outs = [(a.shape, a.dtype) for a in arrays]
    first = 1 if in_hbm else 0
    gate = call(gate_kernel, outs, aliases=[(first + k, k) for k in range(len(arrays))])
    return gate((), (token,), *arrays) if in_hbm else gate((), (), *arrays, token)


def pair_kernel(log_scale, shift, below, above, text_w, image_emb, grad_before, grad, x, back):
    rows = below.shape[0]
    x[pl.ds(0, rows), :] = below[...]
    x[pl.ds(rows, rows), :] = above[...]
    visit(log_scale, shift, x, text_w, image_emb, lambda c: c, back, grad, grad_before)


def received_kernel(
    log_scale, shift, below, above, text_w, image_emb, grad_before, x_1, back_1,
    grad, head, x, back,
):
    pair_kernel(log_scale, shift, below, above, text_w, image_emb, grad_before, grad, x, back)

    @pl.when(on_text())
    def _():
        make_head(head, [(x_1, back_1), (x, back)])


def far_kernel(
    log_scale, shift, far, far_other, text_w, image_emb, grad_before,
    image_near, image_projected, image_inverse, head_before, x_1, back_1,
    own, right_top, right_bottom, left_top, left_bottom, far_right, far_left,
    grad, head, x, back,
):
    rows = far.shape[0]
    x[pl.ds(0, rows), :] = far[...]
    x[pl.ds(rows, rows), :] = far_other[...]

    def inside(sigmoid):
        row = lax.broadcasted_iota(jnp.int32, sigmoid.shape, 0) < rows
        column = lax.broadcasted_iota(jnp.int32, sigmoid.shape, 1) < rows
        return jnp.where(row == column, sigmoid, 0.0)

    visit(log_scale, shift, x, text_w, image_emb, inside, back, grad, grad_before)

    @pl.when(on_text())
    def _():
        make_head(head, [(x_1, back_1), (x, back)], head_before)

    @pl.when(jnp.logical_not(on_text()))
    def _():
        gradient = factor(log_scale) * grad[...]
        inverse = image_inverse[...]
        unit = image_projected[...] * inverse
        radial = jnp.sum(gradient * unit, axis=-1, keepdims=True)
        back[...] = ((gradient - unit * radial) * inverse).astype(bf16)
        make_head(head, [(image_near, back)])

    slab = head.shape[0] // 4
    half = slab // 2
    place = core_place()[1]

    def part(turn, upper, size):
        start = lax.rem(place + turn, 4) * slab + upper
        return head[pl.ds(pl.multiple_of(start, 16), size), :].astype(bf16)

    far_right[...] = part(2, 0, half)
    far_left[...] = part(2, half, half)
    right_top[...] = part(1, 0, half)
    right_bottom[...] = part(1, half, half)
    left_top[...] = part(3, 0, half)
    left_bottom[...] = part(3, half, half)
    own[...] = part(0, 0, slab)


def add_kernel(a, b, out):
    out[...] = (a[...].astype(f32) + b[...].astype(f32)).astype(bf16)


def join_kernel(own, a_top, a_bottom, b_top, b_bottom, out):
    half = a_top.shape[0]
    upper, lower = pl.ds(0, half), pl.ds(half, half)
    out[upper, :] = (
        own[upper, :].astype(f32) + a_top[...].astype(f32) + b_top[...].astype(f32)
    ).astype(bf16)
    out[lower, :] = (
        own[lower, :].astype(f32) + a_bottom[...].astype(f32) + b_bottom[...].astype(f32)
    ).astype(bf16)


OWN, LEFT_TOP, RIGHT_BOTTOM, LEFT_BOTTOM, RIGHT_TOP, ACROSS_TOP, ACROSS_BOTTOM = PIECES = (
    (0, 0), (3, 0), (1, 1), (3, 1), (1, 0), (2, 0), (2, 1)
)


def write(outs, mine, theirs):
    places = [*mine, *theirs]

    def body(*refs):
        pieces, (text, image, sems) = refs[len(outs) : len(outs) + len(places)], refs[-3:]
        core, place, other_place = core_place()

        def copies(first, other):
            moves = []
            for k, (piece, (turn, part)) in enumerate(zip(pieces, places)):
                own = k < len(mine)
                slab = piece.shape[0] * (1 if (turn, part) == OWN else 2)
                start = lax.rem((place if own else other_place) + turn, 4) * slab + part * slab // 2
                at = pl.ds(pl.multiple_of(start, 16), piece.shape[0])
                moves.append(
                    pltpu.make_async_copy(piece, (first if own else other).at[at, :], sems.at[k])
                )
            for move in moves:
                move.start()
            for move in moves:
                move.wait()

        @pl.when(core == TEXT)
        def _():
            copies(text, image)

        @pl.when(core != TEXT)
        def _():
            copies(image, text)

    def run(*arrays, shape):
        return call(
            body,
            [shape, shape],
            [pltpu.SemaphoreType.DMA((len(places),))],
            result=pltpu.HBM,
            aliases=[(k, k) for k in range(len(outs))],
        )((), outs, *arrays)

    return run


def on_device(text_x, image_x, text_w, image_w, position, log_scale, shift):
    rows, width = text_x.shape
    depth = text_w.shape[0]
    slab = depth // 4
    half = slab // 2
    scalars = (log_scale, shift)
    pair, pair_f32 = ((2 * rows, width), bf16), ((2 * rows, width), f32)
    total = ((depth, width), f32)
    matrix = ((depth, width), bf16)
    piece, half_piece = ((slab, width), bf16), ((half, width), bf16)
    with jax.named_scope("band_exchange"):
        text_other = send(text_x, SWAP)
        image_other = send(image_x, SWAP)
        position_other = send(position, SWAP)
        below = send(text_x, shifted(2))
        above = send(text_x, shifted(-2))
        far = send(text_x, FAR)
    with jax.named_scope("near"):
        image_near, weight, image_emb, image_projected, image_inverse, grad, *near = call(
            near_kernel,
            [pair, matrix, pair, pair_f32, ((2 * rows, 1), f32), pair_f32, pair, pair],
            [pltpu.VMEM(*matrix), pltpu.VMEM((rows,), jnp.int32), pltpu.SemaphoreType.DMA((5,))],
            flops=4 * 10**9,
        )(
            scalars, (text_x, image_x, text_w, image_w, position), text_other, image_other,
            position_other[None],
        )
    with jax.named_scope("swap_neighbours"):
        above, below = after(image_inverse, above, below)
        below_other = send(below, SWAP)
        above_other = send(above, SWAP)
    with jax.named_scope("received"):
        grad, head = call(
            received_kernel,
            [pair_f32, total],
            [pltpu.VMEM(*pair), pltpu.VMEM(*pair)],
            flops=4 * 10**9,
        )(scalars, (), below, above, weight, image_emb, grad, *near)
        [far] = after(grad, far)
        far_other = send(far, SWAP)
    with jax.named_scope("partners"):
        grad, *second = call(pair_kernel, [pair_f32, pair, pair], flops=4 * 10**9)(
            scalars, (), below_other, above_other, weight, image_emb, grad
        )
    with jax.named_scope("far"):
        own, right_top, right_bottom, left_top, left_bottom, far_right, far_left = call(
            far_kernel,
            [piece] + [half_piece] * 6,
            [pltpu.VMEM(*pair_f32), pltpu.VMEM(*total), pltpu.VMEM(*pair), pltpu.VMEM(*pair)],
            flops=4 * 10**9,
        )(
            scalars, (), far, far_other, weight, image_emb, grad, image_near, image_projected,
            image_inverse, head, *second,
        )
    with jax.named_scope("sum_first"):
        from_left = send(far_right, RIGHT)
        from_right = send(far_left, LEFT)
        a_bottom = send(right_bottom, RIGHT)
        b_top = send(left_top, LEFT)
        [right_top] = call(add_kernel, [half_piece])((), (), right_top, from_left)
        [left_bottom] = call(add_kernel, [half_piece])((), (), left_bottom, from_right)
        a_top = send(right_top, RIGHT)
        b_bottom = send(left_bottom, LEFT)
        [part] = call(join_kernel, [piece])((), (), own, a_top, a_bottom, b_top, b_bottom)
    with jax.named_scope("sum_second"):
        part = exchange(part.reshape(4, slab // 4, width), SECOND)
        part = jnp.sum(part.astype(f32), axis=0).astype(bf16)
    with jax.named_scope("sum_lines"):
        tiles = (
            part.reshape(slab // 32, 8, width // 128, 128).transpose(0, 2, 1, 3).reshape(-1, 8, 128)
        )
        count = tiles.shape[0]
        each = -(-count // NZ)
        tiles = jnp.concatenate([tiles, jnp.zeros((each * NZ - count, 8, 128), bf16)])
        tiles = exchange(tiles, LINES).reshape(NZ, each, 8, 128)
        tiles = jnp.sum(tiles.astype(f32), axis=0).astype(bf16)
    with jax.named_scope("share_lines"):
        tiles = exchange(jnp.tile(tiles, (NZ, 1, 1)), LINES)[:count]
        part = (
            tiles.reshape(slab // 32, width // 128, 8, 128).transpose(0, 2, 1, 3).reshape(-1, width)
        )
    with jax.named_scope("share_second"):
        own = exchange(jnp.tile(part[None], (4, 1, 1)), SECOND).reshape(slab, width)
    with jax.named_scope("share_first"):
        top, bottom = own[:half], own[half:]
        left_top = send(top, RIGHT)
        right_top = send(top, LEFT)
        left_bottom = send(bottom, RIGHT)
        right_bottom = send(bottom, LEFT)
        own_other = send(own, SWAP)
        across_top = send(left_top, RIGHT)
        across_bottom = send(right_bottom, LEFT)
        others = [send(piece, SWAP) for piece in (left_top, right_bottom, left_bottom, right_top)]
    with jax.named_scope("write"):
        outs = write((), [OWN, LEFT_TOP, RIGHT_BOTTOM, LEFT_BOTTOM, RIGHT_TOP], [OWN])(
            own, left_top, right_bottom, left_bottom, right_top, own_other, shape=matrix
        )
        [across_top] = after(outs[0], across_top, in_hbm=True)
        [across_bottom] = after(outs[0], across_bottom, in_hbm=True)
        across_others = [send(across_top, SWAP), send(across_bottom, SWAP)]
        outs = write(
            tuple(outs),
            [ACROSS_TOP, ACROSS_BOTTOM],
            [LEFT_TOP, RIGHT_BOTTOM, LEFT_BOTTOM, RIGHT_TOP],
        )(across_top, across_bottom, *others, shape=matrix)
        return write(tuple(outs), [], [ACROSS_TOP, ACROSS_BOTTOM])(*across_others, shape=matrix)


def solution(mesh):
    return jax.shard_map(
        on_device,
        mesh=mesh,
        in_specs=(P("dp", None), P("dp", None), P(), P(), P("dp"), P(), P()),
        out_specs=(P(), P()),
        check_vma=False,
    )
```
